32 devices in a mesh: grp: 2 (over y), obs: 4 (over z), par: 4 (over x, core).
Axes of the slice: x: 2, y: 2, z: 4, core: 2. Of those that a mesh axis runs over, the one named last changes fastest.
Arguments:
- predicted: bfloat16 [256, 786432], P(None, ('grp', 'obs', 'par')), parts along dimension 1, may hold values from -120 to 120
- observed: float32 [786432], P(('grp', 'obs', 'par')), parts along dimension 0, may hold values from -120 to 120
- band: float32 [8, 786432], P(None, ('grp', 'obs', 'par')), parts along dimension 1, may hold values from -5 to 5
- offsets: int32 [8], replicated, may hold values from -1024 to 1024, as said below
- rows_count: int32 [32], P(('grp', 'obs', 'par')), parts along dimension 0, may hold values from 12288 to 23552, as said below
- params: bfloat16 [16384, 256], P(('grp', 'obs', 'par')), parts along dimension 0, may hold values from -6 to 6
Outputs:
- params_new: float32 [16384, 256], P(('grp', 'obs', 'par')), parts along dimension 0
- whitened_misfit: float32 [786432], P(('grp', 'obs', 'par')), parts along dimension 0
The draws below stay inside these ranges and needn't reach their ends.
There are 2 independent parts, one for each index of `grp`. The reference program is written for one: setup_inputs(seed, part) draws one part's arguments, and reference() takes and returns one part's arrays. A program takes and returns all parts, laid end to end along the dimension named above; an argument that names none is the same for every part. Nothing has to cross between parts.
Inputs may be any that keep to these rules, and one draw needn't show every extreme that they name: offsets[0] is 0, the 8 offsets are distinct, and both -1024 and 1024 are among them. `rows_count`: every shard holds this many strain observations first, then load observations up to its last 1024 observations, which are strain observations again; in every draw some shard holds exactly 23552 leading strain observations and some exactly 12288.
All inputs are finite; a program needn't handle non-finite values.
Results may differ from the reference program's by a relative error of at most 0.0029.
Values may be sent and summed in bfloat16 or wider, within the bound.
No kernel may reach another device: no remote copies, remote signals or barrier semaphores. Data moves between devices by JAX's collectives and lax.ppermute only.
A program may use at most 256 MiB of HBM per device.

```python
import math
import jax
import jax.numpy as jnp
from jax import lax

M = 256
B = 8
H = 1024
O_DEV = 24576
SHARDS = 16
NOBS = 393216
NPAR = 8192


def shared_parts(key):
    shared = jax.random.normal(jax.random.fold_in(key, 11), (M // 8, NOBS), jnp.float32)
    row_ramp = jnp.arange(NOBS, dtype=jnp.float32) * (math.log(3.0) / NOBS)
    row_scale = jnp.exp(jax.random.uniform(jax.random.fold_in(key, 12), (NOBS,), jnp.float32, -0.8, 0.8) + row_ramp)
    groups = jax.random.permutation(jax.random.fold_in(key, 13), M) // 8
    member_scale = jnp.exp(jax.random.uniform(jax.random.fold_in(key, 14), (M,), jnp.float32, -1.15, 1.15))
    return (shared, row_scale, groups, member_scale)


def draw_predicted(key, part):
    shared, row_scale, groups, member_scale = shared_parts(key)
    noise = jax.random.normal(jax.random.fold_in(key, 21), (M, NOBS), jnp.float32)
    common = shared[groups]
    values = member_scale[:, None] * row_scale[None, :] * (noise + common)
    return jnp.clip(values, -120.0, 120.0).astype(jnp.bfloat16)


def draw_observed(key, part):
    shared, row_scale, groups, member_scale = shared_parts(key)
    noise = jax.random.normal(jax.random.fold_in(key, 31), (NOBS,), jnp.float32)
    values = row_scale * (0.7 * shared[0] + 0.7 * shared[1] + noise)
    return jnp.clip(values, -120.0, 120.0)


def draw_offsets(key, part):
    others = jnp.concatenate([jnp.arange(1 - H, 0, dtype=jnp.int32), jnp.arange(1, H, dtype=jnp.int32)])
    picked = jax.random.permutation(jax.random.fold_in(key, 41), others)[:B - 3]
    rest_values = jnp.concatenate([jnp.array([H, -H], dtype=jnp.int32), picked])
    rest_values = jax.random.permutation(jax.random.fold_in(key, 42), rest_values)
    return jnp.concatenate([jnp.zeros((1,), jnp.int32), rest_values])


def draw_rows_count(key, part):
    counts_drawn = jax.random.randint(jax.random.fold_in(key, 51), (SHARDS,), O_DEV // 2, O_DEV - H + 1, dtype=jnp.int32)
    full_at = jax.random.randint(jax.random.fold_in(key, 52), (), 0, SHARDS, dtype=jnp.int32)
    half_at = (full_at + 1 + jax.random.randint(jax.random.fold_in(key, 53), (), 0, SHARDS - 1, dtype=jnp.int32)) % SHARDS
    counts_drawn = counts_drawn.at[full_at].set(O_DEV - H)
    counts_drawn = counts_drawn.at[half_at].set(O_DEV // 2)
    return counts_drawn


def shard_levels(key, dims, split, low, top_value):
    gain, own = 1.0, jax.random.fold_in(key, 6)
    for dim, blocks in split:
        heights = jnp.exp(jax.random.uniform(jax.random.fold_in(own, dim), (blocks,), jnp.float32, low / len(split), top_value / len(split)))
        gain = gain * jnp.repeat(heights, dims[dim] // blocks).reshape([-1 if axis == dim else 1 for axis in range(len(dims))])
    return gain


def centred(key, shape, deviation, reach, shards=(), held_as=jnp.bfloat16):
    level = shard_levels(key, shape, shards, -0.22, 0.18) if shards else 1.0
    drawn = jax.random.normal(key, shape, jnp.float32) * deviation * level
    return jnp.minimum(jnp.maximum(drawn, -reach), reach).astype(held_as)


def setup_inputs(seed: int = 0, part: int = 0) -> dict:
    key_list = jax.random.split(jax.random.key(seed), 7)
    own_keys = jax.random.split(jax.random.fold_in(key_list[6], part), 7)
    predicted = draw_predicted(jax.random.fold_in(jax.random.fold_in(key_list[6], part), 71), part)
    observed = draw_observed(jax.random.fold_in(jax.random.fold_in(key_list[6], part), 71), part)
    band = centred(own_keys[2], (B, NOBS), 0.35, 5.0, ((1, 16),), jnp.float32)
    offsets = draw_offsets(jax.random.fold_in(key_list[6], 71), part)
    rows_count = draw_rows_count(jax.random.fold_in(jax.random.fold_in(key_list[6], part), 71), part)
    params = centred(own_keys[5], (NPAR, M), 1.0, 6.0, ((0, 16),))
    return {"predicted": predicted, "observed": observed, "band": band, "offsets": offsets, "rows_count": rows_count, "params": params}


def whiten(padded, band_block, offsets, strain):
    columns = band_block.shape[1]

    def shifted(term):
        begin = (H + offsets[term]).astype(jnp.int32)
        return lax.dynamic_slice_in_dim(padded, begin, columns, 1).astype(jnp.float32)
    leading = band_block[0] * shifted(0)
    extra_terms = jnp.zeros_like(leading)
    for term in range(1, B):
        extra_terms = extra_terms + band_block[term] * shifted(term)
    return leading + strain * extra_terms

def reference(predicted, observed, band, offsets, rows_count, params):
    obs_total = O_DEV * SHARDS
    row_factor = 1.0 / math.sqrt(obs_total)
    misfit_factor = math.sqrt((M - 1) / obs_total)
    pred_pad = jnp.pad(predicted, ((0, 0), (H, H)))
    obs_pad = jnp.pad(observed, (H, H))

    def shard_step(carry, shard):
        gram_total, projection = carry
        offset_at = (shard * O_DEV).astype(jnp.int32)
        pred_block = lax.dynamic_slice_in_dim(pred_pad, offset_at, O_DEV + 2 * H, 1).astype(jnp.float32)
        obs_block = lax.dynamic_slice_in_dim(obs_pad, offset_at, O_DEV + 2 * H, 0)
        mean_pred = lax.optimization_barrier(jnp.mean(pred_block, axis=0))
        anomaly = lax.optimization_barrier((pred_block - mean_pred).astype(jnp.bfloat16))
        innovation = lax.optimization_barrier((obs_block - mean_pred).astype(jnp.bfloat16))
        joint = jnp.concatenate([innovation[None, :], anomaly], 0)
        band_block = lax.dynamic_slice_in_dim(band, offset_at, O_DEV, 1)
        local_index = lax.iota(jnp.int32, O_DEV)
        strain = ((local_index < rows_count[shard]) | (local_index >= O_DEV - H)).astype(jnp.float32)
        whitened = whiten(joint, band_block, offsets, strain)
        anomaly_white = (whitened[1:] * row_factor).astype(jnp.bfloat16)
        misfit = whitened[0] * misfit_factor
        gram_total = gram_total + lax.dot_general(anomaly_white.astype(jnp.float32), anomaly_white.astype(jnp.float32), (((1,), (1,)), ((), ())), preferred_element_type=jnp.float32)
        projection = projection + jnp.dot(anomaly_white.astype(jnp.float32), misfit, precision=lax.Precision.HIGHEST)
        return ((gram_total, projection), misfit)
    initial = (jnp.zeros((M, M), jnp.float32), jnp.zeros((M,), jnp.float32))
    (gram_total, projection), misfits = lax.scan(shard_step, initial, jnp.arange(SHARDS, dtype=jnp.int32))
    whitened_misfit = misfits.reshape(SHARDS * O_DEV)
    identity = jnp.eye(M, dtype=jnp.float32)
    lower_factor = jnp.linalg.cholesky(identity + gram_total)
    weights = jax.scipy.linalg.cho_solve((lower_factor, True), projection)
    inverse_t = jax.scipy.linalg.solve_triangular(lower_factor, identity, lower=True).T
    transform = weights[:, None] / math.sqrt(M - 1) + inverse_t
    params_wide = params.astype(jnp.float32)
    param_mean = lax.optimization_barrier(jnp.mean(params_wide, axis=1, keepdims=True))
    params_new = param_mean + jnp.dot(params_wide - param_mean, transform, precision=lax.Precision.HIGHEST)
    return (params_new, whitened_misfit)
```

```python
import functools
import math

import jax
import jax.numpy as jnp
from jax import lax
from jax.experimental import pallas as pl
from jax.experimental.pallas import tpu as pltpu
from jax.sharding import PartitionSpec as P

H = 1024
LANE = 128
PACK = 16
BLOCK = 64
PANEL = 8
BF = jnp.bfloat16
F32 = jnp.float32


def local_kernel(edge, columns, obs_total, *refs):
    if edge:
        (off_ref, count_ref, pred_ref, obs_ref, band_ref, left_ref, right_ref, gram_in, misfit_in,
         gram_out, misfit_out, raw, joint, aw_a, aw_b, coef, gram, centre, row_out, slots, sems) = refs
    else:
        (off_ref, count_ref, pred_ref, obs_ref, band_ref,
         gram_out, misfit_out, raw, joint, aw_a, aw_b, coef, gram, centre, slots, sems) = refs
    members = pred_ref.shape[0]
    rows = members + PACK
    terms = band_ref.shape[0]
    chunks = columns // H
    tiles = H // LANE
    slices = 4
    part = H // slices
    row_factor = 1.0 / math.sqrt(obs_total)

    if edge:
        copies = [
            pltpu.make_async_copy(left_ref, raw.at[:, pl.ds(0, H)], sems.at[0]),
            pltpu.make_async_copy(right_ref, raw.at[:, pl.ds(5 * H, H)], sems.at[5]),
        ]
        for place, chunk in ((1, 0), (2, 1), (3, chunks - 2), (4, chunks - 1)):
            copies.append(pltpu.make_async_copy(
                pred_ref.at[:, pl.ds(chunk * H, H)],
                raw.at[pl.ds(0, members), pl.ds(place * H, H)], sems.at[place]))
        for copy in copies:
            copy.start()
    else:
        def chunk_copy(place):
            start = pl.multiple_of(place * H, H)
            return pltpu.make_async_copy(
                pred_ref.at[:, pl.ds(start, H)], raw.at[:, pl.ds(start, H)], sems.at[place])

        for place in range(chunks):
            chunk_copy(place).start()

    slots[0, 0] = 0
    slots[0, 1] = 0
    free = jnp.int32(3)
    for term in range(1, terms):
        offset = off_ref[term]
        whole = (offset == H) | (offset == -H)
        place = jnp.where(offset == -H, 1, jnp.where(offset == H, 2, free))
        place = jnp.minimum(place, terms - 1)
        slots[place, 0] = jnp.int32(term)
        slots[place, 1] = offset
        free = free + jnp.where(whole, 0, 1)

    row_index = lax.broadcasted_iota(jnp.int32, (rows, members), 0)
    col_index = lax.broadcasted_iota(jnp.int32, (rows, members), 1)
    mean_part = 1.0 / members
    centre[...] = jnp.where(
        row_index >= members, mean_part, jnp.where(row_index == col_index, 1.0 - mean_part, -mean_part)
    ).astype(BF)
    if edge:
        gram[...] = jnp.zeros_like(gram)
    else:
        gram[...] = jnp.zeros_like(gram)
        aw_b[...] = jnp.zeros_like(aw_b)

    def anomalies(place, step, obs_row):
        at = pl.multiple_of(place * H + step * part, part)
        wide = jnp.dot(centre[...], raw[pl.ds(0, members), pl.ds(at, part)], preferred_element_type=F32)
        joint[pl.ds(0, members), pl.ds(at, part)] = wide[:members].astype(BF)
        joint[pl.ds(members, PACK), pl.ds(at, part)] = (obs_row - wide[members:]).astype(BF)

    def coefficients(column):
        index = column + lax.broadcasted_iota(jnp.int32, (1, H), 1)
        strained = (index < count_ref[0]) | (index >= columns - H)
        strain = jnp.where(strained, row_factor, 0.0)
        for slot in range(terms):
            term = slots[slot, 0]
            row = band_ref[pl.ds(term, 1), pl.ds(column, H)]
            row = row * (row_factor if slot == 0 else strain)
            coef[pl.ds(slot * 8, 8), :] = jnp.broadcast_to(row, (8, H))

    def whiten_rows(place, at_row):
        lane = lax.broadcasted_iota(jnp.int32, (PACK, LANE), 1)
        acc = [None] * tiles

        def load(tile):
            start = pl.multiple_of(tile * LANE, LANE)
            return joint[pl.ds(at_row, PACK), pl.ds(start, LANE)]

        for slot in range(terms):
            offset = slots[slot, 1]
            if slot < 3:
                first = place * tiles + (0, -tiles, tiles)[slot]
                values = [load(first + t) for t in range(tiles)]
            else:
                turn = lax.rem(offset + 8 * LANE, LANE)
                first = place * tiles + lax.div(offset + 8 * LANE, LANE) - 8
                back = lax.rem(LANE - turn, LANE)
                keep = lane < LANE - turn
                rolled = [pltpu.roll(load(first + t), back, 1) for t in range(tiles + 1)]
                values = [jnp.where(keep, rolled[t], rolled[t + 1]) for t in range(tiles)]
            for t in range(tiles):
                weight = coef[pl.ds(slot * 8, 8), pl.ds(t * LANE, LANE)]
                weight = jnp.concatenate([weight, weight], 0)
                product = values[t].astype(F32) * weight
                acc[t] = product if acc[t] is None else acc[t] + product
        return acc

    def products(aw, step):
        at = step * part if isinstance(step, int) else pl.multiple_of(step * part, part)
        block = aw[:, pl.ds(at, part)]
        gram[...] += lax.dot_general(
            block, block[:members], (((1,), (1,)), ((), ())), preferred_element_type=F32)

    def whiten_chunk(place, column, aw, before, store_misfit, more=None):
        coefficients(column)
        acc = whiten_rows(place, members)
        row = lax.broadcasted_iota(jnp.int32, (PACK, LANE), 0)
        for t in range(tiles):
            wide = acc[t]
            high = wide.astype(BF).astype(F32)
            rest = wide - high
            middle = rest.astype(BF).astype(F32)
            low = rest - middle
            split = jnp.where(row == 0, high, jnp.where(row == 1, middle, jnp.where(row == 2, low, 0.0)))
            aw[pl.ds(members, PACK), pl.ds(t * LANE, LANE)] = split.astype(BF)
            store_misfit(t, wide[0:1] * math.sqrt(members - 1))

        def step_body(step, carry):
            if before is not None:
                products(before, step)
            for piece in range(members // PACK // slices):
                at_row = pl.multiple_of(step * (members // slices) + piece * PACK, PACK)
                out = whiten_rows(place, at_row)
                for t in range(tiles):
                    aw[pl.ds(at_row, PACK), pl.ds(t * LANE, LANE)] = out[t].astype(BF)
            if more is not None:
                more(step)
            return carry

        lax.fori_loop(0, slices, step_body, 0)

    if edge:
        for copy in copies:
            copy.wait()
        for place, chunk in ((0, None), (1, 0), (2, 1), (3, chunks - 2), (4, chunks - 1), (5, None)):
            def edge_step(step, carry):
                if chunk is None:
                    at = pl.multiple_of(place * H + step * part, part)
                    pieces = raw[pl.ds(members, PACK), pl.ds(at, part)].astype(F32)
                    obs_row = pieces[0:1] + pieces[1:2] + pieces[2:3]
                else:
                    obs_row = obs_ref[:, pl.ds(pl.multiple_of(chunk * H + step * part, part), part)]
                anomalies(place, step, obs_row)
                return carry
            lax.fori_loop(0, slices, edge_step, 0)
        for place, chunk, aw, before in ((1, 0, aw_a, None), (4, chunks - 1, aw_b, aw_a)):
            def store_misfit(t, value):
                row_out[:, pl.ds((0 if place == 1 else H) + t * LANE, LANE)] = value
            whiten_chunk(place, chunk * H, aw, before, store_misfit)
        out_copies = [
            pltpu.make_async_copy(row_out.at[:, pl.ds(0, H)], misfit_out.at[:, pl.ds(0, H)], sems.at[0]),
            pltpu.make_async_copy(row_out.at[:, pl.ds(H, H)], misfit_out.at[:, pl.ds(columns - H, H)], sems.at[1]),
        ]
        for copy in out_copies:
            copy.start()
        for step in range(slices):
            products(aw_b, step)
        gram_out[pl.ds(0, members), :] = gram_in[pl.ds(0, members), :] + gram[pl.ds(0, members), :]
        tail = gram[pl.ds(members, 8), :]
        total = tail[0:1] + tail[1:2] + tail[2:3]
        first = lax.broadcasted_iota(jnp.int32, (8, members), 0) == 0
        gram_out[pl.ds(members, 8), :] = gram_in[pl.ds(members, 8), :] + jnp.where(first, total, 0.0)
        for copy in out_copies:
            copy.wait()
    else:
        def make_ready(place, step):
            obs_row = obs_ref[:, pl.ds(pl.multiple_of(place * H + step * part, part), part)]
            anomalies(place, step, obs_row)

        for place in range(3):
            chunk_copy(place).wait()

            def first_step(step, carry, place=place):
                make_ready(place, step)
                return carry
            lax.fori_loop(0, slices, first_step, 0)

        def chunk_step(place, aw, before):
            ahead = jnp.minimum(place + 2, chunks - 1)

            @pl.when(place + 2 < chunks)
            def _():
                chunk_copy(ahead).wait()

            column = pl.multiple_of(place * H, H)

            def store_misfit(t, value):
                misfit_out[:, pl.ds(column + t * LANE, LANE)] = value

            whiten_chunk(place, column, aw, before, store_misfit, lambda step: make_ready(ahead, step))

        def pair(index, carry):
            chunk_step(1 + 2 * index, aw_a, aw_b)
            chunk_step(2 + 2 * index, aw_b, aw_a)
            return carry

        lax.fori_loop(0, (chunks - 2) // 2, pair, 0)
        for step in range(slices):
            products(aw_b, step)
        gram_out[pl.ds(0, members), :] = gram[pl.ds(0, members), :]
        tail = gram[pl.ds(members, 8), :]
        total = tail[0:1] + tail[1:2] + tail[2:3]
        first = lax.broadcasted_iota(jnp.int32, (8, members), 0) == 0
        gram_out[pl.ds(members, 8), :] = jnp.where(first, total, 0.0)


def local_call(edge, obs_total, offsets, rows_count, predicted, observed, band, *more):
    members, columns = predicted.shape
    rows = members + PACK
    places = 6 if edge else columns // H
    vmem = pl.BlockSpec(memory_space=pltpu.VMEM)
    smem = pl.BlockSpec(memory_space=pltpu.SMEM)
    anywhere = pl.BlockSpec(memory_space=pl.ANY)
    in_specs = [smem, smem, anywhere, vmem, vmem]
    out_specs = [vmem, anywhere if edge else vmem]
    if edge:
        in_specs += [anywhere, anywhere, vmem, anywhere]
    scratch = [
        pltpu.VMEM((rows if edge else members, places * H), BF),
        pltpu.VMEM((rows, places * H), BF),
        pltpu.VMEM((rows, H), BF),
        pltpu.VMEM((rows, H), BF),
        pltpu.VMEM((8 * band.shape[0], H), F32),
        pltpu.VMEM((rows, members), F32),
        pltpu.VMEM((rows, members), BF),
    ]
    if edge:
        scratch.append(pltpu.VMEM((1, 2 * H), F32))
    scratch += [pltpu.SMEM((8, 2), jnp.int32), pltpu.SemaphoreType.DMA((places,))]
    work = 2 if edge else places - 2
    return pl.pallas_call(
        functools.partial(local_kernel, edge, columns, obs_total),
        out_shape=(
            jax.ShapeDtypeStruct((members + 8, members), F32),
            jax.ShapeDtypeStruct((1, columns), F32),
        ),
        in_specs=in_specs,
        out_specs=out_specs,
        scratch_shapes=scratch,
        input_output_aliases={8: 1} if edge else {},
        compiler_params=pltpu.CompilerParams(vmem_limit_bytes=50 * 2**20),
        cost_estimate=pl.CostEstimate(
            flops=2 * rows * members * H * work * 2, bytes_accessed=members * H * places * 2, transcendentals=0),
        name="edges" if edge else "inner",
    )(offsets, rows_count, predicted, observed, band, *more)


def update_kernel(sum_ref, params_ref, out_ref, work):
    members = params_ref.shape[1]
    highest = lax.Precision.HIGHEST
    row_index = lax.broadcasted_iota(jnp.int32, (members, members), 0)
    col_index = lax.broadcasted_iota(jnp.int32, (members, members), 1)
    identity = jnp.where(row_index == col_index, 1.0, 0.0).astype(F32)
    work[:, pl.ds(0, members)] = sum_ref[pl.ds(0, members), :] + identity
    work[:, pl.ds(members, members)] = identity
    panels = BLOCK // PANEL
    sub = lax.broadcasted_iota(jnp.int32, (PANEL, LANE), 0)
    eye = identity[:BLOCK, :BLOCK]

    def across(tile, column):
        return jnp.broadcast_to(tile[:, column:column + 1], (PANEL, LANE))

    def down(tile, row):
        return jnp.broadcast_to(tile[row:row + 1, :], (PANEL, LANE))

    for block in range(members // BLOCK):
        r0 = block * BLOCK
        start = jnp.concatenate([work[pl.ds(r0, BLOCK), pl.ds(r0, BLOCK)], eye], axis=1)
        tiles = [start[PANEL * t:PANEL * (t + 1)] for t in range(panels)]
        done = []
        for p in range(panels):
            c0 = PANEL * p
            tile = tiles[p]
            upper = tile
            full = tile
            cols = [across(tile, c0 + j) for j in range(PANEL)]
            full_cols = list(cols)
            scale = jnp.zeros((PANEL, LANE), F32)
            for k in range(PANEL):
                pivot = down(cols[k], k)
                inverse = 1.0 / pivot
                scale = jnp.where(sub == k, pivot, scale)
                below = jnp.where(sub > k, cols[k] * inverse, 0.0)

                def clear(values):
                    row = down(values, k) * inverse
                    return jnp.where(sub == k, row, values - full_cols[k] * row)

                for j in range(k + 1, PANEL):
                    cols[j] = cols[j] - below * down(cols[j], k)
                    full_cols[j] = clear(full_cols[j])
                upper = upper - below * down(upper, k)
                full = clear(full)
            done.append(upper * lax.rsqrt(scale))
            rows_of = [down(full, k) for k in range(PANEL)]
            for t in range(p + 1, panels):
                tile_t = tiles[t]
                change = [across(tile_t, c0 + k) * rows_of[k] for k in range(PANEL)]
                while len(change) > 1:
                    change = [a + b for a, b in zip(change[::2], change[1::2])]
                tiles[t] = tile_t - change[0]
        lower_inverse = jnp.concatenate(done, axis=0)[:, BLOCK:2 * BLOCK]
        solved = jnp.dot(lower_inverse, work[pl.ds(r0, BLOCK), :], precision=highest, preferred_element_type=F32)
        work[pl.ds(r0, BLOCK), :] = solved
        if r0 + BLOCK < members:
            rest = members - r0 - BLOCK
            factor = solved[:, r0 + BLOCK:members]
            work[pl.ds(r0 + BLOCK, rest), :] = work[pl.ds(r0 + BLOCK, rest), :] - lax.dot_general(
                factor, solved, (((0,), (0,)), ((), ())), precision=highest, preferred_element_type=F32)

    inverse = jnp.where(row_index >= col_index, work[:, pl.ds(members, members)], 0.0)
    projection = sum_ref[pl.ds(members, 1), :]
    half = jnp.sum(inverse * projection, axis=1, keepdims=True)
    weights = jnp.sum(inverse * half, axis=0, keepdims=True)
    turned = inverse + weights
    turned = turned - jnp.mean(turned, axis=1, keepdims=True) + 1.0 / members
    high = turned.astype(BF)
    rest = turned - high.astype(F32)
    middle = rest.astype(BF)
    low = (rest - middle.astype(F32)).astype(BF)
    params = params_ref[...]

    def times(part):
        return lax.dot_general(params, part, (((1,), (1,)), ((), ())), preferred_element_type=F32)

    out_ref[...] = times(high) + (times(middle) + times(low))


def update(total, params):
    members = params.shape[1]
    vmem = pl.BlockSpec(memory_space=pltpu.VMEM)
    return pl.pallas_call(
        update_kernel,
        out_shape=jax.ShapeDtypeStruct(params.shape, F32),
        in_specs=[vmem, vmem],
        out_specs=vmem,
        scratch_shapes=[pltpu.VMEM((members, 2 * members), F32)],
        compiler_params=pltpu.CompilerParams(vmem_limit_bytes=32 * 2**20),
        name="update",
    )(total, params)


def halo_block(predicted, observed):
    high = lax.reduce_precision(observed, 8, 7)
    rest = observed - high
    middle = lax.reduce_precision(rest, 8, 7)
    low = rest - middle
    pieces = jnp.concatenate(
        [high[None], middle[None], low[None], jnp.zeros((PACK - 3, observed.shape[0]), F32)], 0)
    return jnp.concatenate([predicted, pieces.astype(BF)], 0)


def body(predicted, observed, band, offsets, rows_count, params):
    columns = predicted.shape[1]
    axes = ("obs", "par")
    shards = lax.axis_size(axes)
    obs_total = columns * shards
    up = [(i, i + 1) for i in range(shards - 1)]
    down = [(j, i) for i, j in up]
    left = lax.ppermute(halo_block(predicted[:, columns - H:], observed[columns - H:]), axes, up)
    right = lax.ppermute(halo_block(predicted[:, :H], observed[:H]), axes, down)
    obs_row = observed[None, :]
    gram, misfit = local_call(False, obs_total, offsets, rows_count, predicted, obs_row, band)
    gram, misfit = local_call(
        True, obs_total, offsets, rows_count, predicted, obs_row, band, left, right, gram, misfit)
    total = lax.psum(gram, axes)
    return (update(total, params), misfit[0])


def solution(mesh):
    in_specs = (
        P(None, ("grp", "obs", "par")),
        P(("grp", "obs", "par")),
        P(None, ("grp", "obs", "par")),
        P(),
        P(("grp", "obs", "par")),
        P(("grp", "obs", "par"), None),
    )
    out_specs = (P(("grp", "obs", "par"), None), P(("grp", "obs", "par")))
    return jax.shard_map(body, mesh=mesh, in_specs=in_specs, out_specs=out_specs, check_vma=False)
```

```python
import functools
import math

import jax
import jax.numpy as jnp
from jax import lax
from jax.experimental import pallas as pl
from jax.experimental.pallas import tpu as pltpu
from jax.sharding import PartitionSpec as P

H = 1024
LANE = 128
PACK = 16
BLOCK = 64
PANEL = 8
BF = jnp.bfloat16
F32 = jnp.float32


def local_kernel(edge, columns, obs_total, *refs):
    if edge:
        (off_ref, count_ref, pred_ref, obs_ref, band_ref, left_ref, right_ref, gram_in, misfit_in,
         gram_out, misfit_out, raw, joint, fresh, aw_a, aw_b, coef, gram, centre, obs, band, row_out, slots,
         sems) = refs
    else:
        (off_ref, count_ref, pred_ref, obs_ref, band_ref,
         gram_out, misfit_out, raw, joint, fresh, aw_a, aw_b, coef, gram, centre, obs, band, row_out, slots,
         sems) = refs
    members = pred_ref.shape[0]
    terms = band_ref.shape[0]
    chunks = columns // H
    tiles = H // LANE
    half = members // 2
    row_factor = 1.0 / math.sqrt(obs_total)

    if edge:
        copies = [
            pltpu.make_async_copy(left_ref, raw.at[:, pl.ds(0, H)], sems.at[0]),
            pltpu.make_async_copy(right_ref, raw.at[:, pl.ds(5 * H, H)], sems.at[5]),
        ]
        for place, chunk in ((1, 0), (2, 1), (3, chunks - 2), (4, chunks - 1)):
            copies.append(pltpu.make_async_copy(
                pred_ref.at[:, pl.ds(chunk * H, H)],
                raw.at[pl.ds(0, members), pl.ds(place * H, H)], sems.at[place]))
        for which in range(2):
            there = which * (columns - 2 * H)
            copies.append(pltpu.make_async_copy(
                obs_ref.at[:, pl.ds(there, 2 * H)], obs.at[:, pl.ds(which * 2 * H, 2 * H)], sems.at[6 + which]))
            there = which * (columns - H)
            copies.append(pltpu.make_async_copy(
                band_ref.at[:, pl.ds(there, H)], band.at[:, pl.ds(which * H, H)], sems.at[8 + which]))
        for copy in copies:
            copy.start()
    else:
        def chunk_copy(place):
            start = pl.multiple_of(place * H, H)
            return pltpu.make_async_copy(
                pred_ref.at[:, pl.ds(start, H)], raw.at[:, pl.ds(start, H)], sems.at[place])

        copies = [
            pltpu.make_async_copy(obs_ref, obs, sems.at[chunks]),
            pltpu.make_async_copy(band_ref, band, sems.at[chunks + 1]),
        ]
        for place in range(chunks):
            chunk_copy(place).start()
            if place == 2:
                for copy in copies:
                    copy.start()

    slots[0, 0] = 0
    slots[0, 1] = 0
    free = jnp.int32(3)
    for term in range(1, terms):
        offset = off_ref[term]
        whole = (offset == H) | (offset == -H)
        place = jnp.where(offset == -H, 1, jnp.where(offset == H, 2, free))
        place = jnp.minimum(place, terms - 1)
        slots[place, 0] = jnp.int32(term)
        slots[place, 1] = offset
        free = free + jnp.where(whole, 0, 1)

    rows = members + PACK
    row_index = lax.broadcasted_iota(jnp.int32, (rows, members), 0)
    col_index = lax.broadcasted_iota(jnp.int32, (rows, members), 1)
    mean_part = 1.0 / members
    centre[...] = jnp.where(
        row_index >= members, mean_part, jnp.where(row_index == col_index, 1.0 - mean_part, -mean_part)
    ).astype(BF)
    gram[...] = jnp.zeros_like(gram)
    if not edge:
        aw_b[...] = jnp.zeros_like(aw_b)

    def anomalies(place, obs_row, target, at):
        wide = jnp.dot(
            centre[...], raw[pl.ds(0, members), pl.ds(pl.multiple_of(place * H, H), H)],
            preferred_element_type=F32)
        target[pl.ds(0, members), pl.ds(at, H)] = wide[:members].astype(BF)
        target[pl.ds(members, PACK), pl.ds(at, H)] = (obs_row - wide[members:]).astype(BF)

    def coefficients(column, at):
        index = column + lax.broadcasted_iota(jnp.int32, (1, H), 1)
        strained = (index < count_ref[0]) | (index >= columns - H)
        strain = jnp.where(strained, row_factor, 0.0)
        for slot in range(terms):
            term = slots[slot, 0]
            row = band[pl.ds(term, 1), pl.ds(at, H)]
            row = row * (row_factor if slot == 0 else strain)
            coef[pl.ds(slot * 8, 8), :] = jnp.broadcast_to(row, (8, H))

    def plan(place):
        lane = lax.broadcasted_iota(jnp.int32, (PACK, LANE), 1)
        steps = []
        for slot in range(terms):
            if slot < 3:
                steps.append((place * tiles + (0, -tiles, tiles)[slot], None, None))
            else:
                offset = slots[slot, 1] + 8 * LANE
                turn = lax.rem(offset, LANE)
                first = place * tiles + lax.div(offset, LANE) - 8
                steps.append((first, lax.rem(LANE - turn, LANE), lane < LANE - turn))
        return steps

    def whiten_rows(steps, starts, low, width):
        acc = [[None] * width for _ in starts]
        for slot, (first, back, keep) in enumerate(steps):
            weights = []
            for t in range(width):
                weight = coef[pl.ds(slot * 8, 8), pl.ds((low + t) * LANE, LANE)]
                weights.append(jnp.concatenate([weight, weight], 0))
            for r, at_row in enumerate(starts):
                def load(t):
                    start = pl.multiple_of((first + low + t) * LANE, LANE)
                    return joint[pl.ds(at_row, PACK), pl.ds(start, LANE)]

                if back is None:
                    values = [load(t) for t in range(width)]
                else:
                    rolled = [pltpu.roll(load(t), back, 1) for t in range(width + 1)]
                    values = [jnp.where(keep, rolled[t], rolled[t + 1]) for t in range(width)]
                for t in range(width):
                    product = values[t].astype(F32) * weights[t]
                    acc[r][t] = product if acc[r][t] is None else acc[r][t] + product
        return acc

    def products(aw):
        gram[...] += lax.dot_general(
            aw[...], aw[pl.ds(0, members), :], (((1,), (1,)), ((), ())), preferred_element_type=F32)

    def whiten_chunk(place, column, at, aw, out_at):
        coefficients(column, at)
        steps = plan(place)
        acc = whiten_rows(steps, [members], 0, tiles)[0]
        row = lax.broadcasted_iota(jnp.int32, (PACK, LANE), 0)
        for t in range(tiles):
            wide = acc[t]
            high = wide.astype(BF).astype(F32)
            rest = wide - high
            middle = rest.astype(BF).astype(F32)
            low = rest - middle
            split = jnp.where(row == 0, high, jnp.where(row == 1, middle, jnp.where(row == 2, low, 0.0)))
            aw[pl.ds(members, PACK), pl.ds(t * LANE, LANE)] = split.astype(BF)
            row_out[:, pl.ds(out_at + t * LANE, LANE)] = wide[0:1] * math.sqrt(members - 1)
        width = tiles // 2
        for group in range(members // (2 * PACK)):
            starts = [group * 2 * PACK, group * 2 * PACK + PACK]
            for low in (0, width):
                acc = whiten_rows(steps, starts, low, width)
                for r, at_row in enumerate(starts):
                    for t in range(width):
                        aw[pl.ds(at_row, PACK), pl.ds((low + t) * LANE, LANE)] = acc[r][t].astype(BF)

    if edge:
        for copy in copies:
            copy.wait()
        for place in range(6):
            if place in (0, 5):
                pieces = raw[pl.ds(members, PACK), pl.ds(place * H, H)].astype(F32)
                obs_row = pieces[0:1] + pieces[1:2] + pieces[2:3]
            else:
                obs_row = obs[:, pl.ds((place - 1) * H, H)]
            anomalies(place, obs_row, joint, place * H)
        whiten_chunk(1, 0, 0, aw_a, 0)
        products(aw_a)
        whiten_chunk(4, columns - H, H, aw_b, H)
        out_copies = [
            pltpu.make_async_copy(row_out.at[:, pl.ds(0, H)], misfit_out.at[:, pl.ds(0, H)], sems.at[0]),
            pltpu.make_async_copy(row_out.at[:, pl.ds(H, H)], misfit_out.at[:, pl.ds(columns - H, H)], sems.at[1]),
        ]
        for copy in out_copies:
            copy.start()
        products(aw_b)
    else:
        def ready(place, target, at):
            anomalies(place, obs[:, pl.ds(pl.multiple_of(place * H, H), H)], target, at)

        for copy in copies:
            copy.wait()
        for place in range(3):
            chunk_copy(place).wait()
            ready(place, *((joint, place * H) if place < 2 else (fresh, 0)))

        def chunk_step(place, aw, before):
            ahead = jnp.minimum(place + 2, chunks - 1)

            @pl.when(place + 2 < chunks)
            def _():
                chunk_copy(ahead).wait()

            column = pl.multiple_of(place * H, H)
            joint[:, pl.ds(pl.multiple_of(column + H, H), H)] = fresh[...]
            products(before)
            whiten_chunk(place, column, column, aw, column)
            ready(ahead, fresh, 0)

        def pair(index, carry):
            chunk_step(1 + 2 * index, aw_a, aw_b)
            chunk_step(2 + 2 * index, aw_b, aw_a)
            return carry

        lax.fori_loop(0, (chunks - 2) // 2, pair, 0)
        inside = pl.ds(H, columns - 2 * H)
        out_copies = [pltpu.make_async_copy(row_out.at[:, inside], misfit_out.at[:, inside], sems.at[0])]
        for copy in out_copies:
            copy.start()
        products(aw_b)

    tail = gram[pl.ds(members, 8), :]
    total = tail[0:1] + tail[1:2] + tail[2:3]
    both = gram[pl.ds(0, members), :]
    top = lax.broadcasted_iota(jnp.int32, (half, half), 0)
    corner = jnp.where(top == 0, total[:, :half], jnp.where(top == 1, total[:, half:], 0.0))
    upper = jnp.concatenate([both[:half, :half], corner], 1)
    lower = both[half:]
    if edge:
        upper = upper + gram_in[pl.ds(0, half), :]
        lower = lower + gram_in[pl.ds(half, half), :]
    gram_out[pl.ds(0, half), :] = upper
    gram_out[pl.ds(half, half), :] = lower
    for copy in out_copies:
        copy.wait()


def local_call(edge, obs_total, offsets, rows_count, predicted, observed, band, *more):
    members, columns = predicted.shape
    terms = band.shape[0]
    rows = members + PACK
    places = 6 if edge else columns // H
    vmem = pl.BlockSpec(memory_space=pltpu.VMEM)
    smem = pl.BlockSpec(memory_space=pltpu.SMEM)
    anywhere = pl.BlockSpec(memory_space=pl.ANY)
    in_specs = [smem, smem, anywhere, anywhere, anywhere]
    if edge:
        in_specs += [anywhere, anywhere, vmem, anywhere]
    scratch = [
        pltpu.VMEM((rows if edge else members, places * H), BF),
        pltpu.VMEM((rows, places * H), BF),
        pltpu.VMEM((rows, H), BF),
        pltpu.VMEM((rows, H), BF),
        pltpu.VMEM((rows, H), BF),
        pltpu.VMEM((8 * terms, H), F32),
        pltpu.VMEM((rows, members), F32),
        pltpu.VMEM((rows, members), BF),
        pltpu.VMEM((1, 4 * H if edge else columns), F32),
        pltpu.VMEM((terms, 2 * H if edge else columns), F32),
        pltpu.VMEM((1, 2 * H if edge else columns), F32),
        pltpu.SMEM((8, 2), jnp.int32),
        pltpu.SemaphoreType.DMA((places + 4,)),
    ]
    work = 2 if edge else places - 2
    return pl.pallas_call(
        functools.partial(local_kernel, edge, columns, obs_total),
        out_shape=(
            jax.ShapeDtypeStruct((members, members), F32),
            jax.ShapeDtypeStruct((1, columns), F32),
        ),
        in_specs=in_specs,
        out_specs=[vmem, anywhere],
        scratch_shapes=scratch,
        input_output_aliases={8: 1} if edge else {},
        compiler_params=pltpu.CompilerParams(vmem_limit_bytes=50 * 2**20),
        cost_estimate=pl.CostEstimate(
            flops=2 * rows * members * H * work * 2, bytes_accessed=members * H * places * 2, transcendentals=0),
        name="edges" if edge else "inner",
    )(offsets, rows_count, predicted, observed, band, *more)


def update_kernel(sum_ref, params_ref, out_ref, work):
    members = params_ref.shape[1]
    highest = lax.Precision.HIGHEST
    row_index = lax.broadcasted_iota(jnp.int32, (members, members), 0)
    col_index = lax.broadcasted_iota(jnp.int32, (members, members), 1)
    identity = jnp.where(row_index == col_index, 1.0, 0.0).astype(F32)
    half = members // 2
    work[:, pl.ds(0, half)] = sum_ref[:, pl.ds(0, half)] + identity[:, :half]
    work[pl.ds(0, half), pl.ds(half, half)] = sum_ref[pl.ds(half, half), pl.ds(0, half)].T
    work[pl.ds(half, half), pl.ds(half, half)] = sum_ref[pl.ds(half, half), pl.ds(half, half)] + identity[half:, half:]
    work[:, pl.ds(members, members)] = identity
    panels = BLOCK // PANEL
    sub = lax.broadcasted_iota(jnp.int32, (PANEL, LANE), 0)
    eye = identity[:BLOCK, :BLOCK]

    def across(tile, column):
        return jnp.broadcast_to(tile[:, column:column + 1], (PANEL, LANE))

    def down(tile, row):
        return jnp.broadcast_to(tile[row:row + 1, :], (PANEL, LANE))

    for block in range(members // BLOCK):
        r0 = block * BLOCK
        start = jnp.concatenate([work[pl.ds(r0, BLOCK), pl.ds(r0, BLOCK)], eye], axis=1)
        tiles = [start[PANEL * t:PANEL * (t + 1)] for t in range(panels)]
        done = []
        for p in range(panels):
            c0 = PANEL * p
            tile = tiles[p]
            upper = tile
            full = tile
            cols = [across(tile, c0 + j) for j in range(PANEL)]
            full_cols = list(cols)
            scale = jnp.zeros((PANEL, LANE), F32)
            for k in range(PANEL):
                pivot = down(cols[k], k)
                inverse = 1.0 / pivot
                scale = jnp.where(sub == k, pivot, scale)
                below = jnp.where(sub > k, cols[k] * inverse, 0.0)

                def clear(values):
                    row = down(values, k) * inverse
                    return jnp.where(sub == k, row, values - full_cols[k] * row)

                for j in range(k + 1, PANEL):
                    cols[j] = cols[j] - below * down(cols[j], k)
                    full_cols[j] = clear(full_cols[j])
                upper = upper - below * down(upper, k)
                full = clear(full)
            done.append(upper * lax.rsqrt(scale))
            rows_of = [down(full, k) for k in range(PANEL)]
            for t in range(p + 1, panels):
                tile_t = tiles[t]
                change = [across(tile_t, c0 + k) * rows_of[k] for k in range(PANEL)]
                while len(change) > 1:
                    change = [a + b for a, b in zip(change[::2], change[1::2])]
                tiles[t] = tile_t - change[0]
        lower_inverse = jnp.concatenate(done, axis=0)[:, BLOCK:2 * BLOCK]
        solved = jnp.dot(lower_inverse, work[pl.ds(r0, BLOCK), :], precision=highest, preferred_element_type=F32)
        work[pl.ds(r0, BLOCK), :] = solved
        if r0 + BLOCK < members:
            rest = members - r0 - BLOCK
            factor = solved[:, r0 + BLOCK:members]
            work[pl.ds(r0 + BLOCK, rest), :] = work[pl.ds(r0 + BLOCK, rest), :] - lax.dot_general(
                factor, solved, (((0,), (0,)), ((), ())), precision=highest, preferred_element_type=F32)

    inverse = jnp.where(row_index >= col_index, work[:, pl.ds(members, members)], 0.0)
    projection = jnp.concatenate([sum_ref[pl.ds(r, 1), pl.ds(half, half)] for r in range(2)], 1)
    solved = jnp.sum(inverse * projection, axis=1, keepdims=True)
    weights = jnp.sum(inverse * solved, axis=0, keepdims=True)
    turned = inverse + weights
    turned = turned - jnp.mean(turned, axis=1, keepdims=True) + 1.0 / members
    high = turned.astype(BF)
    rest = turned - high.astype(F32)
    middle = rest.astype(BF)
    low = (rest - middle.astype(F32)).astype(BF)
    params = params_ref[...]

    def times(part):
        return lax.dot_general(params, part, (((1,), (1,)), ((), ())), preferred_element_type=F32)

    out_ref[...] = times(high) + (times(middle) + times(low))


def update(total, params):
    members = params.shape[1]
    vmem = pl.BlockSpec(memory_space=pltpu.VMEM)
    return pl.pallas_call(
        update_kernel,
        out_shape=jax.ShapeDtypeStruct(params.shape, F32),
        in_specs=[vmem, vmem],
        out_specs=vmem,
        scratch_shapes=[pltpu.VMEM((members, 2 * members), F32)],
        compiler_params=pltpu.CompilerParams(vmem_limit_bytes=32 * 2**20),
        name="update",
    )(total, params)


def halo_block(predicted, observed):
    high = lax.reduce_precision(observed, 8, 7)
    rest = observed - high
    middle = lax.reduce_precision(rest, 8, 7)
    low = rest - middle
    pieces = jnp.concatenate(
        [high[None], middle[None], low[None], jnp.zeros((PACK - 3, observed.shape[0]), F32)], 0)
    return jnp.concatenate([predicted, pieces.astype(BF)], 0)


def sum_over(values, axes):
    shards = lax.axis_size(axes)
    rows, width = values.shape
    parts = lax.all_to_all(values, axes, 0, 0, tiled=True)
    own = jnp.sum(parts.reshape(shards, rows // shards, width), axis=0)
    copies = jnp.broadcast_to(own[None], (shards, rows // shards, width)).reshape(rows, width)
    return lax.all_to_all(copies, axes, 0, 0, tiled=True)


def body(predicted, observed, band, offsets, rows_count, params):
    columns = predicted.shape[1]
    axes = ("obs", "par")
    shards = lax.axis_size(axes)
    obs_total = columns * shards
    up = [(i, i + 1) for i in range(shards - 1)]
    down = [(j, i) for i, j in up]
    left = lax.ppermute(halo_block(predicted[:, columns - H:], observed[columns - H:]), axes, up)
    right = lax.ppermute(halo_block(predicted[:, :H], observed[:H]), axes, down)
    obs_row = observed[None, :]
    gram, misfit = local_call(False, obs_total, offsets, rows_count, predicted, obs_row, band)
    gram, misfit = local_call(
        True, obs_total, offsets, rows_count, predicted, obs_row, band, left, right, gram, misfit)
    total = sum_over(gram, axes)
    return (update(total, params), misfit[0])


def solution(mesh):
    in_specs = (
        P(None, ("grp", "obs", "par")),
        P(("grp", "obs", "par")),
        P(None, ("grp", "obs", "par")),
        P(),
        P(("grp", "obs", "par")),
        P(("grp", "obs", "par"), None),
    )
    out_specs = (P(("grp", "obs", "par"), None), P(("grp", "obs", "par")))
    return jax.shard_map(body, mesh=mesh, in_specs=in_specs, out_specs=out_specs, check_vma=False)
```

```python
import functools
import math

import jax
import jax.numpy as jnp
from jax import lax
from jax.experimental import pallas as pl
from jax.experimental.pallas import tpu as pltpu
from jax.sharding import PartitionSpec as P

H = 1024
LANE = 128
SUB = 8
PACK = 16
BLOCK = 64
PANEL = 8
VMEM = 64 * 2**20
BF = jnp.bfloat16
F32 = jnp.float32


def local_kernel(edge, columns, obs_total, *refs):
    if edge:
        (off_ref, count_ref, pred_ref, obs_ref, band_ref, left_ref, right_ref, gram_in, misfit_in,
         gram_out, misfit_out, raw, joint, fresh, aw_a, aw_b, coef, gram, centre, obs, band, row_out, slots,
         sems) = refs
    else:
        (off_ref, count_ref, pred_ref, obs_ref, band_ref,
         gram_out, misfit_out, raw, joint, fresh, aw_a, aw_b, coef, gram, centre, obs, band, row_out, slots,
         sems) = refs
    members = pred_ref.shape[0]
    terms = band_ref.shape[0]
    chunks = columns // H
    tiles = H // LANE
    half = members // 2
    row_factor = 1.0 / math.sqrt(obs_total)

    if edge:
        copies = [
            pltpu.make_async_copy(left_ref, raw.at[:, pl.ds(0, H)], sems.at[0]),
            pltpu.make_async_copy(right_ref, raw.at[:, pl.ds(5 * H, H)], sems.at[5]),
        ]
        for place, chunk in ((1, 0), (2, 1), (3, chunks - 2), (4, chunks - 1)):
            copies.append(pltpu.make_async_copy(
                pred_ref.at[:, pl.ds(chunk * H, H)],
                raw.at[pl.ds(0, members), pl.ds(place * H, H)], sems.at[place]))
        for which in range(2):
            there = which * (columns - 2 * H)
            copies.append(pltpu.make_async_copy(
                obs_ref.at[:, pl.ds(there, 2 * H)], obs.at[:, pl.ds(which * 2 * H, 2 * H)], sems.at[6 + which]))
            there = which * (columns - H)
            copies.append(pltpu.make_async_copy(
                band_ref.at[:, pl.ds(there, H)], band.at[:, pl.ds(which * H, H)], sems.at[8 + which]))
        for copy in copies:
            copy.start()
    else:
        def chunk_copy(place):
            start = pl.multiple_of(place * H, H)
            return pltpu.make_async_copy(
                pred_ref.at[:, pl.ds(start, H)], raw.at[:, pl.ds(start, H)], sems.at[place])

        copies = [
            pltpu.make_async_copy(obs_ref, obs, sems.at[chunks]),
            pltpu.make_async_copy(band_ref, band, sems.at[chunks + 1]),
        ]
        for place in range(chunks):
            chunk_copy(place).start()
            if place == 2:
                for copy in copies:
                    copy.start()

    slots[0, 0] = 0
    slots[0, 1] = 0
    free = jnp.int32(3)
    for term in range(1, terms):
        offset = off_ref[term]
        whole = (offset == H) | (offset == -H)
        place = jnp.where(offset == -H, 1, jnp.where(offset == H, 2, free))
        place = jnp.minimum(place, terms - 1)
        slots[place, 0] = jnp.int32(term)
        slots[place, 1] = offset
        free = free + jnp.where(whole, 0, 1)

    rows = members + PACK
    row_index = lax.broadcasted_iota(jnp.int32, (rows, members), 0)
    col_index = lax.broadcasted_iota(jnp.int32, (rows, members), 1)
    mean_part = 1.0 / members
    centre[...] = jnp.where(
        row_index >= members, mean_part, jnp.where(row_index == col_index, 1.0 - mean_part, -mean_part)
    ).astype(BF)
    gram[...] = jnp.zeros_like(gram)
    if not edge:
        aw_b[...] = jnp.zeros_like(aw_b)

    def anomalies(place, obs_row, target, at):
        wide = jnp.dot(
            centre[...], raw[pl.ds(0, members), pl.ds(pl.multiple_of(place * H, H), H)],
            preferred_element_type=F32)
        target[pl.ds(0, members), pl.ds(at, H)] = wide[:members]
        innovation = obs_row - wide[members:members + SUB]
        target[pl.ds(members, SUB), pl.ds(at, H)] = innovation.astype(BF).astype(F32)

    def coefficients(column, at):
        index = column + lax.broadcasted_iota(jnp.int32, (1, H), 1)
        strained = (index < count_ref[0]) | (index >= columns - H)
        strain = jnp.where(strained, 1.0, 0.0)
        for slot in range(terms):
            term = slots[slot, 0]
            row = band[pl.ds(term, 1), pl.ds(at, H)]
            if slot > 0:
                row = row * strain
            coef[pl.ds(slot * SUB, SUB), :] = jnp.broadcast_to(row, (SUB, H))

    def plan(place):
        lane = lax.broadcasted_iota(jnp.int32, (SUB, LANE), 1)
        steps = []
        for slot in range(terms):
            if slot < 3:
                steps.append((place * tiles + (0, -tiles, tiles)[slot], None, None))
            else:
                offset = slots[slot, 1] + 8 * LANE
                turn = lax.rem(offset, LANE)
                first = place * tiles + lax.div(offset, LANE) - 8
                steps.append((first, lax.rem(LANE - turn, LANE), lane < LANE - turn))
        return steps

    def whiten_rows(steps, starts):
        acc = [[None] * tiles for _ in starts]
        for slot, (first, back, keep) in enumerate(steps):
            weights = [coef[pl.ds(slot * SUB, SUB), pl.ds(t * LANE, LANE)] for t in range(tiles)]
            for r, at_row in enumerate(starts):
                def load(t):
                    start = pl.multiple_of((first + t) * LANE, LANE)
                    return joint[pl.ds(at_row, SUB), pl.ds(start, LANE)]

                if back is None:
                    values = [load(t) for t in range(tiles)]
                else:
                    rolled = [pltpu.roll(load(t), back, 1) for t in range(tiles + 1)]
                    values = [jnp.where(keep, rolled[t], rolled[t + 1]) for t in range(tiles)]
                for t in range(tiles):
                    product = values[t] * weights[t]
                    acc[r][t] = product if acc[r][t] is None else acc[r][t] + product
        return acc

    def products(aw):
        gram[...] += lax.dot_general(
            aw[...], aw[pl.ds(0, members), :], (((1,), (1,)), ((), ())), preferred_element_type=F32)

    def whiten_chunk(place, column, at, aw, out_at):
        coefficients(column, at)
        steps = plan(place)
        acc = whiten_rows(steps, [members])[0]
        row = lax.broadcasted_iota(jnp.int32, (PACK, LANE), 0)
        for t in range(tiles):
            row_out[:, pl.ds(out_at + t * LANE, LANE)] = acc[t][0:1] * (math.sqrt(members - 1) * row_factor)
            wide = jnp.concatenate([acc[t], acc[t]], 0)
            high = wide.astype(BF).astype(F32)
            rest = wide - high
            middle = rest.astype(BF).astype(F32)
            low = rest - middle
            split = jnp.where(row == 0, high, jnp.where(row == 1, middle, jnp.where(row == 2, low, 0.0)))
            aw[pl.ds(members, PACK), pl.ds(t * LANE, LANE)] = split.astype(BF)
        for group in range(members // PACK):
            low, high = whiten_rows(steps, [group * PACK, group * PACK + SUB])
            for t in range(tiles):
                aw[pl.ds(group * PACK, PACK), pl.ds(t * LANE, LANE)] = jnp.concatenate(
                    [low[t], high[t]], 0).astype(BF)

    if edge:
        for copy in copies:
            copy.wait()
        for place in range(6):
            if place in (0, 5):
                pieces = raw[pl.ds(members, PACK), pl.ds(place * H, H)].astype(F32)
                obs_row = pieces[0:1] + pieces[1:2] + pieces[2:3]
            else:
                obs_row = obs[:, pl.ds((place - 1) * H, H)]
            anomalies(place, obs_row, joint, place * H)
        whiten_chunk(1, 0, 0, aw_a, 0)
        products(aw_a)
        whiten_chunk(4, columns - H, H, aw_b, H)
        out_copies = [
            pltpu.make_async_copy(row_out.at[:, pl.ds(0, H)], misfit_out.at[:, pl.ds(0, H)], sems.at[0]),
            pltpu.make_async_copy(row_out.at[:, pl.ds(H, H)], misfit_out.at[:, pl.ds(columns - H, H)], sems.at[1]),
        ]
        for copy in out_copies:
            copy.start()
        products(aw_b)
    else:
        def ready(place, target, at):
            anomalies(place, obs[:, pl.ds(pl.multiple_of(place * H, H), H)], target, at)

        for copy in copies:
            copy.wait()
        for place in range(3):
            chunk_copy(place).wait()
            ready(place, *((joint, place * H) if place < 2 else (fresh, 0)))

        def chunk_step(place, aw, before):
            ahead = jnp.minimum(place + 2, chunks - 1)

            @pl.when(place + 2 < chunks)
            def _():
                chunk_copy(ahead).wait()

            column = pl.multiple_of(place * H, H)
            joint[:, pl.ds(pl.multiple_of(column + H, H), H)] = fresh[...]
            products(before)
            whiten_chunk(place, column, column, aw, column)
            ready(ahead, fresh, 0)

        def pair(index, carry):
            chunk_step(1 + 2 * index, aw_a, aw_b)
            chunk_step(2 + 2 * index, aw_b, aw_a)
            return carry

        lax.fori_loop(0, (chunks - 2) // 2, pair, 0)
        inside = pl.ds(H, columns - 2 * H)
        out_copies = [pltpu.make_async_copy(row_out.at[:, inside], misfit_out.at[:, inside], sems.at[0])]
        for copy in out_copies:
            copy.start()
        products(aw_b)

    tail = gram[pl.ds(members, 8), :]
    total = tail[0:1] + tail[1:2] + tail[2:3]
    both = gram[pl.ds(0, members), :]
    top = lax.broadcasted_iota(jnp.int32, (half, half), 0)
    corner = jnp.where(top == 0, total[:, :half], jnp.where(top == 1, total[:, half:], 0.0))
    upper = jnp.concatenate([both[:half, :half], corner], 1)
    lower = both[half:]
    upper = upper * (1.0 / obs_total)
    lower = lower * (1.0 / obs_total)
    if edge:
        upper = upper + gram_in[pl.ds(0, half), :]
        lower = lower + gram_in[pl.ds(half, half), :]
    gram_out[pl.ds(0, half), :] = upper
    gram_out[pl.ds(half, half), :] = lower
    for copy in out_copies:
        copy.wait()


def local_call(edge, obs_total, offsets, rows_count, predicted, observed, band, *more):
    members, columns = predicted.shape
    terms = band.shape[0]
    rows = members + PACK
    places = 6 if edge else columns // H
    vmem = pl.BlockSpec(memory_space=pltpu.VMEM)
    smem = pl.BlockSpec(memory_space=pltpu.SMEM)
    far = pl.BlockSpec(memory_space=pltpu.HBM)
    in_specs = [smem, smem, far, far, far]
    if edge:
        in_specs += [far, far, vmem, far]
    scratch = [
        pltpu.VMEM((rows if edge else members, places * H), BF),
        pltpu.VMEM((members + SUB, places * H), F32),
        pltpu.VMEM((members + SUB, H), F32),
        pltpu.VMEM((rows, H), BF),
        pltpu.VMEM((rows, H), BF),
        pltpu.VMEM((SUB * terms, H), F32),
        pltpu.VMEM((rows, members), F32),
        pltpu.VMEM((rows, members), BF),
        pltpu.VMEM((1, 4 * H if edge else columns), F32),
        pltpu.VMEM((terms, 2 * H if edge else columns), F32),
        pltpu.VMEM((1, 2 * H if edge else columns), F32),
        pltpu.SMEM((8, 2), jnp.int32),
        pltpu.SemaphoreType.DMA((places + 4,)),
    ]
    work = 2 if edge else places - 2
    return pl.pallas_call(
        functools.partial(local_kernel, edge, columns, obs_total),
        out_shape=(
            jax.ShapeDtypeStruct((members, members), F32),
            jax.ShapeDtypeStruct((1, columns), F32),
        ),
        in_specs=in_specs,
        out_specs=[vmem, far],
        scratch_shapes=scratch,
        input_output_aliases={8: 1} if edge else {},
        compiler_params=pltpu.CompilerParams(vmem_limit_bytes=VMEM),
        cost_estimate=pl.CostEstimate(
            flops=2 * rows * members * H * work * 2, bytes_accessed=members * H * places * 2, transcendentals=0),
        name="edges" if edge else "inner",
    )(offsets, rows_count, predicted, observed, band, *more)


def update_kernel(sum_ref, params_ref, out_ref, work):
    members = params_ref.shape[1]
    highest = lax.Precision.HIGHEST
    row_index = lax.broadcasted_iota(jnp.int32, (members, members), 0)
    col_index = lax.broadcasted_iota(jnp.int32, (members, members), 1)
    identity = jnp.where(row_index == col_index, 1.0, 0.0).astype(F32)
    half = members // 2
    work[:, pl.ds(0, half)] = sum_ref[:, pl.ds(0, half)] + identity[:, :half]
    work[pl.ds(0, half), pl.ds(half, half)] = sum_ref[pl.ds(half, half), pl.ds(0, half)].T
    work[pl.ds(half, half), pl.ds(half, half)] = sum_ref[pl.ds(half, half), pl.ds(half, half)] + identity[half:, half:]
    work[:, pl.ds(members, members)] = identity
    panels = BLOCK // PANEL
    sub = lax.broadcasted_iota(jnp.int32, (PANEL, LANE), 0)
    eye = identity[:BLOCK, :BLOCK]

    def across(tile, column):
        return jnp.broadcast_to(tile[:, column:column + 1], (PANEL, LANE))

    def down(tile, row):
        return jnp.broadcast_to(tile[row:row + 1, :], (PANEL, LANE))

    for block in range(members // BLOCK):
        r0 = block * BLOCK
        start = jnp.concatenate([work[pl.ds(r0, BLOCK), pl.ds(r0, BLOCK)], eye], axis=1)
        tiles = [start[PANEL * t:PANEL * (t + 1)] for t in range(panels)]
        done = []
        for p in range(panels):
            c0 = PANEL * p
            tile = tiles[p]
            upper = tile
            full = tile
            cols = [across(tile, c0 + j) for j in range(PANEL)]
            full_cols = list(cols)
            scale = jnp.zeros((PANEL, LANE), F32)
            for k in range(PANEL):
                pivot = down(cols[k], k)
                inverse = 1.0 / pivot
                scale = jnp.where(sub == k, pivot, scale)
                below = jnp.where(sub > k, cols[k] * inverse, 0.0)

                def clear(values):
                    row = down(values, k) * inverse
                    return jnp.where(sub == k, row, values - full_cols[k] * row)

                for j in range(k + 1, PANEL):
                    cols[j] = cols[j] - below * down(cols[j], k)
                    full_cols[j] = clear(full_cols[j])
                upper = upper - below * down(upper, k)
                full = clear(full)
            done.append(upper * lax.rsqrt(scale))
            rows_of = [down(full, k) for k in range(PANEL)]
            for t in range(p + 1, panels):
                tile_t = tiles[t]
                change = [across(tile_t, c0 + k) * rows_of[k] for k in range(PANEL)]
                while len(change) > 1:
                    change = [a + b for a, b in zip(change[::2], change[1::2])]
                tiles[t] = tile_t - change[0]
        lower_inverse = jnp.concatenate(done, axis=0)[:, BLOCK:2 * BLOCK]
        solved = jnp.dot(lower_inverse, work[pl.ds(r0, BLOCK), :], precision=highest, preferred_element_type=F32)
        work[pl.ds(r0, BLOCK), :] = solved
        if r0 + BLOCK < members:
            rest = members - r0 - BLOCK
            factor = solved[:, r0 + BLOCK:members]
            work[pl.ds(r0 + BLOCK, rest), :] = work[pl.ds(r0 + BLOCK, rest), :] - lax.dot_general(
                factor, solved, (((0,), (0,)), ((), ())), precision=highest, preferred_element_type=F32)

    inverse = jnp.where(row_index >= col_index, work[:, pl.ds(members, members)], 0.0)
    projection = jnp.concatenate([sum_ref[pl.ds(r, 1), pl.ds(half, half)] for r in range(2)], 1)
    solved = jnp.sum(inverse * projection, axis=1, keepdims=True)
    weights = jnp.sum(inverse * solved, axis=0, keepdims=True)
    turned = inverse + weights
    turned = turned - jnp.mean(turned, axis=1, keepdims=True) + 1.0 / members
    high = turned.astype(BF)
    rest = turned - high.astype(F32)
    middle = rest.astype(BF)
    low = (rest - middle.astype(F32)).astype(BF)
    params = params_ref[...]

    def times(part):
        return lax.dot_general(params, part, (((1,), (1,)), ((), ())), preferred_element_type=F32)

    out_ref[...] = times(high) + (times(middle) + times(low))


def update(total, params):
    members = params.shape[1]
    vmem = pl.BlockSpec(memory_space=pltpu.VMEM)
    return pl.pallas_call(
        update_kernel,
        out_shape=jax.ShapeDtypeStruct(params.shape, F32),
        in_specs=[vmem, vmem],
        out_specs=vmem,
        scratch_shapes=[pltpu.VMEM((members, 2 * members), F32)],
        compiler_params=pltpu.CompilerParams(vmem_limit_bytes=VMEM),
        name="update",
    )(total, params)


def halo_kernel(columns, pred_ref, obs_ref, first_ref, last_ref, obs, pieces, sems):
    members = pred_ref.shape[0]
    copies = []
    for side, (out, at) in enumerate(((first_ref, 0), (last_ref, columns - H))):
        copies.append(pltpu.make_async_copy(
            pred_ref.at[:, pl.ds(at, H)], out.at[pl.ds(0, members), :], sems.at[side]))
        copies.append(pltpu.make_async_copy(
            obs_ref.at[:, pl.ds(at, H)], obs.at[:, pl.ds(side * H, H)], sems.at[2 + side]))
    for copy in copies:
        copy.start()
    for copy in copies[1::2]:
        copy.wait()
    wide = jnp.broadcast_to(obs[...], (PACK, 2 * H))
    high = wide.astype(BF).astype(F32)
    rest = wide - high
    middle = rest.astype(BF).astype(F32)
    low = rest - middle
    row = lax.broadcasted_iota(jnp.int32, (PACK, 2 * H), 0)
    split = jnp.where(row == 0, high, jnp.where(row == 1, middle, jnp.where(row == 2, low, 0.0)))
    pieces[...] = split.astype(BF)
    ends = [
        pltpu.make_async_copy(
            pieces.at[:, pl.ds(side * H, H)], out.at[pl.ds(members, PACK), :], sems.at[4 + side])
        for side, out in enumerate((first_ref, last_ref))
    ]
    for copy in ends:
        copy.start()
    for copy in copies[0::2] + ends:
        copy.wait()


def halo_blocks(predicted, observed):
    members, columns = predicted.shape
    far = pl.BlockSpec(memory_space=pltpu.HBM)
    block = jax.ShapeDtypeStruct((members + PACK, H), BF)
    return pl.pallas_call(
        functools.partial(halo_kernel, columns),
        out_shape=(block, block),
        in_specs=[far, far],
        out_specs=[far, far],
        scratch_shapes=[
            pltpu.VMEM((1, 2 * H), F32), pltpu.VMEM((PACK, 2 * H), BF), pltpu.SemaphoreType.DMA((6,))],
        compiler_params=pltpu.CompilerParams(vmem_limit_bytes=VMEM),
        name="halos",
    )(predicted, observed)


def sum_over(values, axes):
    shards = lax.axis_size(axes)
    rows, width = values.shape
    parts = lax.all_to_all(values, axes, 0, 0, tiled=True)
    own = jnp.sum(parts.reshape(shards, rows // shards, width), axis=0)
    copies = jnp.broadcast_to(own[None], (shards, rows // shards, width)).reshape(rows, width)
    return lax.all_to_all(copies, axes, 0, 0, tiled=True)


def body(predicted, observed, band, offsets, rows_count, params):
    columns = predicted.shape[1]
    axes = ("obs", "par")
    shards = lax.axis_size(axes)
    obs_total = columns * shards
    up = [(i, i + 1) for i in range(shards - 1)]
    down = [(j, i) for i, j in up]
    obs_row = observed[None, :]
    first, last = halo_blocks(predicted, obs_row)
    left = lax.ppermute(last, axes, up)
    right = lax.ppermute(first, axes, down)
    gram, misfit = local_call(False, obs_total, offsets, rows_count, predicted, obs_row, band)
    gram, misfit = local_call(
        True, obs_total, offsets, rows_count, predicted, obs_row, band, left, right, gram, misfit)
    total = sum_over(gram, axes)
    return (update(total, params), misfit[0])


def solution(mesh):
    in_specs = (
        P(None, ("grp", "obs", "par")),
        P(("grp", "obs", "par")),
        P(None, ("grp", "obs", "par")),
        P(),
        P(("grp", "obs", "par")),
        P(("grp", "obs", "par"), None),
    )
    out_specs = (P(("grp", "obs", "par"), None), P(("grp", "obs", "par")))
    return jax.shard_map(body, mesh=mesh, in_specs=in_specs, out_specs=out_specs, check_vma=False)
```

```python
import functools
import math

import jax
import jax.numpy as jnp
from jax import lax
from jax.experimental import pallas as pl
from jax.experimental.pallas import tpu as pltpu
from jax.sharding import PartitionSpec as P

H = 1024
LANE = 128
SUB = 8
PACK = 16
GROUP = 64
BLOCK = 64
PANEL = 8
VMEM = 64 * 2**20
BF = jnp.bfloat16
F32 = jnp.float32


def local_kernel(edge, columns, obs_total, *refs):
    if edge:
        (off_ref, count_ref, pred_ref, obs_ref, band_ref, left_ref, right_ref, gram_in, misfit_in,
         gram_out, misfit_out, raw, joint, aw, coef, gram, centre, obs, band, row_out, slots,
         sems) = refs
    else:
        (off_ref, count_ref, pred_ref, obs_ref, band_ref,
         gram_out, misfit_out, raw, joint, aw, coef, gram, centre, obs, band, row_out, slots,
         sems) = refs
    members = pred_ref.shape[0]
    terms = band_ref.shape[0]
    chunks = columns // H
    tiles = H // LANE
    half = members // 2
    row_factor = 1.0 / math.sqrt(obs_total)

    if edge:
        copies = [
            pltpu.make_async_copy(left_ref, raw.at[:, pl.ds(0, H)], sems.at[0]),
            pltpu.make_async_copy(right_ref, raw.at[:, pl.ds(5 * H, H)], sems.at[5]),
        ]
        for place, chunk in ((1, 0), (2, 1), (3, chunks - 2), (4, chunks - 1)):
            copies.append(pltpu.make_async_copy(
                pred_ref.at[:, pl.ds(chunk * H, H)],
                raw.at[pl.ds(0, members), pl.ds(place * H, H)], sems.at[place]))
        for which in range(2):
            there = which * (columns - 2 * H)
            copies.append(pltpu.make_async_copy(
                obs_ref.at[:, pl.ds(there, 2 * H)], obs.at[:, pl.ds((1 + which * 2) * H, 2 * H)], sems.at[6 + which]))
            there = which * (columns - H)
            copies.append(pltpu.make_async_copy(
                band_ref.at[:, pl.ds(there, H)], band.at[:, pl.ds(which * H, H)], sems.at[8 + which]))
        for copy in copies:
            copy.start()
    else:
        def chunk_copy(place):
            start = pl.multiple_of(place * H, H)
            return pltpu.make_async_copy(
                pred_ref.at[:, pl.ds(start, H)], raw.at[:, pl.ds(start, H)], sems.at[place])

        copies = [
            pltpu.make_async_copy(obs_ref, obs, sems.at[chunks]),
            pltpu.make_async_copy(band_ref, band, sems.at[chunks + 1]),
        ]
        for place in range(chunks):
            chunk_copy(place).start()
            if place == 2:
                for copy in copies:
                    copy.start()

    slots[0, 0] = 0
    slots[0, 1] = 0
    free = jnp.int32(3)
    for term in range(1, terms):
        offset = off_ref[term]
        whole = (offset == H) | (offset == -H)
        place = jnp.where(offset == -H, 1, jnp.where(offset == H, 2, free))
        place = jnp.minimum(place, terms - 1)
        slots[place, 0] = jnp.int32(term)
        slots[place, 1] = offset
        free = free + jnp.where(whole, 0, 1)

    rows = members + PACK
    row_index = lax.broadcasted_iota(jnp.int32, (rows, members), 0)
    col_index = lax.broadcasted_iota(jnp.int32, (rows, members), 1)
    mean_part = 1.0 / members
    centre[...] = jnp.where(
        row_index >= members, mean_part, jnp.where(row_index == col_index, 1.0 - mean_part, -mean_part)
    ).astype(BF)
    gram[...] = jnp.zeros_like(gram)
    aw[...] = jnp.zeros_like(aw)

    def anomalies(place):
        at = pl.ds(pl.multiple_of(place * H, H), H)
        wide = jnp.dot(centre[...], raw[pl.ds(0, members), at], preferred_element_type=F32)
        joint[pl.ds(0, members), at] = wide[:members]
        innovation = obs[:, at] - wide[members:members + SUB]
        joint[pl.ds(members, SUB), at] = innovation.astype(BF).astype(F32)

    def coefficients(column, at):
        index = column + lax.broadcasted_iota(jnp.int32, (1, H), 1)
        strained = (index < count_ref[0]) | (index >= columns - H)
        strain = jnp.where(strained, 1.0, 0.0)
        for slot in range(terms):
            term = slots[slot, 0]
            row = band[pl.ds(term, 1), pl.ds(at, H)]
            if slot > 0:
                row = row * strain
            coef[pl.ds(slot * SUB, SUB), :] = jnp.broadcast_to(row, (SUB, H))

    def plan(place):
        lane = lax.broadcasted_iota(jnp.int32, (SUB, LANE), 1)
        steps = []
        for slot in range(terms):
            if slot < 3:
                steps.append((place * tiles + (0, -tiles, tiles)[slot], None, None))
            else:
                offset = slots[slot, 1] + 8 * LANE
                turn = lax.rem(offset, LANE)
                first = place * tiles + lax.div(offset, LANE) - 8
                steps.append((first, lax.rem(LANE - turn, LANE), lane < LANE - turn))
        return steps

    def whiten_rows(steps, starts):
        acc = [[None] * tiles for _ in starts]
        for slot, (first, back, keep) in enumerate(steps):
            weights = [coef[pl.ds(slot * SUB, SUB), pl.ds(t * LANE, LANE)] for t in range(tiles)]
            for r, at_row in enumerate(starts):
                def load(t):
                    start = pl.multiple_of((first + t) * LANE, LANE)
                    return joint[pl.ds(at_row, SUB), pl.ds(start, LANE)]

                if back is None:
                    values = [load(t) for t in range(tiles)]
                else:
                    rolled = [pltpu.roll(load(t), back, 1) for t in range(tiles + 1)]
                    values = [jnp.where(keep, rolled[t], rolled[t + 1]) for t in range(tiles)]
                for t in range(tiles):
                    product = values[t] * weights[t]
                    acc[r][t] = product if acc[r][t] is None else acc[r][t] + product
        return acc

    def products():
        gram[...] += lax.dot_general(
            aw[...], aw[pl.ds(0, members), :], (((1,), (1,)), ((), ())), preferred_element_type=F32)

    def whiten_chunk(place, column, at):
        coefficients(column, at)
        steps = plan(place)
        acc = whiten_rows(steps, [members])[0]
        row = lax.broadcasted_iota(jnp.int32, (PACK, LANE), 0)
        for t in range(tiles):
            row_out[:, pl.ds(at + t * LANE, LANE)] = acc[t][0:1] * (math.sqrt(members - 1) * row_factor)
            wide = jnp.concatenate([acc[t], acc[t]], 0)
            high = wide.astype(BF).astype(F32)
            rest = wide - high
            middle = rest.astype(BF).astype(F32)
            low = rest - middle
            split = jnp.where(row == 0, high, jnp.where(row == 1, middle, jnp.where(row == 2, low, 0.0)))
            aw[pl.ds(members, PACK), pl.ds(t * LANE, LANE)] = split.astype(BF)

        def group(index, carry):
            for pair in range(GROUP // PACK):
                at_row = pl.multiple_of(index * GROUP + pair * PACK, PACK)
                low, high = whiten_rows(steps, [at_row, pl.multiple_of(at_row + SUB, SUB)])
                for t in range(tiles):
                    aw[pl.ds(at_row, PACK), pl.ds(t * LANE, LANE)] = jnp.concatenate(
                        [low[t], high[t]], 0).astype(BF)
            return carry

        lax.fori_loop(0, members // GROUP, group, 0)

    if edge:
        for copy in copies:
            copy.wait()
        for place in (0, 5):
            pieces = raw[pl.ds(members, PACK), pl.ds(place * H, H)].astype(F32)
            obs[:, pl.ds(place * H, H)] = pieces[0:1] + pieces[1:2] + pieces[2:3]

        def centre_step(place, carry):
            anomalies(place)
            return carry

        lax.fori_loop(0, 6, centre_step, 0)

        def chunk_step(which, carry):
            products()
            whiten_chunk(1 + 3 * which, which * (columns - H), pl.multiple_of(which * H, H))
            return carry

        lax.fori_loop(0, 2, chunk_step, 0)
        out_copies = [
            pltpu.make_async_copy(row_out.at[:, pl.ds(0, H)], misfit_out.at[:, pl.ds(0, H)], sems.at[0]),
            pltpu.make_async_copy(row_out.at[:, pl.ds(H, H)], misfit_out.at[:, pl.ds(columns - H, H)], sems.at[1]),
        ]
    else:
        for copy in copies:
            copy.wait()

        def centre_step(place, carry):
            chunk_copy(place).wait()
            anomalies(place)
            return carry

        lax.fori_loop(0, 2, centre_step, 0)

        def chunk_step(place, carry):
            chunk_copy(place + 1).wait()
            products()
            anomalies(place + 1)
            column = pl.multiple_of(place * H, H)
            whiten_chunk(place, column, column)
            return carry

        lax.fori_loop(1, chunks - 1, chunk_step, 0)
        inside = pl.ds(H, columns - 2 * H)
        out_copies = [pltpu.make_async_copy(row_out.at[:, inside], misfit_out.at[:, inside], sems.at[0])]
    for copy in out_copies:
        copy.start()
    products()

    tail = gram[pl.ds(members, 8), :]
    total = tail[0:1] + tail[1:2] + tail[2:3]
    both = gram[pl.ds(0, members), :]
    top = lax.broadcasted_iota(jnp.int32, (half, half), 0)
    corner = jnp.where(top == 0, total[:, :half], jnp.where(top == 1, total[:, half:], 0.0))
    upper = jnp.concatenate([both[:half, :half], corner], 1)
    lower = both[half:]
    upper = upper * (1.0 / obs_total)
    lower = lower * (1.0 / obs_total)
    if edge:
        upper = upper + gram_in[pl.ds(0, half), :]
        lower = lower + gram_in[pl.ds(half, half), :]
    gram_out[pl.ds(0, half), :] = upper
    gram_out[pl.ds(half, half), :] = lower
    for copy in out_copies:
        copy.wait()


def local_call(edge, obs_total, offsets, rows_count, predicted, observed, band, *more):
    members, columns = predicted.shape
    terms = band.shape[0]
    rows = members + PACK
    places = 6 if edge else columns // H
    vmem = pl.BlockSpec(memory_space=pltpu.VMEM)
    smem = pl.BlockSpec(memory_space=pltpu.SMEM)
    far = pl.BlockSpec(memory_space=pltpu.HBM)
    in_specs = [smem, smem, far, far, far]
    if edge:
        in_specs += [far, far, vmem, far]
    scratch = [
        pltpu.VMEM((rows if edge else members, places * H), BF),
        pltpu.VMEM((members + SUB, places * H), F32),
        pltpu.VMEM((rows, H), BF),
        pltpu.VMEM((SUB * terms, H), F32),
        pltpu.VMEM((rows, members), F32),
        pltpu.VMEM((rows, members), BF),
        pltpu.VMEM((1, places * H), F32),
        pltpu.VMEM((terms, 2 * H if edge else columns), F32),
        pltpu.VMEM((1, 2 * H if edge else columns), F32),
        pltpu.SMEM((8, 2), jnp.int32),
        pltpu.SemaphoreType.DMA((places + 4,)),
    ]
    work = 2 if edge else places - 2
    return pl.pallas_call(
        functools.partial(local_kernel, edge, columns, obs_total),
        out_shape=(
            jax.ShapeDtypeStruct((members, members), F32),
            jax.ShapeDtypeStruct((1, columns), F32),
        ),
        in_specs=in_specs,
        out_specs=[vmem, far],
        scratch_shapes=scratch,
        input_output_aliases={8: 1} if edge else {},
        compiler_params=pltpu.CompilerParams(vmem_limit_bytes=VMEM),
        cost_estimate=pl.CostEstimate(
            flops=2 * rows * members * H * work * 2, bytes_accessed=members * H * places * 2, transcendentals=0),
        name="edges" if edge else "inner",
    )(offsets, rows_count, predicted, observed, band, *more)


def update_kernel(sum_ref, params_ref, out_ref, work):
    members = params_ref.shape[1]
    highest = lax.Precision.HIGHEST
    row_index = lax.broadcasted_iota(jnp.int32, (members, members), 0)
    col_index = lax.broadcasted_iota(jnp.int32, (members, members), 1)
    identity = jnp.where(row_index == col_index, 1.0, 0.0).astype(F32)
    half = members // 2
    work[:, pl.ds(0, half)] = sum_ref[:, pl.ds(0, half)] + identity[:, :half]
    work[pl.ds(0, half), pl.ds(half, half)] = sum_ref[pl.ds(half, half), pl.ds(0, half)].T
    work[pl.ds(half, half), pl.ds(half, half)] = sum_ref[pl.ds(half, half), pl.ds(half, half)] + identity[half:, half:]
    work[:, pl.ds(members, members)] = identity
    panels = BLOCK // PANEL
    sub = lax.broadcasted_iota(jnp.int32, (PANEL, LANE), 0)
    eye = identity[:BLOCK, :BLOCK]

    def across(tile, column):
        return jnp.broadcast_to(tile[:, column:column + 1], (PANEL, LANE))

    def down(tile, row):
        return jnp.broadcast_to(tile[row:row + 1, :], (PANEL, LANE))

    for block in range(members // BLOCK):
        r0 = block * BLOCK
        start = jnp.concatenate([work[pl.ds(r0, BLOCK), pl.ds(r0, BLOCK)], eye], axis=1)
        tiles = [start[PANEL * t:PANEL * (t + 1)] for t in range(panels)]
        done = []
        for p in range(panels):
            c0 = PANEL * p
            tile = tiles[p]
            upper = tile
            full = tile
            cols = [across(tile, c0 + j) for j in range(PANEL)]
            full_cols = list(cols)
            scale = jnp.zeros((PANEL, LANE), F32)
            for k in range(PANEL):
                pivot = down(cols[k], k)
                inverse = 1.0 / pivot
                scale = jnp.where(sub == k, pivot, scale)
                below = jnp.where(sub > k, cols[k] * inverse, 0.0)

                def clear(values):
                    row = down(values, k) * inverse
                    return jnp.where(sub == k, row, values - full_cols[k] * row)

                for j in range(k + 1, PANEL):
                    cols[j] = cols[j] - below * down(cols[j], k)
                    full_cols[j] = clear(full_cols[j])
                upper = upper - below * down(upper, k)
                full = clear(full)
            done.append(upper * lax.rsqrt(scale))
            rows_of = [down(full, k) for k in range(PANEL)]
            for t in range(p + 1, panels):
                tile_t = tiles[t]
                change = [across(tile_t, c0 + k) * rows_of[k] for k in range(PANEL)]
                while len(change) > 1:
                    change = [a + b for a, b in zip(change[::2], change[1::2])]
                tiles[t] = tile_t - change[0]
        lower_inverse = jnp.concatenate(done, axis=0)[:, BLOCK:2 * BLOCK]
        solved = jnp.dot(lower_inverse, work[pl.ds(r0, BLOCK), :], precision=highest, preferred_element_type=F32)
        work[pl.ds(r0, BLOCK), :] = solved
        if r0 + BLOCK < members:
            rest = members - r0 - BLOCK
            factor = solved[:, r0 + BLOCK:members]
            work[pl.ds(r0 + BLOCK, rest), :] = work[pl.ds(r0 + BLOCK, rest), :] - lax.dot_general(
                factor, solved, (((0,), (0,)), ((), ())), precision=highest, preferred_element_type=F32)

    inverse = jnp.where(row_index >= col_index, work[:, pl.ds(members, members)], 0.0)
    projection = jnp.concatenate([sum_ref[pl.ds(r, 1), pl.ds(half, half)] for r in range(2)], 1)
    solved = jnp.sum(inverse * projection, axis=1, keepdims=True)
    weights = jnp.sum(inverse * solved, axis=0, keepdims=True)
    turned = inverse + weights
    turned = turned - jnp.mean(turned, axis=1, keepdims=True) + 1.0 / members
    high = turned.astype(BF)
    rest = turned - high.astype(F32)
    middle = rest.astype(BF)
    low = (rest - middle.astype(F32)).astype(BF)
    params = params_ref[...]

    def times(part):
        return lax.dot_general(params, part, (((1,), (1,)), ((), ())), preferred_element_type=F32)

    out_ref[...] = times(high) + (times(middle) + times(low))


def update(total, params):
    members = params.shape[1]
    vmem = pl.BlockSpec(memory_space=pltpu.VMEM)
    return pl.pallas_call(
        update_kernel,
        out_shape=jax.ShapeDtypeStruct(params.shape, F32),
        in_specs=[vmem, vmem],
        out_specs=vmem,
        scratch_shapes=[pltpu.VMEM((members, 2 * members), F32)],
        compiler_params=pltpu.CompilerParams(vmem_limit_bytes=VMEM),
        name="update",
    )(total, params)


def halo_kernel(columns, pred_ref, obs_ref, first_ref, last_ref, obs, sems):
    members = pred_ref.shape[0]
    copies = []
    for side, (out, at) in enumerate(((first_ref, 0), (last_ref, columns - H))):
        copies.append(pltpu.make_async_copy(
            pred_ref.at[:, pl.ds(at, H)], out.at[pl.ds(0, members), :], sems.at[side]))
        copies.append(pltpu.make_async_copy(
            obs_ref.at[:, pl.ds(at, H)], obs.at[:, pl.ds(side * H, H)], sems.at[2 + side]))
    for copy in copies:
        copy.start()
    for copy in copies[1::2]:
        copy.wait()
    row = lax.broadcasted_iota(jnp.int32, (PACK, H), 0)
    for side, out in enumerate((first_ref, last_ref)):
        wide = jnp.broadcast_to(obs[:, pl.ds(side * H, H)], (PACK, H))
        high = wide.astype(BF).astype(F32)
        rest = wide - high
        middle = rest.astype(BF).astype(F32)
        low = rest - middle
        split = jnp.where(row == 0, high, jnp.where(row == 1, middle, jnp.where(row == 2, low, 0.0)))
        out[pl.ds(members, PACK), :] = split.astype(BF)
    for copy in copies[0::2]:
        copy.wait()


def halo_blocks(predicted, observed):
    members, columns = predicted.shape
    far = pl.BlockSpec(memory_space=pltpu.HBM)
    near = pl.BlockSpec(memory_space=pltpu.VMEM)
    block = jax.ShapeDtypeStruct((members + PACK, H), BF)
    return pl.pallas_call(
        functools.partial(halo_kernel, columns),
        out_shape=(block, block),
        in_specs=[far, far],
        out_specs=[near, near],
        scratch_shapes=[pltpu.VMEM((1, 2 * H), F32), pltpu.SemaphoreType.DMA((4,))],
        compiler_params=pltpu.CompilerParams(vmem_limit_bytes=VMEM),
        name="halos",
    )(predicted, observed)


def sum_over(values, axes):
    shards = lax.axis_size(axes)
    rows, width = values.shape
    parts = lax.all_to_all(values, axes, 0, 0, tiled=True)
    own = jnp.sum(parts.reshape(shards, rows // shards, width), axis=0)
    copies = jnp.broadcast_to(own[None], (shards, rows // shards, width)).reshape(rows, width)
    return lax.all_to_all(copies, axes, 0, 0, tiled=True)


def body(predicted, observed, band, offsets, rows_count, params):
    columns = predicted.shape[1]
    axes = ("obs", "par")
    shards = lax.axis_size(axes)
    obs_total = columns * shards
    up = [(i, i + 1) for i in range(shards - 1)]
    down = [(j, i) for i, j in up]
    obs_row = observed[None, :]
    first, last = halo_blocks(predicted, obs_row)
    left = lax.ppermute(last, axes, up)
    right = lax.ppermute(first, axes, down)
    gram, misfit = local_call(False, obs_total, offsets, rows_count, predicted, obs_row, band)
    gram, misfit = local_call(
        True, obs_total, offsets, rows_count, predicted, obs_row, band, left, right, gram, misfit)
    total = sum_over(gram, axes)
    return (update(total, params), misfit[0])


def solution(mesh):
    in_specs = (
        P(None, ("grp", "obs", "par")),
        P(("grp", "obs", "par")),
        P(None, ("grp", "obs", "par")),
        P(),
        P(("grp", "obs", "par")),
        P(("grp", "obs", "par"), None),
    )
    out_specs = (P(("grp", "obs", "par"), None), P(("grp", "obs", "par")))
    return jax.shard_map(body, mesh=mesh, in_specs=in_specs, out_specs=out_specs, check_vma=False)
```

```python
import functools
import math

import jax
import jax.numpy as jnp
from jax import lax
from jax.experimental import pallas as pl
from jax.experimental.pallas import tpu as pltpu
from jax.sharding import PartitionSpec as P

H = 1024
LANE = 128
SUB = 8
PACK = 16
LATE = 2
BLOCK = 64
PANEL = 8
VMEM = 64 * 2**20
BF = jnp.bfloat16
F32 = jnp.float32


def local_kernel(edge, columns, obs_total, *refs):
    if edge:
        (off_ref, count_ref, pred_ref, obs_ref, band_ref, left_ref, right_ref, gram_in, misfit_in,
         gram_out, misfit_out, raw, joint, aw, coef, gram, centre, obs, band, row_out, slots,
         sems) = refs
    else:
        (off_ref, count_ref, pred_ref, obs_ref, band_ref,
         gram_out, misfit_out, raw, joint, aw, coef, gram, centre, obs, band, row_out, slots,
         sems) = refs
    members = pred_ref.shape[0]
    terms = band_ref.shape[0]
    chunks = columns // H
    tiles = H // LANE
    half = members // 2
    row_factor = 1.0 / math.sqrt(obs_total)

    if edge:
        copies = [
            pltpu.make_async_copy(left_ref, raw.at[:, pl.ds(0, H)], sems.at[0]),
            pltpu.make_async_copy(right_ref, raw.at[:, pl.ds(5 * H, H)], sems.at[5]),
        ]
        for place, chunk in ((1, 0), (2, 1), (3, chunks - 2), (4, chunks - 1)):
            copies.append(pltpu.make_async_copy(
                pred_ref.at[:, pl.ds(chunk * H, H)],
                raw.at[pl.ds(0, members), pl.ds(place * H, H)], sems.at[place]))
        for which in range(2):
            there = which * (columns - 2 * H)
            copies.append(pltpu.make_async_copy(
                obs_ref.at[:, pl.ds(there, 2 * H)], obs.at[:, pl.ds((1 + which * 2) * H, 2 * H)], sems.at[6 + which]))
            there = which * (columns - H)
            copies.append(pltpu.make_async_copy(
                band_ref.at[:, pl.ds(there, H)], band.at[:, pl.ds(which * H, H)], sems.at[8 + which]))
        for copy in copies:
            copy.start()
    else:
        def chunk_copy(place):
            start = pl.multiple_of(place * H, H)
            return pltpu.make_async_copy(
                pred_ref.at[:, pl.ds(start, H)], raw.at[:, pl.ds(start, H)], sems.at[place])

        copies = [
            pltpu.make_async_copy(obs_ref, obs, sems.at[chunks]),
            pltpu.make_async_copy(band_ref, band, sems.at[chunks + 1]),
        ]
        for place in range(chunks):
            chunk_copy(place).start()
            if place == 2:
                for copy in copies:
                    copy.start()

    slots[0, 0] = 0
    slots[0, 1] = 0
    free = jnp.int32(3)
    for term in range(1, terms):
        offset = off_ref[term]
        whole = (offset == H) | (offset == -H)
        place = jnp.where(offset == -H, 1, jnp.where(offset == H, 2, free))
        place = jnp.minimum(place, terms - 1)
        slots[place, 0] = jnp.int32(term)
        slots[place, 1] = offset
        free = free + jnp.where(whole, 0, 1)

    rows = members + PACK
    row_index = lax.broadcasted_iota(jnp.int32, (rows, members), 0)
    col_index = lax.broadcasted_iota(jnp.int32, (rows, members), 1)
    mean_part = 1.0 / members
    centre[...] = jnp.where(
        row_index >= members, mean_part, jnp.where(row_index == col_index, 1.0 - mean_part, -mean_part)
    ).astype(BF)
    gram[...] = jnp.zeros_like(gram)
    aw[...] = jnp.zeros_like(aw)

    def anomalies(place):
        at = pl.ds(pl.multiple_of(place * H, H), H)
        wide = jnp.dot(centre[...], raw[pl.ds(0, members), at], preferred_element_type=F32)
        joint[pl.ds(0, members), at] = wide[:members]
        innovation = obs[:, at] - wide[members:members + SUB]
        joint[pl.ds(members, SUB), at] = innovation.astype(BF).astype(F32)

    def coefficients(column, at):
        index = column + lax.broadcasted_iota(jnp.int32, (1, H), 1)
        strained = (index < count_ref[0]) | (index >= columns - H)
        strain = jnp.where(strained, 1.0, 0.0)
        for slot in range(terms):
            term = slots[slot, 0]
            row = band[pl.ds(term, 1), pl.ds(at, H)]
            if slot > 0:
                row = row * strain
            coef[pl.ds(slot * SUB, SUB), :] = jnp.broadcast_to(row, (SUB, H))

    def plan(place):
        lane = lax.broadcasted_iota(jnp.int32, (SUB, LANE), 1)
        steps = []
        for slot in range(terms):
            if slot < 3:
                steps.append((place * tiles + (0, -tiles, tiles)[slot], None, None))
            else:
                offset = slots[slot, 1] + 8 * LANE
                turn = lax.rem(offset, LANE)
                first = place * tiles + lax.div(offset, LANE) - 8
                steps.append((first, lax.rem(LANE - turn, LANE), lane < LANE - turn))
        return steps

    def whiten_rows(steps, starts):
        acc = [[None] * tiles for _ in starts]
        for slot, (first, back, keep) in enumerate(steps):
            weights = [coef[pl.ds(slot * SUB, SUB), pl.ds(t * LANE, LANE)] for t in range(tiles)]
            for r, at_row in enumerate(starts):
                def load(t):
                    start = pl.multiple_of((first + t) * LANE, LANE)
                    return joint[pl.ds(at_row, SUB), pl.ds(start, LANE)]

                if back is None:
                    values = [load(t) for t in range(tiles)]
                else:
                    rolled = [pltpu.roll(load(t), back, 1) for t in range(tiles + 1)]
                    values = [jnp.where(keep, rolled[t], rolled[t + 1]) for t in range(tiles)]
                for t in range(tiles):
                    product = values[t] * weights[t]
                    acc[r][t] = product if acc[r][t] is None else acc[r][t] + product
        return acc

    def products():
        gram[...] += lax.dot_general(
            aw[...], aw[pl.ds(0, members), :], (((1,), (1,)), ((), ())), preferred_element_type=F32)

    def whiten_chunk(place, column, at):
        coefficients(column, at)
        steps = plan(place)
        pending = []

        def store_oldest():
            at_row, values = pending.pop(0)
            for t in range(tiles):
                aw[pl.ds(at_row, PACK), pl.ds(t * LANE, LANE)] = values[t]

        acc = whiten_rows(steps, [members])[0]
        row = lax.broadcasted_iota(jnp.int32, (PACK, LANE), 0)
        parts = []
        for t in range(tiles):
            wide = jnp.concatenate([acc[t], acc[t]], 0)
            high = wide.astype(BF).astype(F32)
            rest = wide - high
            middle = rest.astype(BF).astype(F32)
            low = rest - middle
            split = jnp.where(row == 0, high, jnp.where(row == 1, middle, jnp.where(row == 2, low, 0.0)))
            parts.append(split.astype(BF))
        pending.append((members, parts))
        scale = math.sqrt(members - 1) * row_factor
        misfit = [acc[t][0:1] * scale for t in range(tiles)]
        for group in range(members // PACK):
            low, high = whiten_rows(steps, [group * PACK, group * PACK + SUB])
            pending.append((group * PACK, [jnp.concatenate([low[t], high[t]], 0).astype(BF) for t in range(tiles)]))
            if len(pending) > LATE:
                store_oldest()
        while pending:
            store_oldest()
        for t in range(tiles):
            row_out[:, pl.ds(at + t * LANE, LANE)] = misfit[t]

    if edge:
        for copy in copies:
            copy.wait()
        for place in (0, 5):
            pieces = raw[pl.ds(members, PACK), pl.ds(place * H, H)].astype(F32)
            obs[:, pl.ds(place * H, H)] = pieces[0:1] + pieces[1:2] + pieces[2:3]

        def centre_step(place, carry):
            anomalies(place)
            return carry

        lax.fori_loop(0, 6, centre_step, 0)

        def chunk_step(which, carry):
            products()
            whiten_chunk(1 + 3 * which, which * (columns - H), pl.multiple_of(which * H, H))
            return carry

        lax.fori_loop(0, 2, chunk_step, 0)
        out_copies = [
            pltpu.make_async_copy(row_out.at[:, pl.ds(0, H)], misfit_out.at[:, pl.ds(0, H)], sems.at[0]),
            pltpu.make_async_copy(row_out.at[:, pl.ds(H, H)], misfit_out.at[:, pl.ds(columns - H, H)], sems.at[1]),
        ]
    else:
        for copy in copies:
            copy.wait()

        def centre_step(place, carry):
            chunk_copy(place).wait()
            anomalies(place)
            return carry

        lax.fori_loop(0, 2, centre_step, 0)

        def chunk_step(place, carry):
            chunk_copy(place + 1).wait()
            products()
            anomalies(place + 1)
            column = pl.multiple_of(place * H, H)
            whiten_chunk(place, column, column)
            return carry

        lax.fori_loop(1, chunks - 1, chunk_step, 0)
        inside = pl.ds(H, columns - 2 * H)
        out_copies = [pltpu.make_async_copy(row_out.at[:, inside], misfit_out.at[:, inside], sems.at[0])]
    for copy in out_copies:
        copy.start()
    products()

    tail = gram[pl.ds(members, 8), :]
    total = tail[0:1] + tail[1:2] + tail[2:3]
    both = gram[pl.ds(0, members), :]
    top = lax.broadcasted_iota(jnp.int32, (half, half), 0)
    corner = jnp.where(top == 0, total[:, :half], jnp.where(top == 1, total[:, half:], 0.0))
    upper = jnp.concatenate([both[:half, :half], corner], 1)
    lower = both[half:]
    upper = upper * (1.0 / obs_total)
    lower = lower * (1.0 / obs_total)
    if edge:
        upper = upper + gram_in[pl.ds(0, half), :]
        lower = lower + gram_in[pl.ds(half, half), :]
    gram_out[pl.ds(0, half), :] = upper
    gram_out[pl.ds(half, half), :] = lower
    for copy in out_copies:
        copy.wait()


def local_call(edge, obs_total, offsets, rows_count, predicted, observed, band, *more):
    members, columns = predicted.shape
    terms = band.shape[0]
    rows = members + PACK
    places = 6 if edge else columns // H
    vmem = pl.BlockSpec(memory_space=pltpu.VMEM)
    smem = pl.BlockSpec(memory_space=pltpu.SMEM)
    far = pl.BlockSpec(memory_space=pltpu.HBM)
    in_specs = [smem, smem, far, far, far]
    if edge:
        in_specs += [far, far, vmem, far]
    scratch = [
        pltpu.VMEM((rows if edge else members, places * H), BF),
        pltpu.VMEM((members + SUB, places * H), F32),
        pltpu.VMEM((rows, H), BF),
        pltpu.VMEM((SUB * terms, H), F32),
        pltpu.VMEM((rows, members), F32),
        pltpu.VMEM((rows, members), BF),
        pltpu.VMEM((1, places * H), F32),
        pltpu.VMEM((terms, 2 * H if edge else columns), F32),
        pltpu.VMEM((1, 2 * H if edge else columns), F32),
        pltpu.SMEM((8, 2), jnp.int32),
        pltpu.SemaphoreType.DMA((places + 4,)),
    ]
    work = 2 if edge else places - 2
    return pl.pallas_call(
        functools.partial(local_kernel, edge, columns, obs_total),
        out_shape=(
            jax.ShapeDtypeStruct((members, members), F32),
            jax.ShapeDtypeStruct((1, columns), F32),
        ),
        in_specs=in_specs,
        out_specs=[vmem, far],
        scratch_shapes=scratch,
        input_output_aliases={8: 1} if edge else {},
        compiler_params=pltpu.CompilerParams(vmem_limit_bytes=VMEM),
        cost_estimate=pl.CostEstimate(
            flops=2 * rows * members * H * work * 2, bytes_accessed=members * H * places * 2, transcendentals=0),
        name="edges" if edge else "inner",
    )(offsets, rows_count, predicted, observed, band, *more)


def update_kernel(sum_ref, params_ref, out_ref, work):
    members = params_ref.shape[1]
    highest = lax.Precision.HIGHEST
    row_index = lax.broadcasted_iota(jnp.int32, (members, members), 0)
    col_index = lax.broadcasted_iota(jnp.int32, (members, members), 1)
    identity = jnp.where(row_index == col_index, 1.0, 0.0).astype(F32)
    half = members // 2
    work[:, pl.ds(0, half)] = sum_ref[:, pl.ds(0, half)] + identity[:, :half]
    work[pl.ds(0, half), pl.ds(half, half)] = sum_ref[pl.ds(half, half), pl.ds(0, half)].T
    work[pl.ds(half, half), pl.ds(half, half)] = sum_ref[pl.ds(half, half), pl.ds(half, half)] + identity[half:, half:]
    work[:, pl.ds(members, members)] = identity
    panels = BLOCK // PANEL
    sub = lax.broadcasted_iota(jnp.int32, (PANEL, LANE), 0)
    eye = identity[:BLOCK, :BLOCK]

    def across(tile, column):
        return jnp.broadcast_to(tile[:, column:column + 1], (PANEL, LANE))

    def down(tile, row):
        return jnp.broadcast_to(tile[row:row + 1, :], (PANEL, LANE))

    for block in range(members // BLOCK):
        r0 = block * BLOCK
        start = jnp.concatenate([work[pl.ds(r0, BLOCK), pl.ds(r0, BLOCK)], eye], axis=1)
        tiles = [start[PANEL * t:PANEL * (t + 1)] for t in range(panels)]
        done = []
        for p in range(panels):
            c0 = PANEL * p
            tile = tiles[p]
            upper = tile
            full = tile
            cols = [across(tile, c0 + j) for j in range(PANEL)]
            full_cols = list(cols)
            scale = jnp.zeros((PANEL, LANE), F32)
            for k in range(PANEL):
                pivot = down(cols[k], k)
                inverse = 1.0 / pivot
                scale = jnp.where(sub == k, pivot, scale)
                below = jnp.where(sub > k, cols[k] * inverse, 0.0)

                def clear(values):
                    row = down(values, k) * inverse
                    return jnp.where(sub == k, row, values - full_cols[k] * row)

                for j in range(k + 1, PANEL):
                    cols[j] = cols[j] - below * down(cols[j], k)
                    full_cols[j] = clear(full_cols[j])
                upper = upper - below * down(upper, k)
                full = clear(full)
            done.append(upper * lax.rsqrt(scale))
            rows_of = [down(full, k) for k in range(PANEL)]
            for t in range(p + 1, panels):
                tile_t = tiles[t]
                change = [across(tile_t, c0 + k) * rows_of[k] for k in range(PANEL)]
                while len(change) > 1:
                    change = [a + b for a, b in zip(change[::2], change[1::2])]
                tiles[t] = tile_t - change[0]
        lower_inverse = jnp.concatenate(done, axis=0)[:, BLOCK:2 * BLOCK]
        solved = jnp.dot(lower_inverse, work[pl.ds(r0, BLOCK), :], precision=highest, preferred_element_type=F32)
        work[pl.ds(r0, BLOCK), :] = solved
        if r0 + BLOCK < members:
            rest = members - r0 - BLOCK
            factor = solved[:, r0 + BLOCK:members]
            work[pl.ds(r0 + BLOCK, rest), :] = work[pl.ds(r0 + BLOCK, rest), :] - lax.dot_general(
                factor, solved, (((0,), (0,)), ((), ())), precision=highest, preferred_element_type=F32)

    inverse = jnp.where(row_index >= col_index, work[:, pl.ds(members, members)], 0.0)
    projection = jnp.concatenate([sum_ref[pl.ds(r, 1), pl.ds(half, half)] for r in range(2)], 1)
    solved = jnp.sum(inverse * projection, axis=1, keepdims=True)
    weights = jnp.sum(inverse * solved, axis=0, keepdims=True)
    turned = inverse + weights
    turned = turned - jnp.mean(turned, axis=1, keepdims=True) + 1.0 / members
    high = turned.astype(BF)
    rest = turned - high.astype(F32)
    middle = rest.astype(BF)
    low = (rest - middle.astype(F32)).astype(BF)
    params = params_ref[...]

    def times(part):
        return lax.dot_general(params, part, (((1,), (1,)), ((), ())), preferred_element_type=F32)

    out_ref[...] = times(high) + (times(middle) + times(low))


def update(total, params):
    members = params.shape[1]
    vmem = pl.BlockSpec(memory_space=pltpu.VMEM)
    return pl.pallas_call(
        update_kernel,
        out_shape=jax.ShapeDtypeStruct(params.shape, F32),
        in_specs=[vmem, vmem],
        out_specs=vmem,
        scratch_shapes=[pltpu.VMEM((members, 2 * members), F32)],
        compiler_params=pltpu.CompilerParams(vmem_limit_bytes=VMEM),
        name="update",
    )(total, params)


def halo_kernel(columns, pred_ref, obs_ref, first_ref, last_ref, obs, sems):
    members = pred_ref.shape[0]
    copies = []
    for side, (out, at) in enumerate(((first_ref, 0), (last_ref, columns - H))):
        copies.append(pltpu.make_async_copy(
            pred_ref.at[:, pl.ds(at, H)], out.at[pl.ds(0, members), :], sems.at[side]))
        copies.append(pltpu.make_async_copy(
            obs_ref.at[:, pl.ds(at, H)], obs.at[:, pl.ds(side * H, H)], sems.at[2 + side]))
    for copy in copies:
        copy.start()
    for copy in copies[1::2]:
        copy.wait()
    row = lax.broadcasted_iota(jnp.int32, (PACK, H), 0)
    for side, out in enumerate((first_ref, last_ref)):
        wide = jnp.broadcast_to(obs[:, pl.ds(side * H, H)], (PACK, H))
        high = wide.astype(BF).astype(F32)
        rest = wide - high
        middle = rest.astype(BF).astype(F32)
        low = rest - middle
        split = jnp.where(row == 0, high, jnp.where(row == 1, middle, jnp.where(row == 2, low, 0.0)))
        out[pl.ds(members, PACK), :] = split.astype(BF)
    for copy in copies[0::2]:
        copy.wait()


def halo_blocks(predicted, observed):
    members, columns = predicted.shape
    far = pl.BlockSpec(memory_space=pltpu.HBM)
    near = pl.BlockSpec(memory_space=pltpu.VMEM)
    block = jax.ShapeDtypeStruct((members + PACK, H), BF)
    return pl.pallas_call(
        functools.partial(halo_kernel, columns),
        out_shape=(block, block),
        in_specs=[far, far],
        out_specs=[near, near],
        scratch_shapes=[pltpu.VMEM((1, 2 * H), F32), pltpu.SemaphoreType.DMA((4,))],
        compiler_params=pltpu.CompilerParams(vmem_limit_bytes=VMEM),
        name="halos",
    )(predicted, observed)


def sum_over(values, axes):
    shards = lax.axis_size(axes)
    rows, width = values.shape
    parts = lax.all_to_all(values, axes, 0, 0, tiled=True)
    own = jnp.sum(parts.reshape(shards, rows // shards, width), axis=0)
    copies = jnp.broadcast_to(own[None], (shards, rows // shards, width)).reshape(rows, width)
    return lax.all_to_all(copies, axes, 0, 0, tiled=True)


def body(predicted, observed, band, offsets, rows_count, params):
    columns = predicted.shape[1]
    axes = ("obs", "par")
    shards = lax.axis_size(axes)
    obs_total = columns * shards
    up = [(i, i + 1) for i in range(shards - 1)]
    down = [(j, i) for i, j in up]
    obs_row = observed[None, :]
    first, last = halo_blocks(predicted, obs_row)
    left = lax.ppermute(last, axes, up)
    right = lax.ppermute(first, axes, down)
    gram, misfit = local_call(False, obs_total, offsets, rows_count, predicted, obs_row, band)
    gram, misfit = local_call(
        True, obs_total, offsets, rows_count, predicted, obs_row, band, left, right, gram, misfit)
    total = sum_over(gram, axes)
    return (update(total, params), misfit[0])


def solution(mesh):
    in_specs = (
        P(None, ("grp", "obs", "par")),
        P(("grp", "obs", "par")),
        P(None, ("grp", "obs", "par")),
        P(),
        P(("grp", "obs", "par")),
        P(("grp", "obs", "par"), None),
    )
    out_specs = (P(("grp", "obs", "par"), None), P(("grp", "obs", "par")))
    return jax.shard_map(body, mesh=mesh, in_specs=in_specs, out_specs=out_specs, check_vma=False)
```

```python
import functools
import math

import jax
import jax.numpy as jnp
from jax import lax
from jax.experimental import pallas as pl
from jax.experimental.pallas import tpu as pltpu
from jax.sharding import PartitionSpec as P

H = 1024
LANE = 128
SUB = 8
PACK = 16
LATE = 2
BLOCK = 64
PANEL = 8
VMEM = 64 * 2**20
BF = jnp.bfloat16
F32 = jnp.float32


def local_kernel(edge, columns, obs_total, *refs):
    if edge:
        (off_ref, count_ref, pred_ref, obs_ref, band_ref, left_ref, right_ref, gram_in, misfit_in,
         gram_out, misfit_out, raw, joint, aw, coef, gram, obs, band, row_out, slots,
         sems) = refs
    else:
        (off_ref, count_ref, pred_ref, obs_ref, band_ref,
         gram_out, misfit_out, raw, joint, aw, coef, gram, obs, band, row_out, slots,
         sems) = refs
    members = pred_ref.shape[0]
    terms = band_ref.shape[0]
    chunks = columns // H
    tiles = H // LANE
    half = members // 2
    row_factor = 1.0 / math.sqrt(obs_total)

    if edge:
        copies = [
            pltpu.make_async_copy(left_ref, raw.at[:, pl.ds(0, H)], sems.at[0]),
            pltpu.make_async_copy(right_ref, raw.at[:, pl.ds(5 * H, H)], sems.at[5]),
        ]
        for place, chunk in ((1, 0), (2, 1), (3, chunks - 2), (4, chunks - 1)):
            copies.append(pltpu.make_async_copy(
                pred_ref.at[:, pl.ds(chunk * H, H)],
                raw.at[pl.ds(0, members), pl.ds(place * H, H)], sems.at[place]))
        for which in range(2):
            there = which * (columns - 2 * H)
            copies.append(pltpu.make_async_copy(
                obs_ref.at[:, pl.ds(there, 2 * H)], obs.at[:, pl.ds((1 + which * 2) * H, 2 * H)], sems.at[6 + which]))
            there = which * (columns - H)
            copies.append(pltpu.make_async_copy(
                band_ref.at[:, pl.ds(there, H)], band.at[:, pl.ds(which * H, H)], sems.at[8 + which]))
        for copy in copies:
            copy.start()
    else:
        def chunk_copy(place):
            start = pl.multiple_of(place * H, H)
            return pltpu.make_async_copy(
                pred_ref.at[:, pl.ds(start, H)], raw.at[:, pl.ds(start, H)], sems.at[place])

        copies = [
            pltpu.make_async_copy(obs_ref, obs, sems.at[chunks]),
            pltpu.make_async_copy(band_ref, band, sems.at[chunks + 1]),
        ]
        for place in range(chunks):
            chunk_copy(place).start()
            if place == 2:
                for copy in copies:
                    copy.start()

    slots[0, 0] = 0
    slots[0, 1] = 0
    free = jnp.int32(3)
    for term in range(1, terms):
        offset = off_ref[term]
        whole = (offset == H) | (offset == -H)
        place = jnp.where(offset == -H, 1, jnp.where(offset == H, 2, free))
        place = jnp.minimum(place, terms - 1)
        slots[place, 0] = jnp.int32(term)
        slots[place, 1] = offset
        free = free + jnp.where(whole, 0, 1)

    gram[...] = jnp.zeros_like(gram)
    aw[...] = jnp.zeros_like(aw)

    def anomalies(place):
        columns_of = [pl.ds(pl.multiple_of(place * H + t * LANE, LANE), LANE) for t in range(tiles)]
        means = []
        for at in columns_of:
            wide = raw[pl.ds(0, members), at].astype(F32)
            means.append(jnp.sum(wide, axis=0, keepdims=True) * (1.0 / members))
        for at, mean in zip(columns_of, means):
            joint[pl.ds(0, members), at] = (raw[pl.ds(0, members), at].astype(F32) - mean).astype(BF)
            innovation = jnp.broadcast_to(obs[:, at] - mean, (PACK, LANE))
            joint[pl.ds(members, PACK), at] = innovation.astype(BF)

    def coefficients(column, at):
        index = column + lax.broadcasted_iota(jnp.int32, (1, H), 1)
        strained = (index < count_ref[0]) | (index >= columns - H)
        strain = jnp.where(strained, 1.0, 0.0)
        for slot in range(terms):
            term = slots[slot, 0]
            row = band[pl.ds(term, 1), pl.ds(at, H)]
            if slot > 0:
                row = row * strain
            coef[pl.ds(slot * SUB, SUB), :] = jnp.broadcast_to(row, (SUB, H))

    def plan(place):
        lane = lax.broadcasted_iota(jnp.int32, (PACK, LANE), 1)
        steps = []
        for slot in range(terms):
            if slot < 3:
                steps.append((place * tiles + (0, -tiles, tiles)[slot], None, None))
            else:
                offset = slots[slot, 1] + 8 * LANE
                turn = lax.rem(offset, LANE)
                first = place * tiles + lax.div(offset, LANE) - 8
                steps.append((first, lax.rem(LANE - turn, LANE), lane < LANE - turn))
        return steps

    def whiten_rows(steps, starts, low, width):
        acc = [[None] * width for _ in starts]
        for slot, (first, back, keep) in enumerate(steps):
            weights = []
            for t in range(width):
                weight = coef[pl.ds(slot * SUB, SUB), pl.ds((low + t) * LANE, LANE)]
                weights.append(jnp.concatenate([weight, weight], 0))
            for r, at_row in enumerate(starts):
                def load(t):
                    start = pl.multiple_of((first + low + t) * LANE, LANE)
                    return joint[pl.ds(at_row, PACK), pl.ds(start, LANE)]

                if back is None:
                    values = [load(t) for t in range(width)]
                else:
                    rolled = [pltpu.roll(load(t), back, 1) for t in range(width + 1)]
                    values = [jnp.where(keep, rolled[t], rolled[t + 1]) for t in range(width)]
                for t in range(width):
                    product = values[t].astype(F32) * weights[t]
                    acc[r][t] = product if acc[r][t] is None else acc[r][t] + product
        return acc

    def products():
        return lax.dot_general(
            aw[...], aw[pl.ds(0, members), :], (((1,), (1,)), ((), ())), preferred_element_type=F32)

    def whiten_chunk(place, column, at):
        coefficients(column, at)
        steps = plan(place)
        pending = []

        def store_oldest():
            for at_row, tile, value in pending.pop(0):
                aw[pl.ds(at_row, PACK), pl.ds(tile * LANE, LANE)] = value

        acc = whiten_rows(steps, [members], 0, tiles)[0]
        row = lax.broadcasted_iota(jnp.int32, (PACK, LANE), 0)
        parts = []
        for t in range(tiles):
            wide = acc[t]
            high = wide.astype(BF).astype(F32)
            rest = wide - high
            middle = rest.astype(BF).astype(F32)
            low = rest - middle
            split = jnp.where(row == 0, high, jnp.where(row == 1, middle, jnp.where(row == 2, low, 0.0)))
            parts.append((members, t, split.astype(BF)))
        pending.append(parts)
        scale = math.sqrt(members - 1) * row_factor
        misfit = [acc[t][0:1] * scale for t in range(tiles)]
        width = tiles // 2
        for group in range(members // (2 * PACK)):
            starts = [group * 2 * PACK, group * 2 * PACK + PACK]
            for first in (0, width):
                out = whiten_rows(steps, starts, first, width)
                pending.append([
                    (at_row, first + t, out[r][t].astype(BF))
                    for r, at_row in enumerate(starts) for t in range(width)])
                if len(pending) > LATE:
                    store_oldest()
        while pending:
            store_oldest()
        for t in range(tiles):
            row_out[:, pl.ds(at + t * LANE, LANE)] = misfit[t]

    if edge:
        for copy in copies:
            copy.wait()
        for place in (0, 5):
            pieces = raw[pl.ds(members, PACK), pl.ds(place * H, H)].astype(F32)
            obs[:, pl.ds(place * H, H)] = pieces[0:1] + pieces[1:2] + pieces[2:3]

        def centre_step(place, carry):
            anomalies(place)
            return carry

        lax.fori_loop(0, 6, centre_step, 0)

        def chunk_step(which, carry):
            added = products()
            whiten_chunk(1 + 3 * which, which * (columns - H), pl.multiple_of(which * H, H))
            gram[...] += added
            return carry

        lax.fori_loop(0, 2, chunk_step, 0)
        out_copies = [
            pltpu.make_async_copy(row_out.at[:, pl.ds(0, H)], misfit_out.at[:, pl.ds(0, H)], sems.at[0]),
            pltpu.make_async_copy(row_out.at[:, pl.ds(H, H)], misfit_out.at[:, pl.ds(columns - H, H)], sems.at[1]),
        ]
    else:
        for copy in copies:
            copy.wait()

        def centre_step(place, carry):
            chunk_copy(place).wait()
            anomalies(place)
            return carry

        lax.fori_loop(0, 2, centre_step, 0)

        def chunk_step(place, carry):
            chunk_copy(place + 1).wait()
            added = products()
            anomalies(place + 1)
            column = pl.multiple_of(place * H, H)
            whiten_chunk(place, column, column)
            gram[...] += added
            return carry

        lax.fori_loop(1, chunks - 1, chunk_step, 0)
        inside = pl.ds(H, columns - 2 * H)
        out_copies = [pltpu.make_async_copy(row_out.at[:, inside], misfit_out.at[:, inside], sems.at[0])]
    for copy in out_copies:
        copy.start()
    gram[...] += products()

    tail = gram[pl.ds(members, 8), :]
    total = tail[0:1] + tail[1:2] + tail[2:3]
    both = gram[pl.ds(0, members), :]
    top = lax.broadcasted_iota(jnp.int32, (half, half), 0)
    corner = jnp.where(top == 0, total[:, :half], jnp.where(top == 1, total[:, half:], 0.0))
    upper = jnp.concatenate([both[:half, :half], corner], 1)
    lower = both[half:]
    upper = upper * (1.0 / obs_total)
    lower = lower * (1.0 / obs_total)
    if edge:
        upper = upper + gram_in[pl.ds(0, half), :]
        lower = lower + gram_in[pl.ds(half, half), :]
    gram_out[pl.ds(0, half), :] = upper
    gram_out[pl.ds(half, half), :] = lower
    for copy in out_copies:
        copy.wait()


def local_call(edge, obs_total, offsets, rows_count, predicted, observed, band, *more):
    members, columns = predicted.shape
    terms = band.shape[0]
    rows = members + PACK
    places = 6 if edge else columns // H
    vmem = pl.BlockSpec(memory_space=pltpu.VMEM)
    smem = pl.BlockSpec(memory_space=pltpu.SMEM)
    far = pl.BlockSpec(memory_space=pltpu.HBM)
    in_specs = [smem, smem, far, far, far]
    if edge:
        in_specs += [far, far, vmem, far]
    scratch = [
        pltpu.VMEM((rows if edge else members, places * H), BF),
        pltpu.VMEM((rows, places * H), BF),
        pltpu.VMEM((rows, H), BF),
        pltpu.VMEM((SUB * terms, H), F32),
        pltpu.VMEM((rows, members), F32),
        pltpu.VMEM((1, places * H), F32),
        pltpu.VMEM((terms, 2 * H if edge else columns), F32),
        pltpu.VMEM((1, 2 * H if edge else columns), F32),
        pltpu.SMEM((8, 2), jnp.int32),
        pltpu.SemaphoreType.DMA((places + 4,)),
    ]
    work = 2 if edge else places - 2
    return pl.pallas_call(
        functools.partial(local_kernel, edge, columns, obs_total),
        out_shape=(
            jax.ShapeDtypeStruct((members, members), F32),
            jax.ShapeDtypeStruct((1, columns), F32),
        ),
        in_specs=in_specs,
        out_specs=[vmem, far],
        scratch_shapes=scratch,
        input_output_aliases={8: 1} if edge else {},
        compiler_params=pltpu.CompilerParams(vmem_limit_bytes=VMEM),
        cost_estimate=pl.CostEstimate(
            flops=2 * rows * members * H * work * 2, bytes_accessed=members * H * places * 2, transcendentals=0),
        name="edges" if edge else "inner",
    )(offsets, rows_count, predicted, observed, band, *more)


def update_kernel(sum_ref, params_ref, out_ref, work):
    members = params_ref.shape[1]
    highest = lax.Precision.HIGHEST
    row_index = lax.broadcasted_iota(jnp.int32, (members, members), 0)
    col_index = lax.broadcasted_iota(jnp.int32, (members, members), 1)
    identity = jnp.where(row_index == col_index, 1.0, 0.0).astype(F32)
    half = members // 2
    work[:, pl.ds(0, half)] = sum_ref[:, pl.ds(0, half)] + identity[:, :half]
    work[pl.ds(0, half), pl.ds(half, half)] = sum_ref[pl.ds(half, half), pl.ds(0, half)].T
    work[pl.ds(half, half), pl.ds(half, half)] = sum_ref[pl.ds(half, half), pl.ds(half, half)] + identity[half:, half:]
    work[:, pl.ds(members, members)] = identity
    panels = BLOCK // PANEL
    sub = lax.broadcasted_iota(jnp.int32, (PANEL, LANE), 0)
    eye = identity[:BLOCK, :BLOCK]

    def across(tile, column):
        return jnp.broadcast_to(tile[:, column:column + 1], (PANEL, LANE))

    def down(tile, row):
        return jnp.broadcast_to(tile[row:row + 1, :], (PANEL, LANE))

    for block in range(members // BLOCK):
        r0 = block * BLOCK
        start = jnp.concatenate([work[pl.ds(r0, BLOCK), pl.ds(r0, BLOCK)], eye], axis=1)
        tiles = [start[PANEL * t:PANEL * (t + 1)] for t in range(panels)]
        done = []
        for p in range(panels):
            c0 = PANEL * p
            tile = tiles[p]
            upper = tile
            full = tile
            cols = [across(tile, c0 + j) for j in range(PANEL)]
            full_cols = list(cols)
            scale = jnp.zeros((PANEL, LANE), F32)
            for k in range(PANEL):
                pivot = down(cols[k], k)
                inverse = 1.0 / pivot
                scale = jnp.where(sub == k, pivot, scale)
                below = jnp.where(sub > k, cols[k] * inverse, 0.0)

                def clear(values):
                    row = down(values, k) * inverse
                    return jnp.where(sub == k, row, values - full_cols[k] * row)

                for j in range(k + 1, PANEL):
                    cols[j] = cols[j] - below * down(cols[j], k)
                    full_cols[j] = clear(full_cols[j])
                upper = upper - below * down(upper, k)
                full = clear(full)
            done.append(upper * lax.rsqrt(scale))
            rows_of = [down(full, k) for k in range(PANEL)]
            for t in range(p + 1, panels):
                tile_t = tiles[t]
                change = [across(tile_t, c0 + k) * rows_of[k] for k in range(PANEL)]
                while len(change) > 1:
                    change = [a + b for a, b in zip(change[::2], change[1::2])]
                tiles[t] = tile_t - change[0]
        lower_inverse = jnp.concatenate(done, axis=0)[:, BLOCK:2 * BLOCK]
        solved = jnp.dot(lower_inverse, work[pl.ds(r0, BLOCK), :], precision=highest, preferred_element_type=F32)
        work[pl.ds(r0, BLOCK), :] = solved
        if r0 + BLOCK < members:
            rest = members - r0 - BLOCK
            factor = solved[:, r0 + BLOCK:members]
            work[pl.ds(r0 + BLOCK, rest), :] = work[pl.ds(r0 + BLOCK, rest), :] - lax.dot_general(
                factor, solved, (((0,), (0,)), ((), ())), precision=highest, preferred_element_type=F32)

    inverse = jnp.where(row_index >= col_index, work[:, pl.ds(members, members)], 0.0)
    projection = jnp.concatenate([sum_ref[pl.ds(r, 1), pl.ds(half, half)] for r in range(2)], 1)
    solved = jnp.sum(inverse * projection, axis=1, keepdims=True)
    weights = jnp.sum(inverse * solved, axis=0, keepdims=True)
    turned = inverse + weights
    turned = turned - jnp.mean(turned, axis=1, keepdims=True) + 1.0 / members
    high = turned.astype(BF)
    rest = turned - high.astype(F32)
    middle = rest.astype(BF)
    low = (rest - middle.astype(F32)).astype(BF)
    params = params_ref[...]

    def times(part):
        return lax.dot_general(params, part, (((1,), (1,)), ((), ())), preferred_element_type=F32)

    out_ref[...] = times(high) + (times(middle) + times(low))


def update(total, params):
    members = params.shape[1]
    vmem = pl.BlockSpec(memory_space=pltpu.VMEM)
    return pl.pallas_call(
        update_kernel,
        out_shape=jax.ShapeDtypeStruct(params.shape, F32),
        in_specs=[vmem, vmem],
        out_specs=vmem,
        scratch_shapes=[pltpu.VMEM((members, 2 * members), F32)],
        compiler_params=pltpu.CompilerParams(vmem_limit_bytes=VMEM),
        name="update",
    )(total, params)


def halo_kernel(columns, pred_ref, obs_ref, first_ref, last_ref, obs, sems):
    members = pred_ref.shape[0]
    copies = []
    for side, (out, at) in enumerate(((first_ref, 0), (last_ref, columns - H))):
        copies.append(pltpu.make_async_copy(
            pred_ref.at[:, pl.ds(at, H)], out.at[pl.ds(0, members), :], sems.at[side]))
        copies.append(pltpu.make_async_copy(
            obs_ref.at[:, pl.ds(at, H)], obs.at[:, pl.ds(side * H, H)], sems.at[2 + side]))
    for copy in copies:
        copy.start()
    for copy in copies[1::2]:
        copy.wait()
    row = lax.broadcasted_iota(jnp.int32, (PACK, H), 0)
    for side, out in enumerate((first_ref, last_ref)):
        wide = jnp.broadcast_to(obs[:, pl.ds(side * H, H)], (PACK, H))
        high = wide.astype(BF).astype(F32)
        rest = wide - high
        middle = rest.astype(BF).astype(F32)
        low = rest - middle
        split = jnp.where(row == 0, high, jnp.where(row == 1, middle, jnp.where(row == 2, low, 0.0)))
        out[pl.ds(members, PACK), :] = split.astype(BF)
    for copy in copies[0::2]:
        copy.wait()


def halo_blocks(predicted, observed):
    members, columns = predicted.shape
    far = pl.BlockSpec(memory_space=pltpu.HBM)
    near = pl.BlockSpec(memory_space=pltpu.VMEM)
    block = jax.ShapeDtypeStruct((members + PACK, H), BF)
    return pl.pallas_call(
        functools.partial(halo_kernel, columns),
        out_shape=(block, block),
        in_specs=[far, far],
        out_specs=[near, near],
        scratch_shapes=[pltpu.VMEM((1, 2 * H), F32), pltpu.SemaphoreType.DMA((4,))],
        compiler_params=pltpu.CompilerParams(vmem_limit_bytes=VMEM),
        name="halos",
    )(predicted, observed)


def scatter_sum(values, axis):
    size, (rows, width) = lax.axis_size(axis), values.shape
    parts = lax.all_to_all(values, axis, 0, 0, tiled=True)
    return jnp.sum(parts.reshape(size, rows // size, width), axis=0)


def gather_rows(values, axis):
    size, (rows, width) = lax.axis_size(axis), values.shape
    copies = jnp.broadcast_to(values[None], (size, rows, width)).reshape(size * rows, width)
    return lax.all_to_all(copies, axis, 0, 0, tiled=True)


def sum_over(values, axes):
    outer, inner = axes
    own = scatter_sum(scatter_sum(values, inner), outer)
    return gather_rows(gather_rows(own, outer), inner)


def body(predicted, observed, band, offsets, rows_count, params):
    columns = predicted.shape[1]
    axes = ("obs", "par")
    shards = lax.axis_size(axes)
    obs_total = columns * shards
    up = [(i, i + 1) for i in range(shards - 1)]
    down = [(j, i) for i, j in up]
    obs_row = observed[None, :]
    first, last = halo_blocks(predicted, obs_row)
    left = lax.ppermute(last, axes, up)
    right = lax.ppermute(first, axes, down)
    gram, misfit = local_call(False, obs_total, offsets, rows_count, predicted, obs_row, band)
    gram, misfit = local_call(
        True, obs_total, offsets, rows_count, predicted, obs_row, band, left, right, gram, misfit)
    total = sum_over(gram, axes)
    return (update(total, params), misfit[0])


def solution(mesh):
    in_specs = (
        P(None, ("grp", "obs", "par")),
        P(("grp", "obs", "par")),
        P(None, ("grp", "obs", "par")),
        P(),
        P(("grp", "obs", "par")),
        P(("grp", "obs", "par"), None),
    )
    out_specs = (P(("grp", "obs", "par"), None), P(("grp", "obs", "par")))
    return jax.shard_map(body, mesh=mesh, in_specs=in_specs, out_specs=out_specs, check_vma=False)
```

```python
import functools
import math

import jax
import jax.numpy as jnp
from jax import lax
from jax.experimental import pallas as pl
from jax.experimental.pallas import tpu as pltpu
from jax.sharding import PartitionSpec as P

H = 1024
LANE = 128
SUB = 8
PACK = 16
LATE = 2
AHEAD = 5
BLOCK = 64
PANEL = 8
VMEM = 64 * 2**20
BF = jnp.bfloat16
F32 = jnp.float32


def local_kernel(edge, columns, obs_total, *refs):
    if edge:
        (off_ref, count_ref, pred_ref, obs_ref, band_ref, left_ref, right_ref, gram_in, misfit_in,
         gram_out, misfit_out, raw, joint, aw, coef, gram, obs, band, row_out, slots,
         sems) = refs
    else:
        (off_ref, count_ref, pred_ref, obs_ref, band_ref,
         gram_out, misfit_out, raw, joint, aw, coef, gram, obs, band, row_out, slots,
         sems) = refs
    members = pred_ref.shape[0]
    terms = band_ref.shape[0]
    chunks = columns // H
    tiles = H // LANE
    half = members // 2
    row_factor = 1.0 / math.sqrt(obs_total)

    def tile_copies(source, column, place, height):
        for t in range(tiles):
            pltpu.make_async_copy(
                source.at[:, pl.ds(column + t * LANE, LANE)],
                raw.at[place * tiles + t, pl.ds(0, height), :], sems.at[place]).start()

    def tile_wait(place, height):
        whole = raw.at[pl.ds(place * tiles, tiles), pl.ds(0, height), :]
        pltpu.make_async_copy(whole, whole, sems.at[place]).wait()

    if edge:
        tile_copies(left_ref, 0, 0, members + PACK)
        for place, chunk in ((1, 0), (2, 1), (3, chunks - 2), (4, chunks - 1)):
            tile_copies(pred_ref, chunk * H, place, members)
        tile_copies(right_ref, 0, 5, members + PACK)
        copies = []
        for which in range(2):
            there = which * (columns - 2 * H)
            copies.append(pltpu.make_async_copy(
                obs_ref.at[:, pl.ds(there, 2 * H)], obs.at[:, pl.ds((1 + which * 2) * H, 2 * H)], sems.at[6 + which]))
            there = which * (columns - H)
            copies.append(pltpu.make_async_copy(
                band_ref.at[:, pl.ds(there, H)], band.at[:, pl.ds(which * H, H)], sems.at[8 + which]))
    else:
        copies = [
            pltpu.make_async_copy(obs_ref, obs, sems.at[chunks]),
            pltpu.make_async_copy(band_ref, band, sems.at[chunks + 1]),
        ]
        for place in range(AHEAD):
            tile_copies(pred_ref, place * H, place, members)
    for copy in copies:
        copy.start()

    slots[0, 0] = 0
    slots[0, 1] = 0
    free = jnp.int32(3)
    for term in range(1, terms):
        offset = off_ref[term]
        whole = (offset == H) | (offset == -H)
        place = jnp.where(offset == -H, 1, jnp.where(offset == H, 2, free))
        place = jnp.minimum(place, terms - 1)
        slots[place, 0] = jnp.int32(term)
        slots[place, 1] = offset
        free = free + jnp.where(whole, 0, 1)

    gram[...] = jnp.zeros_like(gram)
    aw[...] = jnp.zeros_like(aw)

    def anomalies(place):
        means = []
        for t in range(tiles):
            wide = raw[place * tiles + t, pl.ds(0, members), :].astype(F32)
            means.append(jnp.sum(wide, axis=0, keepdims=True) * (1.0 / members))
        for t, mean in enumerate(means):
            tile = place * tiles + t
            joint[tile, pl.ds(0, members), :] = (
                raw[tile, pl.ds(0, members), :].astype(F32) - mean).astype(BF)
            seen = obs[:, pl.ds(pl.multiple_of(place * H + t * LANE, LANE), LANE)]
            joint[tile, pl.ds(members, PACK), :] = jnp.broadcast_to(seen - mean, (PACK, LANE)).astype(BF)

    def coefficients(column, at):
        index = column + lax.broadcasted_iota(jnp.int32, (1, H), 1)
        strained = (index < count_ref[0]) | (index >= columns - H)
        strain = jnp.where(strained, 1.0, 0.0)
        for slot in range(terms):
            term = slots[slot, 0]
            row = band[pl.ds(term, 1), pl.ds(at, H)]
            if slot > 0:
                row = row * strain
            coef[pl.ds(slot * SUB, SUB), :] = jnp.broadcast_to(row, (SUB, H))

    def plan(place):
        lane = lax.broadcasted_iota(jnp.int32, (PACK, LANE), 1)
        steps = []
        for slot in range(terms):
            if slot < 3:
                steps.append((place * tiles + (0, -tiles, tiles)[slot], None, None))
            else:
                offset = slots[slot, 1] + 8 * LANE
                turn = lax.rem(offset, LANE)
                first = place * tiles + lax.div(offset, LANE) - 8
                steps.append((first, lax.rem(LANE - turn, LANE), lane < LANE - turn))
        return steps

    def whiten_rows(steps, starts, low, width):
        acc = [[None] * width for _ in starts]
        for slot, (first, back, keep) in enumerate(steps):
            weights = []
            for t in range(width):
                weight = coef[pl.ds(slot * SUB, SUB), pl.ds((low + t) * LANE, LANE)]
                weights.append(jnp.concatenate([weight, weight], 0))
            for r, at_row in enumerate(starts):
                def load(t):
                    return joint[first + low + t, pl.ds(at_row, PACK), :]

                if back is None:
                    values = [load(t) for t in range(width)]
                else:
                    rolled = [pltpu.roll(load(t), back, 1) for t in range(width + 1)]
                    values = [jnp.where(keep, rolled[t], rolled[t + 1]) for t in range(width)]
                for t in range(width):
                    product = values[t].astype(F32) * weights[t]
                    acc[r][t] = product if acc[r][t] is None else acc[r][t] + product
        return acc

    def products():
        block = jnp.concatenate([aw[t] for t in range(tiles)], axis=1)
        return lax.dot_general(
            block, block[:members], (((1,), (1,)), ((), ())), preferred_element_type=F32)

    def whiten_chunk(place, column, at):
        coefficients(column, at)
        steps = plan(place)
        pending = []

        def store_oldest():
            for at_row, tile, value in pending.pop(0):
                aw[tile, pl.ds(at_row, PACK), :] = value

        acc = whiten_rows(steps, [members], 0, tiles)[0]
        row = lax.broadcasted_iota(jnp.int32, (PACK, LANE), 0)
        parts = []
        for t in range(tiles):
            wide = acc[t]
            high = wide.astype(BF).astype(F32)
            rest = wide - high
            middle = rest.astype(BF).astype(F32)
            low = rest - middle
            split = jnp.where(row == 0, high, jnp.where(row == 1, middle, jnp.where(row == 2, low, 0.0)))
            parts.append((members, t, split.astype(BF)))
        pending.append(parts)
        scale = math.sqrt(members - 1) * row_factor
        misfit = [acc[t][0:1] * scale for t in range(tiles)]
        width = tiles // 2
        for group in range(members // (2 * PACK)):
            starts = [group * 2 * PACK, group * 2 * PACK + PACK]
            for first in (0, width):
                out = whiten_rows(steps, starts, first, width)
                pending.append([
                    (at_row, first + t, out[r][t].astype(BF))
                    for r, at_row in enumerate(starts) for t in range(width)])
                if len(pending) > LATE:
                    store_oldest()
        while pending:
            store_oldest()
        for t in range(tiles):
            row_out[:, pl.ds(at + t * LANE, LANE)] = misfit[t]

    if edge:
        for copy in copies:
            copy.wait()
        for place in range(6):
            tile_wait(place, members + (PACK if place in (0, 5) else 0))
        for place in (0, 5):
            for t in range(tiles):
                pieces = raw[place * tiles + t, pl.ds(members, PACK), :].astype(F32)
                obs[:, pl.ds(place * H + t * LANE, LANE)] = pieces[0:1] + pieces[1:2] + pieces[2:3]

        def centre_step(place, carry):
            anomalies(place)
            return carry

        lax.fori_loop(0, 6, centre_step, 0)

        def chunk_step(which, carry):
            added = products()
            whiten_chunk(1 + 3 * which, which * (columns - H), pl.multiple_of(which * H, H))
            gram[...] += added
            return carry

        lax.fori_loop(0, 2, chunk_step, 0)
        out_copies = [
            pltpu.make_async_copy(row_out.at[:, pl.ds(0, H)], misfit_out.at[:, pl.ds(0, H)], sems.at[0]),
            pltpu.make_async_copy(row_out.at[:, pl.ds(H, H)], misfit_out.at[:, pl.ds(columns - H, H)], sems.at[1]),
        ]
    else:
        for copy in copies:
            copy.wait()

        def centre_step(place, carry):
            tile_wait(place, members)
            anomalies(place)
            return carry

        lax.fori_loop(0, 2, centre_step, 0)

        def chunk_step(place, carry):
            tile_wait(place + 1, members)

            @pl.when(place + AHEAD - 1 < chunks)
            def _():
                coming = place + AHEAD - 1
                tile_copies(pred_ref, pl.multiple_of(coming * H, H), coming, members)

            added = products()
            anomalies(place + 1)
            column = pl.multiple_of(place * H, H)
            whiten_chunk(place, column, column)
            gram[...] += added
            return carry

        lax.fori_loop(1, chunks - 1, chunk_step, 0)
        inside = pl.ds(H, columns - 2 * H)
        out_copies = [pltpu.make_async_copy(row_out.at[:, inside], misfit_out.at[:, inside], sems.at[0])]
    for copy in out_copies:
        copy.start()
    gram[...] += products()

    tail = gram[pl.ds(members, 8), :]
    total = tail[0:1] + tail[1:2] + tail[2:3]
    both = gram[pl.ds(0, members), :]
    top = lax.broadcasted_iota(jnp.int32, (half, half), 0)
    corner = jnp.where(top == 0, total[:, :half], jnp.where(top == 1, total[:, half:], 0.0))
    upper = jnp.concatenate([both[:half, :half], corner], 1)
    lower = both[half:]
    upper = upper * (1.0 / obs_total)
    lower = lower * (1.0 / obs_total)
    if edge:
        upper = upper + gram_in[pl.ds(0, half), :]
        lower = lower + gram_in[pl.ds(half, half), :]
    gram_out[pl.ds(0, half), :] = upper
    gram_out[pl.ds(half, half), :] = lower
    for copy in out_copies:
        copy.wait()


def local_call(edge, obs_total, offsets, rows_count, predicted, observed, band, *more):
    members, columns = predicted.shape
    terms = band.shape[0]
    rows = members + PACK
    places = 6 if edge else columns // H
    tiles = places * (H // LANE)
    vmem = pl.BlockSpec(memory_space=pltpu.VMEM)
    smem = pl.BlockSpec(memory_space=pltpu.SMEM)
    far = pl.BlockSpec(memory_space=pltpu.HBM)
    in_specs = [smem, smem, far, far, far]
    if edge:
        in_specs += [far, far, vmem, far]
    scratch = [
        pltpu.VMEM((tiles, rows if edge else members, LANE), BF),
        pltpu.VMEM((tiles, rows, LANE), BF),
        pltpu.VMEM((H // LANE, rows, LANE), BF),
        pltpu.VMEM((SUB * terms, H), F32),
        pltpu.VMEM((rows, members), F32),
        pltpu.VMEM((1, places * H), F32),
        pltpu.VMEM((terms, 2 * H if edge else columns), F32),
        pltpu.VMEM((1, 2 * H if edge else columns), F32),
        pltpu.SMEM((8, 2), jnp.int32),
        pltpu.SemaphoreType.DMA((places + 4,)),
    ]
    work = 2 if edge else places - 2
    return pl.pallas_call(
        functools.partial(local_kernel, edge, columns, obs_total),
        out_shape=(
            jax.ShapeDtypeStruct((members, members), F32),
            jax.ShapeDtypeStruct((1, columns), F32),
        ),
        in_specs=in_specs,
        out_specs=[vmem, far],
        scratch_shapes=scratch,
        input_output_aliases={8: 1} if edge else {},
        compiler_params=pltpu.CompilerParams(vmem_limit_bytes=VMEM),
        cost_estimate=pl.CostEstimate(
            flops=2 * rows * members * H * work * 2, bytes_accessed=members * H * places * 2, transcendentals=0),
        name="edges" if edge else "inner",
    )(offsets, rows_count, predicted, observed, band, *more)


def update_kernel(sum_ref, params_ref, out_ref, work):
    members = params_ref.shape[1]
    highest = lax.Precision.HIGHEST
    row_index = lax.broadcasted_iota(jnp.int32, (members, members), 0)
    col_index = lax.broadcasted_iota(jnp.int32, (members, members), 1)
    identity = jnp.where(row_index == col_index, 1.0, 0.0).astype(F32)
    half = members // 2
    work[:, pl.ds(0, half)] = sum_ref[:, pl.ds(0, half)] + identity[:, :half]
    work[pl.ds(0, half), pl.ds(half, half)] = sum_ref[pl.ds(half, half), pl.ds(0, half)].T
    work[pl.ds(half, half), pl.ds(half, half)] = sum_ref[pl.ds(half, half), pl.ds(half, half)] + identity[half:, half:]
    work[:, pl.ds(members, members)] = identity
    panels = BLOCK // PANEL
    sub = lax.broadcasted_iota(jnp.int32, (PANEL, LANE), 0)
    eye = identity[:BLOCK, :BLOCK]

    def across(tile, column):
        return jnp.broadcast_to(tile[:, column:column + 1], (PANEL, LANE))

    def down(tile, row):
        return jnp.broadcast_to(tile[row:row + 1, :], (PANEL, LANE))

    for block in range(members // BLOCK):
        r0 = block * BLOCK
        start = jnp.concatenate([work[pl.ds(r0, BLOCK), pl.ds(r0, BLOCK)], eye], axis=1)
        tiles = [start[PANEL * t:PANEL * (t + 1)] for t in range(panels)]
        done = []
        for p in range(panels):
            c0 = PANEL * p
            tile = tiles[p]
            upper = tile
            full = tile
            cols = [across(tile, c0 + j) for j in range(PANEL)]
            full_cols = list(cols)
            scale = jnp.zeros((PANEL, LANE), F32)
            for k in range(PANEL):
                pivot = down(cols[k], k)
                inverse = 1.0 / pivot
                scale = jnp.where(sub == k, pivot, scale)
                below = jnp.where(sub > k, cols[k] * inverse, 0.0)

                def clear(values):
                    row = down(values, k) * inverse
                    return jnp.where(sub == k, row, values - full_cols[k] * row)

                for j in range(k + 1, PANEL):
                    cols[j] = cols[j] - below * down(cols[j], k)
                    full_cols[j] = clear(full_cols[j])
                upper = upper - below * down(upper, k)
                full = clear(full)
            done.append(upper * lax.rsqrt(scale))
            rows_of = [down(full, k) for k in range(PANEL)]
            for t in range(p + 1, panels):
                tile_t = tiles[t]
                change = [across(tile_t, c0 + k) * rows_of[k] for k in range(PANEL)]
                while len(change) > 1:
                    change = [a + b for a, b in zip(change[::2], change[1::2])]
                tiles[t] = tile_t - change[0]
        lower_inverse = jnp.concatenate(done, axis=0)[:, BLOCK:2 * BLOCK]
        solved = jnp.dot(lower_inverse, work[pl.ds(r0, BLOCK), :], precision=highest, preferred_element_type=F32)
        work[pl.ds(r0, BLOCK), :] = solved
        if r0 + BLOCK < members:
            rest = members - r0 - BLOCK
            factor = solved[:, r0 + BLOCK:members]
            work[pl.ds(r0 + BLOCK, rest), :] = work[pl.ds(r0 + BLOCK, rest), :] - lax.dot_general(
                factor, solved, (((0,), (0,)), ((), ())), precision=highest, preferred_element_type=F32)

    inverse = jnp.where(row_index >= col_index, work[:, pl.ds(members, members)], 0.0)
    projection = jnp.concatenate([sum_ref[pl.ds(r, 1), pl.ds(half, half)] for r in range(2)], 1)
    solved = jnp.sum(inverse * projection, axis=1, keepdims=True)
    weights = jnp.sum(inverse * solved, axis=0, keepdims=True)
    turned = inverse + weights
    turned = turned - jnp.mean(turned, axis=1, keepdims=True) + 1.0 / members
    high = turned.astype(BF)
    rest = turned - high.astype(F32)
    middle = rest.astype(BF)
    low = (rest - middle.astype(F32)).astype(BF)
    params = params_ref[...]

    def times(part):
        return lax.dot_general(params, part, (((1,), (1,)), ((), ())), preferred_element_type=F32)

    out_ref[...] = times(high) + (times(middle) + times(low))


def update(total, params):
    members = params.shape[1]
    vmem = pl.BlockSpec(memory_space=pltpu.VMEM)
    return pl.pallas_call(
        update_kernel,
        out_shape=jax.ShapeDtypeStruct(params.shape, F32),
        in_specs=[vmem, vmem],
        out_specs=vmem,
        scratch_shapes=[pltpu.VMEM((members, 2 * members), F32)],
        compiler_params=pltpu.CompilerParams(vmem_limit_bytes=VMEM // 4),
        name="update",
    )(total, params)


def halo_kernel(columns, pred_ref, obs_ref, first_ref, last_ref, obs, sems):
    members = pred_ref.shape[0]
    copies = []
    for side, (out, at) in enumerate(((first_ref, 0), (last_ref, columns - H))):
        copies.append(pltpu.make_async_copy(
            pred_ref.at[:, pl.ds(at, H)], out.at[pl.ds(0, members), :], sems.at[side]))
        copies.append(pltpu.make_async_copy(
            obs_ref.at[:, pl.ds(at, H)], obs.at[:, pl.ds(side * H, H)], sems.at[2 + side]))
    for copy in copies:
        copy.start()
    for copy in copies[1::2]:
        copy.wait()
    row = lax.broadcasted_iota(jnp.int32, (PACK, H), 0)
    for side, out in enumerate((first_ref, last_ref)):
        wide = jnp.broadcast_to(obs[:, pl.ds(side * H, H)], (PACK, H))
        high = wide.astype(BF).astype(F32)
        rest = wide - high
        middle = rest.astype(BF).astype(F32)
        low = rest - middle
        split = jnp.where(row == 0, high, jnp.where(row == 1, middle, jnp.where(row == 2, low, 0.0)))
        out[pl.ds(members, PACK), :] = split.astype(BF)
    for copy in copies[0::2]:
        copy.wait()


def halo_blocks(predicted, observed):
    members, columns = predicted.shape
    far = pl.BlockSpec(memory_space=pltpu.HBM)
    near = pl.BlockSpec(memory_space=pltpu.VMEM)
    block = jax.ShapeDtypeStruct((members + PACK, H), BF)
    return pl.pallas_call(
        functools.partial(halo_kernel, columns),
        out_shape=(block, block),
        in_specs=[far, far],
        out_specs=[near, near],
        scratch_shapes=[pltpu.VMEM((1, 2 * H), F32), pltpu.SemaphoreType.DMA((4,))],
        compiler_params=pltpu.CompilerParams(vmem_limit_bytes=VMEM),
        name="halos",
    )(predicted, observed)


def sum_over(values, axes):
    shards = lax.axis_size(axes)
    rows, width = values.shape
    parts = lax.all_to_all(values, axes, 0, 0, tiled=True)
    own = jnp.sum(parts.reshape(shards, rows // shards, width), axis=0)
    copies = jnp.broadcast_to(own[None], (shards, rows // shards, width)).reshape(rows, width)
    return lax.all_to_all(copies, axes, 0, 0, tiled=True)


def body(predicted, observed, band, offsets, rows_count, params):
    columns = predicted.shape[1]
    axes = ("obs", "par")
    shards = lax.axis_size(axes)
    obs_total = columns * shards
    up = [(i, i + 1) for i in range(shards - 1)]
    down = [(j, i) for i, j in up]
    obs_row = observed[None, :]
    first, last = halo_blocks(predicted, obs_row)
    left = lax.ppermute(last, axes, up)
    right = lax.ppermute(first, axes, down)
    gram, misfit = local_call(False, obs_total, offsets, rows_count, predicted, obs_row, band)
    gram, misfit = local_call(
        True, obs_total, offsets, rows_count, predicted, obs_row, band, left, right, gram, misfit)
    total = sum_over(gram, axes)
    return (update(total, params), misfit[0])


def solution(mesh):
    in_specs = (
        P(None, ("grp", "obs", "par")),
        P(("grp", "obs", "par")),
        P(None, ("grp", "obs", "par")),
        P(),
        P(("grp", "obs", "par")),
        P(("grp", "obs", "par"), None),
    )
    out_specs = (P(("grp", "obs", "par"), None), P(("grp", "obs", "par")))
    return jax.shard_map(body, mesh=mesh, in_specs=in_specs, out_specs=out_specs, check_vma=False)
```

```python
import functools
import math

import jax
import jax.numpy as jnp
from jax import lax
from jax.experimental import pallas as pl
from jax.experimental.pallas import tpu as pltpu
from jax.sharding import PartitionSpec as P

H = 1024
LANE = 128
SUB = 8
PACK = 16
TALL = 4
LATE = 0
AHEAD = 5
BLOCK = 64
PANEL = 8
VMEM = 64 * 2**20
BF = jnp.bfloat16
F32 = jnp.float32


def local_kernel(edge, columns, obs_total, *refs):
    if edge:
        (off_ref, count_ref, pred_ref, obs_ref, band_ref, left_ref, right_ref, gram_in, misfit_in,
         gram_out, misfit_out, raw, joint, aw, coef, gram, obs, band, row_out, slots,
         sems) = refs
    else:
        (off_ref, count_ref, pred_ref, obs_ref, band_ref,
         gram_out, misfit_out, raw, joint, aw, coef, gram, obs, band, row_out, slots,
         sems) = refs
    members = pred_ref.shape[0]
    terms = band_ref.shape[0]
    chunks = columns // H
    tiles = H // LANE
    half = members // 2
    row_factor = 1.0 / math.sqrt(obs_total)

    def tile_copies(source, column, place, height):
        for t in range(tiles):
            pltpu.make_async_copy(
                source.at[:, pl.ds(column + t * LANE, LANE)],
                raw.at[place * tiles + t, pl.ds(0, height), :], sems.at[place]).start()

    def tile_wait(place, height):
        whole = raw.at[pl.ds(place * tiles, tiles), pl.ds(0, height), :]
        pltpu.make_async_copy(whole, whole, sems.at[place]).wait()

    if edge:
        tile_copies(left_ref, 0, 0, members + PACK)
        for place, chunk in ((1, 0), (2, 1), (3, chunks - 2), (4, chunks - 1)):
            tile_copies(pred_ref, chunk * H, place, members)
        tile_copies(right_ref, 0, 5, members + PACK)
        copies = []
        for which in range(2):
            there = which * (columns - 2 * H)
            copies.append(pltpu.make_async_copy(
                obs_ref.at[:, pl.ds(there, 2 * H)], obs.at[:, pl.ds((1 + which * 2) * H, 2 * H)], sems.at[6 + which]))
            there = which * (columns - H)
            copies.append(pltpu.make_async_copy(
                band_ref.at[:, pl.ds(there, H)], band.at[:, pl.ds(which * H, H)], sems.at[8 + which]))
    else:
        copies = [
            pltpu.make_async_copy(obs_ref, obs, sems.at[chunks]),
            pltpu.make_async_copy(band_ref, band, sems.at[chunks + 1]),
        ]
        for place in range(AHEAD):
            tile_copies(pred_ref, place * H, place, members)
    for copy in copies:
        copy.start()

    slots[0, 0] = 0
    slots[0, 1] = 0
    free = jnp.int32(3)
    for term in range(1, terms):
        offset = off_ref[term]
        whole = (offset == H) | (offset == -H)
        place = jnp.where(offset == -H, 1, jnp.where(offset == H, 2, free))
        place = jnp.minimum(place, terms - 1)
        slots[place, 0] = jnp.int32(term)
        slots[place, 1] = offset
        free = free + jnp.where(whole, 0, 1)

    gram[...] = jnp.zeros_like(gram)
    aw[...] = jnp.zeros_like(aw)

    def anomalies(place):
        means = []
        for t in range(tiles):
            wide = raw[place * tiles + t, pl.ds(0, members), :].astype(F32)
            means.append(jnp.sum(wide, axis=0, keepdims=True) * (1.0 / members))
        for t, mean in enumerate(means):
            tile = place * tiles + t
            joint[tile, pl.ds(0, members), :] = (
                raw[tile, pl.ds(0, members), :].astype(F32) - mean).astype(BF)
            seen = obs[:, pl.ds(pl.multiple_of(place * H + t * LANE, LANE), LANE)]
            joint[tile, pl.ds(members, PACK), :] = jnp.broadcast_to(seen - mean, (PACK, LANE)).astype(BF)

    def coefficients(column, at):
        index = column + lax.broadcasted_iota(jnp.int32, (1, H), 1)
        strained = (index < count_ref[0]) | (index >= columns - H)
        strain = jnp.where(strained, 1.0, 0.0)
        for slot in range(terms):
            term = slots[slot, 0]
            row = band[pl.ds(term, 1), pl.ds(at, H)]
            if slot > 0:
                row = row * strain
            coef[pl.ds(slot * SUB, SUB), :] = jnp.broadcast_to(row, (SUB, H))

    def plan(place):
        lane = lax.broadcasted_iota(jnp.int32, (PACK, LANE), 1)
        steps = []
        for slot in range(terms):
            if slot < 3:
                steps.append((place * tiles + (0, -tiles, tiles)[slot], None, None))
            else:
                offset = slots[slot, 1] + 8 * LANE
                turn = lax.rem(offset, LANE)
                first = place * tiles + lax.div(offset, LANE) - 8
                steps.append((first, lax.rem(LANE - turn, LANE), lane < LANE - turn))
        return steps

    def whiten_rows(steps, starts, low, width):
        acc = [[None] * width for _ in starts]
        for slot, (first, back, keep) in enumerate(steps):
            weights = []
            for t in range(width):
                weight = coef[pl.ds(slot * SUB, SUB), pl.ds((low + t) * LANE, LANE)]
                weights.append(jnp.concatenate([weight, weight], 0))
            for r, at_row in enumerate(starts):
                def load(t):
                    return joint[first + low + t, pl.ds(at_row, PACK), :]

                if back is None:
                    values = [load(t) for t in range(width)]
                else:
                    rolled = [pltpu.roll(load(t), back, 1) for t in range(width + 1)]
                    values = [jnp.where(keep, rolled[t], rolled[t + 1]) for t in range(width)]
                for t in range(width):
                    product = values[t].astype(F32) * weights[t]
                    acc[r][t] = product if acc[r][t] is None else acc[r][t] + product
        return acc

    def products():
        block = jnp.concatenate([aw[t] for t in range(tiles)], axis=1)
        return lax.dot_general(
            block, block[:members], (((1,), (1,)), ((), ())), preferred_element_type=F32)

    def whiten_chunk(place, column, at):
        coefficients(column, at)
        steps = plan(place)
        pending = []

        def store_oldest():
            for at_row, tile, value in pending.pop(0):
                aw[tile, pl.ds(at_row, PACK), :] = value

        acc = whiten_rows(steps, [members], 0, tiles)[0]
        row = lax.broadcasted_iota(jnp.int32, (PACK, LANE), 0)
        parts = []
        for t in range(tiles):
            wide = acc[t]
            high = wide.astype(BF).astype(F32)
            rest = wide - high
            middle = rest.astype(BF).astype(F32)
            low = rest - middle
            split = jnp.where(row == 0, high, jnp.where(row == 1, middle, jnp.where(row == 2, low, 0.0)))
            parts.append((members, t, split.astype(BF)))
        pending.append(parts)
        scale = math.sqrt(members - 1) * row_factor
        misfit = [acc[t][0:1] * scale for t in range(tiles)]
        width = tiles // 2
        for group in range(members // (TALL * PACK)):
            starts = [(group * TALL + r) * PACK for r in range(TALL)]
            for first in (0, width):
                out = whiten_rows(steps, starts, first, width)
                pending.append([
                    (at_row, first + t, out[r][t].astype(BF))
                    for r, at_row in enumerate(starts) for t in range(width)])
                if len(pending) > LATE:
                    store_oldest()
        while pending:
            store_oldest()
        for t in range(tiles):
            row_out[:, pl.ds(at + t * LANE, LANE)] = misfit[t]

    if edge:
        for copy in copies:
            copy.wait()
        for place in range(6):
            tile_wait(place, members + (PACK if place in (0, 5) else 0))
        for place in (0, 5):
            for t in range(tiles):
                pieces = raw[place * tiles + t, pl.ds(members, PACK), :].astype(F32)
                obs[:, pl.ds(place * H + t * LANE, LANE)] = pieces[0:1] + pieces[1:2] + pieces[2:3]

        def centre_step(place, carry):
            anomalies(place)
            return carry

        lax.fori_loop(0, 6, centre_step, 0)

        def chunk_step(which, carry):
            added = products()
            whiten_chunk(1 + 3 * which, which * (columns - H), pl.multiple_of(which * H, H))
            gram[...] += added
            return carry

        lax.fori_loop(0, 2, chunk_step, 0)
        out_copies = [
            pltpu.make_async_copy(row_out.at[:, pl.ds(0, H)], misfit_out.at[:, pl.ds(0, H)], sems.at[0]),
            pltpu.make_async_copy(row_out.at[:, pl.ds(H, H)], misfit_out.at[:, pl.ds(columns - H, H)], sems.at[1]),
        ]
    else:
        for copy in copies:
            copy.wait()

        def centre_step(place, carry):
            tile_wait(place, members)
            anomalies(place)
            return carry

        lax.fori_loop(0, 2, centre_step, 0)

        def chunk_step(place, carry):
            tile_wait(place + 1, members)

            @pl.when(place + AHEAD - 1 < chunks)
            def _():
                coming = place + AHEAD - 1
                tile_copies(pred_ref, pl.multiple_of(coming * H, H), coming, members)

            added = products()
            anomalies(place + 1)
            column = pl.multiple_of(place * H, H)
            whiten_chunk(place, column, column)
            gram[...] += added
            return carry

        lax.fori_loop(1, chunks - 1, chunk_step, 0)
        inside = pl.ds(H, columns - 2 * H)
        out_copies = [pltpu.make_async_copy(row_out.at[:, inside], misfit_out.at[:, inside], sems.at[0])]
    for copy in out_copies:
        copy.start()
    gram[...] += products()

    tail = gram[pl.ds(members, 8), :]
    total = tail[0:1] + tail[1:2] + tail[2:3]
    both = gram[pl.ds(0, members), :]
    down = lax.broadcasted_iota(jnp.int32, (half, half), 0)
    across = lax.broadcasted_iota(jnp.int32, (half, half), 1)

    def tuck(block, piece):
        block = jnp.where((down == 1) & (across == half - 1), piece[:, :1], block)
        return jnp.where((down == 0) & (across > 0), piece, block)

    blocks = (
        tuck(both[:half, :half], total[:, :half]),
        both[half:, :half],
        tuck(both[half:, half:], total[:, half:]),
    )
    for index, block in enumerate(blocks):
        at = pl.ds(index * half, half)
        block = block * (1.0 / obs_total)
        gram_out[:, at] = block + gram_in[:, at] if edge else block
    for copy in out_copies:
        copy.wait()


def local_call(edge, obs_total, offsets, rows_count, predicted, observed, band, *more):
    members, columns = predicted.shape
    terms = band.shape[0]
    rows = members + PACK
    places = 6 if edge else columns // H
    tiles = places * (H // LANE)
    vmem = pl.BlockSpec(memory_space=pltpu.VMEM)
    smem = pl.BlockSpec(memory_space=pltpu.SMEM)
    far = pl.BlockSpec(memory_space=pltpu.HBM)
    in_specs = [smem, smem, far, far, far]
    if edge:
        in_specs += [far, far, vmem, far]
    scratch = [
        pltpu.VMEM((tiles, rows if edge else members, LANE), BF),
        pltpu.VMEM((tiles, rows, LANE), BF),
        pltpu.VMEM((H // LANE, rows, LANE), BF),
        pltpu.VMEM((SUB * terms, H), F32),
        pltpu.VMEM((rows, members), F32),
        pltpu.VMEM((1, places * H), F32),
        pltpu.VMEM((terms, 2 * H if edge else columns), F32),
        pltpu.VMEM((1, 2 * H if edge else columns), F32),
        pltpu.SMEM((8, 2), jnp.int32),
        pltpu.SemaphoreType.DMA((places + 4,)),
    ]
    work = 2 if edge else places - 2
    return pl.pallas_call(
        functools.partial(local_kernel, edge, columns, obs_total),
        out_shape=(
            jax.ShapeDtypeStruct((members // 2, members // 2 * 3), F32),
            jax.ShapeDtypeStruct((1, columns), F32),
        ),
        in_specs=in_specs,
        out_specs=[vmem, far],
        scratch_shapes=scratch,
        input_output_aliases={8: 1} if edge else {},
        compiler_params=pltpu.CompilerParams(vmem_limit_bytes=VMEM),
        cost_estimate=pl.CostEstimate(
            flops=2 * rows * members * H * work * 2, bytes_accessed=members * H * places * 2, transcendentals=0),
        name="edges" if edge else "inner",
    )(offsets, rows_count, predicted, observed, band, *more)


def update_kernel(sum_ref, params_ref, out_ref, work):
    members = params_ref.shape[1]
    highest = lax.Precision.HIGHEST
    row_index = lax.broadcasted_iota(jnp.int32, (members, members), 0)
    col_index = lax.broadcasted_iota(jnp.int32, (members, members), 1)
    identity = jnp.where(row_index == col_index, 1.0, 0.0).astype(F32)
    half = members // 2
    eye_half = identity[:half, :half]
    lower = row_index[:half, :half] >= col_index[:half, :half]

    def mirrored(block):
        return jnp.where(lower, block, block.T) + eye_half

    def tucked(block):
        first = lax.broadcasted_iota(jnp.int32, (1, half), 1) == 0
        return jnp.where(first, block[1:2, half - 1:half], block[0:1, :])

    blocks = [sum_ref[:, pl.ds(index * half, half)] for index in range(3)]
    work[pl.ds(0, half), pl.ds(0, half)] = mirrored(blocks[0])
    work[pl.ds(0, half), pl.ds(half, half)] = blocks[1].T
    work[pl.ds(half, half), pl.ds(0, half)] = blocks[1]
    work[pl.ds(half, half), pl.ds(half, half)] = mirrored(blocks[2])
    projection = jnp.concatenate([tucked(blocks[0]), tucked(blocks[2])], 1)
    work[:, pl.ds(members, members)] = identity
    panels = BLOCK // PANEL
    sub = lax.broadcasted_iota(jnp.int32, (PANEL, LANE), 0)
    eye = identity[:BLOCK, :BLOCK]

    def across(tile, column):
        return jnp.broadcast_to(tile[:, column:column + 1], (PANEL, LANE))

    def down(tile, row):
        return jnp.broadcast_to(tile[row:row + 1, :], (PANEL, LANE))

    for block in range(members // BLOCK):
        r0 = block * BLOCK
        start = jnp.concatenate([work[pl.ds(r0, BLOCK), pl.ds(r0, BLOCK)], eye], axis=1)
        tiles = [start[PANEL * t:PANEL * (t + 1)] for t in range(panels)]
        done = []
        for p in range(panels):
            c0 = PANEL * p
            tile = tiles[p]
            upper = tile
            full = tile
            cols = [across(tile, c0 + j) for j in range(PANEL)]
            scale = jnp.zeros((PANEL, LANE), F32)
            for k in range(0, PANEL, 2):
                left, right = cols[k], cols[k + 1]
                a, b, c = down(left, k), down(left, k + 1), down(right, k + 1)
                det = a * c - b * b
                inverse = 1.0 / det
                ratio = b / a
                scale = jnp.where(sub == k, a, jnp.where(sub == k + 1, c - b * ratio, scale))
                from_left = c * left - b * right
                from_right = a * right - b * left

                def change_of(values):
                    x, y = down(values, k), down(values, k + 1)
                    return x, y, (from_left * x + from_right * y) * inverse

                def clear(values):
                    x, y, change = change_of(values)
                    own = jnp.where(sub == k, c * x - b * y, a * y - b * x) * inverse
                    return jnp.where((sub == k) | (sub == k + 1), own, values - change)

                x, y, change = change_of(upper)
                upper = upper - jnp.where(sub > k + 1, change, jnp.where(sub == k + 1, ratio * x, 0.0))
                full = clear(full)
                for j in range(k + 2, PANEL):
                    cols[j] = clear(cols[j])
            done.append(upper * lax.rsqrt(scale))
            rows_of = [down(full, k) for k in range(PANEL)]
            for t in range(p + 1, panels):
                tile_t = tiles[t]
                change = [across(tile_t, c0 + k) * rows_of[k] for k in range(PANEL)]
                while len(change) > 1:
                    change = [a + b for a, b in zip(change[::2], change[1::2])]
                tiles[t] = tile_t - change[0]
        lower_inverse = jnp.concatenate(done, axis=0)[:, BLOCK:2 * BLOCK]
        solved = jnp.dot(lower_inverse, work[pl.ds(r0, BLOCK), :], precision=highest, preferred_element_type=F32)
        work[pl.ds(r0, BLOCK), :] = solved
        if r0 + BLOCK < members:
            rest = members - r0 - BLOCK
            factor = solved[:, r0 + BLOCK:members]
            work[pl.ds(r0 + BLOCK, rest), :] = work[pl.ds(r0 + BLOCK, rest), :] - lax.dot_general(
                factor, solved, (((0,), (0,)), ((), ())), precision=highest, preferred_element_type=F32)

    inverse = jnp.where(row_index >= col_index, work[:, pl.ds(members, members)], 0.0)
    solved = jnp.sum(inverse * projection, axis=1, keepdims=True)
    weights = jnp.sum(inverse * solved, axis=0, keepdims=True)
    turned = inverse + weights
    turned = turned - jnp.mean(turned, axis=1, keepdims=True) + 1.0 / members
    high = turned.astype(BF)
    rest = turned - high.astype(F32)
    middle = rest.astype(BF)
    low = (rest - middle.astype(F32)).astype(BF)
    params = params_ref[...]

    def times(part):
        return lax.dot_general(params, part, (((1,), (1,)), ((), ())), preferred_element_type=F32)

    out_ref[...] = times(high) + (times(middle) + times(low))


def update(total, params):
    members = params.shape[1]
    vmem = pl.BlockSpec(memory_space=pltpu.VMEM)
    return pl.pallas_call(
        update_kernel,
        out_shape=jax.ShapeDtypeStruct(params.shape, F32),
        in_specs=[vmem, vmem],
        out_specs=vmem,
        scratch_shapes=[pltpu.VMEM((members, 2 * members), F32)],
        compiler_params=pltpu.CompilerParams(vmem_limit_bytes=VMEM // 4),
        name="update",
    )(total, params)


def halo_kernel(columns, pred_ref, obs_ref, first_ref, last_ref, obs, sems):
    members = pred_ref.shape[0]
    copies = []
    for side, (out, at) in enumerate(((first_ref, 0), (last_ref, columns - H))):
        copies.append(pltpu.make_async_copy(
            pred_ref.at[:, pl.ds(at, H)], out.at[pl.ds(0, members), :], sems.at[side]))
        copies.append(pltpu.make_async_copy(
            obs_ref.at[:, pl.ds(at, H)], obs.at[:, pl.ds(side * H, H)], sems.at[2 + side]))
    for copy in copies:
        copy.start()
    for copy in copies[1::2]:
        copy.wait()
    row = lax.broadcasted_iota(jnp.int32, (PACK, H), 0)
    for side, out in enumerate((first_ref, last_ref)):
        wide = jnp.broadcast_to(obs[:, pl.ds(side * H, H)], (PACK, H))
        high = wide.astype(BF).astype(F32)
        rest = wide - high
        middle = rest.astype(BF).astype(F32)
        low = rest - middle
        split = jnp.where(row == 0, high, jnp.where(row == 1, middle, jnp.where(row == 2, low, 0.0)))
        out[pl.ds(members, PACK), :] = split.astype(BF)
    for copy in copies[0::2]:
        copy.wait()


def halo_blocks(predicted, observed):
    members, columns = predicted.shape
    far = pl.BlockSpec(memory_space=pltpu.HBM)
    near = pl.BlockSpec(memory_space=pltpu.VMEM)
    block = jax.ShapeDtypeStruct((members + PACK, H), BF)
    return pl.pallas_call(
        functools.partial(halo_kernel, columns),
        out_shape=(block, block),
        in_specs=[far, far],
        out_specs=[near, near],
        scratch_shapes=[pltpu.VMEM((1, 2 * H), F32), pltpu.SemaphoreType.DMA((4,))],
        compiler_params=pltpu.CompilerParams(vmem_limit_bytes=VMEM),
        name="halos",
    )(predicted, observed)


def sum_over(values, axes):
    shards = lax.axis_size(axes)
    rows, width = values.shape
    parts = lax.all_to_all(values, axes, 0, 0, tiled=True)
    own = jnp.sum(parts.reshape(shards, rows // shards, width), axis=0)
    copies = jnp.broadcast_to(own[None], (shards, rows // shards, width)).reshape(rows, width)
    return lax.all_to_all(copies, axes, 0, 0, tiled=True)


def body(predicted, observed, band, offsets, rows_count, params):
    columns = predicted.shape[1]
    axes = ("obs", "par")
    shards = lax.axis_size(axes)
    obs_total = columns * shards
    up = [(i, i + 1) for i in range(shards - 1)]
    down = [(j, i) for i, j in up]
    obs_row = observed[None, :]
    first, last = halo_blocks(predicted, obs_row)
    left = lax.ppermute(last, axes, up)
    right = lax.ppermute(first, axes, down)
    gram, misfit = local_call(False, obs_total, offsets, rows_count, predicted, obs_row, band)
    gram, misfit = local_call(
        True, obs_total, offsets, rows_count, predicted, obs_row, band, left, right, gram, misfit)
    total = sum_over(gram, axes)
    return (update(total, params), misfit[0])


def solution(mesh):
    in_specs = (
        P(None, ("grp", "obs", "par")),
        P(("grp", "obs", "par")),
        P(None, ("grp", "obs", "par")),
        P(),
        P(("grp", "obs", "par")),
        P(("grp", "obs", "par"), None),
    )
    out_specs = (P(("grp", "obs", "par"), None), P(("grp", "obs", "par")))
    return jax.shard_map(body, mesh=mesh, in_specs=in_specs, out_specs=out_specs, check_vma=False)
```

```python
import functools
import math

import jax
import jax.numpy as jnp
from jax import lax
from jax.experimental import pallas as pl
from jax.experimental.pallas import tpu as pltpu
from jax.sharding import PartitionSpec as P

H = 1024
LANE = 128
SUB = 8
PACK = 16
TALL = 4
LATE = 0
AHEAD = 5
BLOCK = 64
PANEL = 8
VMEM = 64 * 2**20
BF = jnp.bfloat16
F32 = jnp.float32


def local_kernel(edge, columns, obs_total, *refs):
    if edge:
        (off_ref, count_ref, pred_ref, obs_ref, band_ref, left_ref, right_ref, gram_in, misfit_in,
         gram_out, misfit_out, raw, special, aw, coef, mean_white, gram, obs, band, row_out, slots,
         sems) = refs
    else:
        (off_ref, count_ref, pred_ref, obs_ref, band_ref,
         gram_out, misfit_out, raw, special, aw, coef, mean_white, gram, obs, band, row_out, slots,
         sems) = refs
    members = pred_ref.shape[0]
    terms = band_ref.shape[0]
    chunks = columns // H
    tiles = H // LANE
    half = members // 2
    row_factor = 1.0 / math.sqrt(obs_total)

    def tile_copies(source, column, place, height):
        for t in range(tiles):
            pltpu.make_async_copy(
                source.at[:, pl.ds(column + t * LANE, LANE)],
                raw.at[place * tiles + t, pl.ds(0, height), :], sems.at[place]).start()

    def tile_wait(place, height):
        whole = raw.at[pl.ds(place * tiles, tiles), pl.ds(0, height), :]
        pltpu.make_async_copy(whole, whole, sems.at[place]).wait()

    if edge:
        tile_copies(left_ref, 0, 0, members + PACK)
        for place, chunk in ((1, 0), (2, 1), (3, chunks - 2), (4, chunks - 1)):
            tile_copies(pred_ref, chunk * H, place, members)
        tile_copies(right_ref, 0, 5, members + PACK)
        copies = []
        for which in range(2):
            there = which * (columns - 2 * H)
            copies.append(pltpu.make_async_copy(
                obs_ref.at[:, pl.ds(there, 2 * H)], obs.at[:, pl.ds((1 + which * 2) * H, 2 * H)], sems.at[6 + which]))
            there = which * (columns - H)
            copies.append(pltpu.make_async_copy(
                band_ref.at[:, pl.ds(there, H)], band.at[:, pl.ds(which * H, H)], sems.at[8 + which]))
    else:
        copies = [
            pltpu.make_async_copy(obs_ref, obs, sems.at[chunks]),
            pltpu.make_async_copy(band_ref, band, sems.at[chunks + 1]),
        ]
        for place in range(AHEAD):
            tile_copies(pred_ref, place * H, place, members)
    for copy in copies:
        copy.start()

    slots[0, 0] = 0
    slots[0, 1] = 0
    free = jnp.int32(3)
    for term in range(1, terms):
        offset = off_ref[term]
        whole = (offset == H) | (offset == -H)
        place = jnp.where(offset == -H, 1, jnp.where(offset == H, 2, free))
        place = jnp.minimum(place, terms - 1)
        slots[place, 0] = jnp.int32(term)
        slots[place, 1] = offset
        free = free + jnp.where(whole, 0, 1)

    gram[...] = jnp.zeros_like(gram)
    aw[...] = jnp.zeros_like(aw)

    def mean_rows(place):
        block = jnp.concatenate(
            [raw[place * tiles + t, pl.ds(0, members), :] for t in range(tiles)], axis=1)
        return jnp.dot(jnp.full((PACK, members), 1.0 / members, BF), block, preferred_element_type=F32)[:SUB]

    def keep_special(place, mean):
        seen = obs[:, pl.ds(pl.multiple_of(place * H, H), H)]
        innovation = (seen - mean).astype(BF).astype(F32)
        value = jnp.where(lax.broadcasted_iota(jnp.int32, (SUB, H), 0) == 0, innovation, mean)
        for t in range(tiles):
            special[place * tiles + t] = value[:, t * LANE:(t + 1) * LANE]

    def coefficients(column, at):
        index = column + lax.broadcasted_iota(jnp.int32, (1, H), 1)
        strained = (index < count_ref[0]) | (index >= columns - H)
        strain = jnp.where(strained, 1.0, 0.0)
        for slot in range(terms):
            term = slots[slot, 0]
            row = band[pl.ds(term, 1), pl.ds(at, H)]
            if slot > 0:
                row = row * strain
            coef[pl.ds(slot * SUB, SUB), :] = jnp.broadcast_to(row, (SUB, H))

    def plan(place):
        lane = lax.broadcasted_iota(jnp.int32, (PACK, LANE), 1)
        low_lane = lax.broadcasted_iota(jnp.int32, (SUB, LANE), 1)
        steps = []
        for slot in range(terms):
            if slot < 3:
                steps.append((place * tiles + (0, -tiles, tiles)[slot], None, None, None))
            else:
                offset = slots[slot, 1] + 8 * LANE
                turn = lax.rem(offset, LANE)
                first = place * tiles + lax.div(offset, LANE) - 8
                back = lax.rem(LANE - turn, LANE)
                steps.append((first, back, lane < LANE - turn, low_lane < LANE - turn))
        return steps

    def shifted(load, back, keep, width):
        if back is None:
            return [load(t) for t in range(width)]
        rolled = [pltpu.roll(load(t), back, 1) for t in range(width + 1)]
        return [jnp.where(keep, rolled[t], rolled[t + 1]) for t in range(width)]

    def whiten_special(steps):
        acc = [None] * tiles
        for slot, (first, back, _, keep) in enumerate(steps):
            values = shifted(lambda t: special[first + t], back, keep, tiles)
            for t in range(tiles):
                product = values[t] * coef[pl.ds(slot * SUB, SUB), pl.ds(t * LANE, LANE)]
                acc[t] = product if acc[t] is None else acc[t] + product
        return acc

    def whiten_rows(steps, starts, low, width):
        def twice(ref, at_row, t):
            value = ref[pl.ds(at_row, SUB), pl.ds((low + t) * LANE, LANE)]
            return jnp.concatenate([value, value], 0)

        off = [twice(mean_white, 0, t) for t in range(width)]
        acc = [list(off) for _ in starts]
        for slot, (first, back, keep, _) in enumerate(steps):
            weights = [twice(coef, slot * SUB, t) for t in range(width)]
            for r, at_row in enumerate(starts):
                values = shifted(lambda t: raw[first + low + t, pl.ds(at_row, PACK), :], back, keep, width)
                for t in range(width):
                    product = values[t].astype(F32) * weights[t]
                    acc[r][t] = product - acc[r][t] if slot == 0 else acc[r][t] + product
        return acc

    def products():
        block = jnp.concatenate([aw[t] for t in range(tiles)], axis=1)
        return lax.dot_general(
            block, block[:members], (((1,), (1,)), ((), ())), preferred_element_type=F32)

    def whiten_chunk(place, column, at):
        coefficients(column, at)
        steps = plan(place)
        pending = []

        def store_oldest():
            for at_row, tile, value in pending.pop(0):
                aw[tile, pl.ds(at_row, PACK), :] = value

        acc = whiten_special(steps)
        row = lax.broadcasted_iota(jnp.int32, (PACK, LANE), 0)
        parts = []
        for t in range(tiles):
            mean_white[:, pl.ds(t * LANE, LANE)] = jnp.broadcast_to(acc[t][1:2], (SUB, LANE))
            wide = jnp.broadcast_to(acc[t][0:1], (PACK, LANE))
            high = wide.astype(BF).astype(F32)
            rest = wide - high
            middle = rest.astype(BF).astype(F32)
            low = rest - middle
            split = jnp.where(row == 0, high, jnp.where(row == 1, middle, jnp.where(row == 2, low, 0.0)))
            parts.append((members, t, split.astype(BF)))
        pending.append(parts)
        scale = math.sqrt(members - 1) * row_factor
        misfit = [acc[t][0:1] * scale for t in range(tiles)]
        width = tiles // 2
        for group in range(members // (TALL * PACK)):
            starts = [(group * TALL + r) * PACK for r in range(TALL)]
            for first in (0, width):
                out = whiten_rows(steps, starts, first, width)
                pending.append([
                    (at_row, first + t, out[r][t].astype(BF))
                    for r, at_row in enumerate(starts) for t in range(width)])
                if len(pending) > LATE:
                    store_oldest()
        while pending:
            store_oldest()
        for t in range(tiles):
            row_out[:, pl.ds(at + t * LANE, LANE)] = misfit[t]

    if edge:
        for copy in copies:
            copy.wait()
        for place in range(6):
            tile_wait(place, members + (PACK if place in (0, 5) else 0))
        for place in (0, 5):
            for t in range(tiles):
                pieces = raw[place * tiles + t, pl.ds(members, PACK), :].astype(F32)
                obs[:, pl.ds(place * H + t * LANE, LANE)] = pieces[0:1] + pieces[1:2] + pieces[2:3]

        def centre_step(place, carry):
            keep_special(place, mean_rows(place))
            return carry

        lax.fori_loop(0, 6, centre_step, 0)

        def chunk_step(which, carry):
            added = products()
            whiten_chunk(1 + 3 * which, which * (columns - H), pl.multiple_of(which * H, H))
            gram[...] += added
            return carry

        lax.fori_loop(0, 2, chunk_step, 0)
        out_copies = [
            pltpu.make_async_copy(row_out.at[:, pl.ds(0, H)], misfit_out.at[:, pl.ds(0, H)], sems.at[0]),
            pltpu.make_async_copy(row_out.at[:, pl.ds(H, H)], misfit_out.at[:, pl.ds(columns - H, H)], sems.at[1]),
        ]
    else:
        for copy in copies:
            copy.wait()

        def centre_step(place, carry):
            tile_wait(place, members)
            keep_special(place, mean_rows(place))
            return carry

        lax.fori_loop(0, 3, centre_step, 0)

        def chunk_step(place, carry):
            ahead = jnp.minimum(place + 2, chunks - 1)

            @pl.when(place + 2 < chunks)
            def _():
                tile_wait(ahead, members)

            @pl.when(place + AHEAD - 1 < chunks)
            def _():
                coming = place + AHEAD - 1
                tile_copies(pred_ref, pl.multiple_of(coming * H, H), coming, members)

            added = products()
            mean = mean_rows(ahead)
            column = pl.multiple_of(place * H, H)
            whiten_chunk(place, column, column)
            gram[...] += added
            keep_special(ahead, mean)
            return carry

        lax.fori_loop(1, chunks - 1, chunk_step, 0)
        inside = pl.ds(H, columns - 2 * H)
        out_copies = [pltpu.make_async_copy(row_out.at[:, inside], misfit_out.at[:, inside], sems.at[0])]
    for copy in out_copies:
        copy.start()
    gram[...] += products()

    tail = gram[pl.ds(members, 8), :]
    total = tail[0:1] + tail[1:2] + tail[2:3]
    both = gram[pl.ds(0, members), :]
    down = lax.broadcasted_iota(jnp.int32, (half, half), 0)
    across = lax.broadcasted_iota(jnp.int32, (half, half), 1)

    def tuck(block, piece):
        block = jnp.where((down == 1) & (across == half - 1), piece[:, :1], block)
        return jnp.where((down == 0) & (across > 0), piece, block)

    blocks = (
        tuck(both[:half, :half], total[:, :half]),
        both[half:, :half],
        tuck(both[half:, half:], total[:, half:]),
    )
    for index, block in enumerate(blocks):
        at = pl.ds(index * half, half)
        block = block * (1.0 / obs_total)
        gram_out[:, at] = block + gram_in[:, at] if edge else block
    for copy in out_copies:
        copy.wait()


def local_call(edge, obs_total, offsets, rows_count, predicted, observed, band, *more):
    members, columns = predicted.shape
    terms = band.shape[0]
    rows = members + PACK
    places = 6 if edge else columns // H
    tiles = places * (H // LANE)
    vmem = pl.BlockSpec(memory_space=pltpu.VMEM)
    smem = pl.BlockSpec(memory_space=pltpu.SMEM)
    far = pl.BlockSpec(memory_space=pltpu.HBM)
    in_specs = [smem, smem, far, far, far]
    if edge:
        in_specs += [far, far, vmem, far]
    scratch = [
        pltpu.VMEM((tiles, rows if edge else members, LANE), BF),
        pltpu.VMEM((tiles, SUB, LANE), F32),
        pltpu.VMEM((H // LANE, rows, LANE), BF),
        pltpu.VMEM((SUB * terms, H), F32),
        pltpu.VMEM((SUB, H), F32),
        pltpu.VMEM((rows, members), F32),
        pltpu.VMEM((1, places * H), F32),
        pltpu.VMEM((terms, 2 * H if edge else columns), F32),
        pltpu.VMEM((1, 2 * H if edge else columns), F32),
        pltpu.SMEM((8, 2), jnp.int32),
        pltpu.SemaphoreType.DMA((places + 4,)),
    ]
    work = 2 if edge else places - 2
    return pl.pallas_call(
        functools.partial(local_kernel, edge, columns, obs_total),
        out_shape=(
            jax.ShapeDtypeStruct((members // 2, members // 2 * 3), F32),
            jax.ShapeDtypeStruct((1, columns), F32),
        ),
        in_specs=in_specs,
        out_specs=[vmem, far],
        scratch_shapes=scratch,
        input_output_aliases={8: 1} if edge else {},
        compiler_params=pltpu.CompilerParams(vmem_limit_bytes=VMEM),
        cost_estimate=pl.CostEstimate(
            flops=2 * rows * members * H * work * 2, bytes_accessed=members * H * places * 2, transcendentals=0),
        name="edges" if edge else "inner",
    )(offsets, rows_count, predicted, observed, band, *more)


def update_kernel(sum_ref, params_ref, out_ref, work):
    members = params_ref.shape[1]
    highest = lax.Precision.HIGHEST
    row_index = lax.broadcasted_iota(jnp.int32, (members, members), 0)
    col_index = lax.broadcasted_iota(jnp.int32, (members, members), 1)
    identity = jnp.where(row_index == col_index, 1.0, 0.0).astype(F32)
    half = members // 2
    eye_half = identity[:half, :half]
    lower = row_index[:half, :half] >= col_index[:half, :half]

    def mirrored(block):
        return jnp.where(lower, block, block.T) + eye_half

    def tucked(block):
        first = lax.broadcasted_iota(jnp.int32, (1, half), 1) == 0
        return jnp.where(first, block[1:2, half - 1:half], block[0:1, :])

    blocks = [sum_ref[:, pl.ds(index * half, half)] for index in range(3)]
    work[pl.ds(0, half), pl.ds(0, half)] = mirrored(blocks[0])
    work[pl.ds(0, half), pl.ds(half, half)] = blocks[1].T
    work[pl.ds(half, half), pl.ds(0, half)] = blocks[1]
    work[pl.ds(half, half), pl.ds(half, half)] = mirrored(blocks[2])
    projection = jnp.concatenate([tucked(blocks[0]), tucked(blocks[2])], 1)
    work[:, pl.ds(members, members)] = identity
    panels = BLOCK // PANEL
    sub = lax.broadcasted_iota(jnp.int32, (PANEL, LANE), 0)
    eye = identity[:BLOCK, :BLOCK]

    def across(tile, column):
        return jnp.broadcast_to(tile[:, column:column + 1], (PANEL, LANE))

    def down(tile, row):
        return jnp.broadcast_to(tile[row:row + 1, :], (PANEL, LANE))

    for block in range(members // BLOCK):
        r0 = block * BLOCK
        start = jnp.concatenate([work[pl.ds(r0, BLOCK), pl.ds(r0, BLOCK)], eye], axis=1)
        tiles = [start[PANEL * t:PANEL * (t + 1)] for t in range(panels)]
        done = []
        for p in range(panels):
            c0 = PANEL * p
            tile = tiles[p]
            upper = tile
            full = tile
            cols = [across(tile, c0 + j) for j in range(PANEL)]
            scale = jnp.zeros((PANEL, LANE), F32)
            for k in range(0, PANEL, 2):
                left, right = cols[k], cols[k + 1]
                a, b, c = down(left, k), down(left, k + 1), down(right, k + 1)
                det = a * c - b * b
                inverse = 1.0 / det
                ratio = b / a
                scale = jnp.where(sub == k, a, jnp.where(sub == k + 1, c - b * ratio, scale))
                from_left = c * left - b * right
                from_right = a * right - b * left

                def change_of(values):
                    x, y = down(values, k), down(values, k + 1)
                    return x, y, (from_left * x + from_right * y) * inverse

                def clear(values):
                    x, y, change = change_of(values)
                    own = jnp.where(sub == k, c * x - b * y, a * y - b * x) * inverse
                    return jnp.where((sub == k) | (sub == k + 1), own, values - change)

                x, y, change = change_of(upper)
                upper = upper - jnp.where(sub > k + 1, change, jnp.where(sub == k + 1, ratio * x, 0.0))
                full = clear(full)
                for j in range(k + 2, PANEL):
                    cols[j] = clear(cols[j])
            done.append(upper * lax.rsqrt(scale))
            rows_of = [down(full, k) for k in range(PANEL)]
            for t in range(p + 1, panels):
                tile_t = tiles[t]
                change = [across(tile_t, c0 + k) * rows_of[k] for k in range(PANEL)]
                while len(change) > 1:
                    change = [a + b for a, b in zip(change[::2], change[1::2])]
                tiles[t] = tile_t - change[0]
        lower_inverse = jnp.concatenate(done, axis=0)[:, BLOCK:2 * BLOCK]
        solved = jnp.dot(lower_inverse, work[pl.ds(r0, BLOCK), :], precision=highest, preferred_element_type=F32)
        work[pl.ds(r0, BLOCK), :] = solved
        if r0 + BLOCK < members:
            rest = members - r0 - BLOCK
            factor = solved[:, r0 + BLOCK:members]
            work[pl.ds(r0 + BLOCK, rest), :] = work[pl.ds(r0 + BLOCK, rest), :] - lax.dot_general(
                factor, solved, (((0,), (0,)), ((), ())), precision=highest, preferred_element_type=F32)

    inverse = jnp.where(row_index >= col_index, work[:, pl.ds(members, members)], 0.0)
    solved = jnp.sum(inverse * projection, axis=1, keepdims=True)
    weights = jnp.sum(inverse * solved, axis=0, keepdims=True)
    turned = inverse + weights
    turned = turned - jnp.mean(turned, axis=1, keepdims=True) + 1.0 / members
    high = turned.astype(BF)
    rest = turned - high.astype(F32)
    middle = rest.astype(BF)
    low = (rest - middle.astype(F32)).astype(BF)
    params = params_ref[...]

    def times(part):
        return lax.dot_general(params, part, (((1,), (1,)), ((), ())), preferred_element_type=F32)

    out_ref[...] = times(high) + (times(middle) + times(low))


def update(total, params):
    members = params.shape[1]
    vmem = pl.BlockSpec(memory_space=pltpu.VMEM)
    return pl.pallas_call(
        update_kernel,
        out_shape=jax.ShapeDtypeStruct(params.shape, F32),
        in_specs=[vmem, vmem],
        out_specs=vmem,
        scratch_shapes=[pltpu.VMEM((members, 2 * members), F32)],
        compiler_params=pltpu.CompilerParams(vmem_limit_bytes=VMEM // 4),
        name="update",
    )(total, params)


def halo_kernel(columns, pred_ref, obs_ref, first_ref, last_ref, obs, sems):
    members = pred_ref.shape[0]
    copies = []
    for side, (out, at) in enumerate(((first_ref, 0), (last_ref, columns - H))):
        copies.append(pltpu.make_async_copy(
            pred_ref.at[:, pl.ds(at, H)], out.at[pl.ds(0, members), :], sems.at[side]))
        copies.append(pltpu.make_async_copy(
            obs_ref.at[:, pl.ds(at, H)], obs.at[:, pl.ds(side * H, H)], sems.at[2 + side]))
    for copy in copies:
        copy.start()
    for copy in copies[1::2]:
        copy.wait()
    row = lax.broadcasted_iota(jnp.int32, (PACK, H), 0)
    for side, out in enumerate((first_ref, last_ref)):
        wide = jnp.broadcast_to(obs[:, pl.ds(side * H, H)], (PACK, H))
        high = wide.astype(BF).astype(F32)
        rest = wide - high
        middle = rest.astype(BF).astype(F32)
        low = rest - middle
        split = jnp.where(row == 0, high, jnp.where(row == 1, middle, jnp.where(row == 2, low, 0.0)))
        out[pl.ds(members, PACK), :] = split.astype(BF)
    for copy in copies[0::2]:
        copy.wait()


def halo_blocks(predicted, observed):
    members, columns = predicted.shape
    far = pl.BlockSpec(memory_space=pltpu.HBM)
    near = pl.BlockSpec(memory_space=pltpu.VMEM)
    block = jax.ShapeDtypeStruct((members + PACK, H), BF)
    return pl.pallas_call(
        functools.partial(halo_kernel, columns),
        out_shape=(block, block),
        in_specs=[far, far],
        out_specs=[near, near],
        scratch_shapes=[pltpu.VMEM((1, 2 * H), F32), pltpu.SemaphoreType.DMA((4,))],
        compiler_params=pltpu.CompilerParams(vmem_limit_bytes=VMEM),
        name="halos",
    )(predicted, observed)


def sum_over(values, axes):
    shards = lax.axis_size(axes)
    rows, width = values.shape
    parts = lax.all_to_all(values, axes, 0, 0, tiled=True)
    own = jnp.sum(parts.reshape(shards, rows // shards, width), axis=0)
    copies = jnp.broadcast_to(own[None], (shards, rows // shards, width)).reshape(rows, width)
    return lax.all_to_all(copies, axes, 0, 0, tiled=True)


def body(predicted, observed, band, offsets, rows_count, params):
    columns = predicted.shape[1]
    axes = ("obs", "par")
    shards = lax.axis_size(axes)
    obs_total = columns * shards
    up = [(i, i + 1) for i in range(shards - 1)]
    down = [(j, i) for i, j in up]
    obs_row = observed[None, :]
    first, last = halo_blocks(predicted, obs_row)
    left = lax.ppermute(last, axes, up)
    right = lax.ppermute(first, axes, down)
    gram, misfit = local_call(False, obs_total, offsets, rows_count, predicted, obs_row, band)
    gram, misfit = local_call(
        True, obs_total, offsets, rows_count, predicted, obs_row, band, left, right, gram, misfit)
    total = sum_over(gram, axes)
    return (update(total, params), misfit[0])


def solution(mesh):
    in_specs = (
        P(None, ("grp", "obs", "par")),
        P(("grp", "obs", "par")),
        P(None, ("grp", "obs", "par")),
        P(),
        P(("grp", "obs", "par")),
        P(("grp", "obs", "par"), None),
    )
    out_specs = (P(("grp", "obs", "par"), None), P(("grp", "obs", "par")))
    return jax.shard_map(body, mesh=mesh, in_specs=in_specs, out_specs=out_specs, check_vma=False)
```

```python
import functools
import math

import jax
import jax.numpy as jnp
from jax import lax
from jax.experimental import pallas as pl
from jax.experimental.pallas import tpu as pltpu
from jax.sharding import PartitionSpec as P

H = 1024
LANE = 128
SUB = 8
PACK = 16
TALL = 4
LATE = 1
AHEAD = 5
BLOCK = 64
PANEL = 8
VMEM = 64 * 2**20
BF = jnp.bfloat16
F32 = jnp.float32


def local_kernel(edge, columns, obs_total, *refs):
    if edge:
        (off_ref, count_ref, pred_ref, obs_ref, band_ref, left_ref, right_ref, gram_in, misfit_in,
         gram_out, misfit_out, raw, special, aw, coef, mean_white, gram, obs, band, row_out, slots,
         sems) = refs
    else:
        (off_ref, count_ref, pred_ref, obs_ref, band_ref,
         gram_out, misfit_out, raw, special, aw, coef, mean_white, gram, obs, band, row_out, slots,
         sems) = refs
    members = pred_ref.shape[0]
    terms = band_ref.shape[0]
    chunks = columns // H
    tiles = H // LANE
    half = members // 2
    row_factor = 1.0 / math.sqrt(obs_total)

    def tile_copies(source, column, place, height):
        for t in range(tiles):
            pltpu.make_async_copy(
                source.at[:, pl.ds(column + t * LANE, LANE)],
                raw.at[place * tiles + t, pl.ds(0, height), :], sems.at[place]).start()

    def tile_wait(place, height):
        whole = raw.at[pl.ds(place * tiles, tiles), pl.ds(0, height), :]
        pltpu.make_async_copy(whole, whole, sems.at[place]).wait()

    if edge:
        copies = []
        for which in range(2):
            there = which * (columns - 2 * H)
            copies.append(pltpu.make_async_copy(
                obs_ref.at[:, pl.ds(there, 2 * H)], obs.at[:, pl.ds((1 + which * 2) * H, 2 * H)], sems.at[6 + which]))
            there = which * (columns - H)
            copies.append(pltpu.make_async_copy(
                band_ref.at[:, pl.ds(there, H)], band.at[:, pl.ds(which * H, H)], sems.at[8 + which]))
    else:
        copies = [
            pltpu.make_async_copy(obs_ref, obs, sems.at[chunks]),
            pltpu.make_async_copy(band_ref, band, sems.at[chunks + 1]),
        ]
    for copy in copies:
        copy.start()
    if edge:
        tile_copies(left_ref, 0, 0, members + PACK)
        for place, chunk in ((1, 0), (2, 1), (3, chunks - 2), (4, chunks - 1)):
            tile_copies(pred_ref, chunk * H, place, members)
        tile_copies(right_ref, 0, 5, members + PACK)
    else:
        for place in range(AHEAD):
            tile_copies(pred_ref, place * H, place, members)

    slots[0, 0] = 0
    slots[0, 1] = 0
    free = jnp.int32(3)
    for term in range(1, terms):
        offset = off_ref[term]
        whole = (offset == H) | (offset == -H)
        place = jnp.where(offset == -H, 1, jnp.where(offset == H, 2, free))
        place = jnp.minimum(place, terms - 1)
        slots[place, 0] = jnp.int32(term)
        slots[place, 1] = offset
        free = free + jnp.where(whole, 0, 1)

    gram[...] = jnp.zeros_like(gram)
    aw[...] = jnp.zeros_like(aw)

    def mean_rows(place):
        block = jnp.concatenate(
            [raw[place * tiles + t, pl.ds(0, members), :] for t in range(tiles)], axis=1)
        return jnp.dot(jnp.full((PACK, members), 1.0 / members, BF), block, preferred_element_type=F32)[:SUB]

    def keep_special(place, mean):
        seen = obs[:, pl.ds(pl.multiple_of(place * H, H), H)]
        innovation = (seen - mean).astype(BF).astype(F32)
        value = jnp.where(lax.broadcasted_iota(jnp.int32, (SUB, H), 0) == 0, innovation, mean)
        for t in range(tiles):
            special[place * tiles + t] = value[:, t * LANE:(t + 1) * LANE]

    def coefficients(column, at):
        index = column + lax.broadcasted_iota(jnp.int32, (1, H), 1)
        strained = (index < count_ref[0]) | (index >= columns - H)
        strain = jnp.where(strained, 1.0, 0.0)
        for slot in range(terms):
            term = slots[slot, 0]
            row = band[pl.ds(term, 1), pl.ds(at, H)]
            if slot > 0:
                row = row * strain
            coef[pl.ds(slot * SUB, SUB), :] = jnp.broadcast_to(row, (SUB, H))

    def plan(place):
        lane = lax.broadcasted_iota(jnp.int32, (PACK, LANE), 1)
        low_lane = lax.broadcasted_iota(jnp.int32, (SUB, LANE), 1)
        steps = []
        for slot in range(terms):
            if slot < 3:
                steps.append((place * tiles + (0, -tiles, tiles)[slot], None, None, None))
            else:
                offset = slots[slot, 1] + 8 * LANE
                turn = lax.rem(offset, LANE)
                first = place * tiles + lax.div(offset, LANE) - 8
                back = lax.rem(LANE - turn, LANE)
                steps.append((first, back, lane < LANE - turn, low_lane < LANE - turn))
        return steps

    def shifted(load, back, keep, width):
        if back is None:
            return [load(t) for t in range(width)]
        rolled = [pltpu.roll(load(t), back, 1) for t in range(width + 1)]
        return [jnp.where(keep, rolled[t], rolled[t + 1]) for t in range(width)]

    def whiten_special(steps):
        acc = [None] * tiles
        for slot, (first, back, _, keep) in enumerate(steps):
            values = shifted(lambda t: special[first + t], back, keep, tiles)
            for t in range(tiles):
                product = values[t] * coef[pl.ds(slot * SUB, SUB), pl.ds(t * LANE, LANE)]
                acc[t] = product if acc[t] is None else acc[t] + product
        return acc

    def whiten_rows(steps, starts, low, width):
        def twice(ref, at_row, t):
            value = ref[pl.ds(at_row, SUB), pl.ds((low + t) * LANE, LANE)]
            return jnp.concatenate([value, value], 0)

        off = [twice(mean_white, 0, t) for t in range(width)]
        acc = [list(off) for _ in starts]
        for slot, (first, back, keep, _) in enumerate(steps):
            weights = [twice(coef, slot * SUB, t) for t in range(width)]
            for r, at_row in enumerate(starts):
                values = shifted(lambda t: raw[first + low + t, pl.ds(at_row, PACK), :], back, keep, width)
                for t in range(width):
                    product = values[t].astype(F32) * weights[t]
                    acc[r][t] = product - acc[r][t] if slot == 0 else acc[r][t] + product
        return acc

    def products():
        block = jnp.concatenate([aw[t] for t in range(tiles)], axis=1)
        return lax.dot_general(
            block, block[:members], (((1,), (1,)), ((), ())), preferred_element_type=F32)

    def whiten_chunk(place, column, at):
        coefficients(column, at)
        steps = plan(place)
        pending = []

        def store_oldest():
            for at_row, tile, value in pending.pop(0):
                aw[tile, pl.ds(at_row, PACK), :] = value

        acc = whiten_special(steps)
        row = lax.broadcasted_iota(jnp.int32, (PACK, LANE), 0)
        parts = []
        for t in range(tiles):
            mean_white[:, pl.ds(t * LANE, LANE)] = jnp.broadcast_to(acc[t][1:2], (SUB, LANE))
            wide = jnp.broadcast_to(acc[t][0:1], (PACK, LANE))
            high = wide.astype(BF).astype(F32)
            rest = wide - high
            middle = rest.astype(BF).astype(F32)
            low = rest - middle
            split = jnp.where(row == 0, high, jnp.where(row == 1, middle, jnp.where(row == 2, low, 0.0)))
            parts.append((members, t, split.astype(BF)))
        pending.append(parts)
        scale = math.sqrt(members - 1) * row_factor
        misfit = [acc[t][0:1] * scale for t in range(tiles)]
        width = tiles // 2
        for group in range(members // (TALL * PACK)):
            starts = [(group * TALL + r) * PACK for r in range(TALL)]
            for first in (0, width):
                out = whiten_rows(steps, starts, first, width)
                pending.append([
                    (at_row, first + t, out[r][t].astype(BF))
                    for r, at_row in enumerate(starts) for t in range(width)])
                if len(pending) > LATE:
                    store_oldest()
        while pending:
            store_oldest()
        for t in range(tiles):
            row_out[:, pl.ds(at + t * LANE, LANE)] = misfit[t]

    if edge:
        for copy in copies:
            copy.wait()
        for which in range(2):
            near = range(3 * which, 3 * which + 3)
            halo = 5 * which
            for place in near:
                tile_wait(place, members + (PACK if place == halo else 0))
            if which == 1:
                gram[...] += products()
            means = [mean_rows(place) for place in near]
            for t in range(tiles):
                pieces = raw[halo * tiles + t, pl.ds(members, PACK), :].astype(F32)
                obs[:, pl.ds(halo * H + t * LANE, LANE)] = pieces[0:1] + pieces[1:2] + pieces[2:3]
            for place, mean in zip(near, means):
                keep_special(place, mean)
            whiten_chunk(1 + 3 * which, which * (columns - H), which * H)
        out_copies = [
            pltpu.make_async_copy(row_out.at[:, pl.ds(0, H)], misfit_out.at[:, pl.ds(0, H)], sems.at[0]),
            pltpu.make_async_copy(row_out.at[:, pl.ds(H, H)], misfit_out.at[:, pl.ds(columns - H, H)], sems.at[1]),
        ]
    else:
        for copy in copies:
            copy.wait()

        def centre_step(place, carry):
            tile_wait(place, members)
            keep_special(place, mean_rows(place))
            return carry

        lax.fori_loop(0, 3, centre_step, 0)

        def chunk_step(place, carry):
            ahead = jnp.minimum(place + 2, chunks - 1)

            @pl.when(place + 2 < chunks)
            def _():
                tile_wait(ahead, members)

            @pl.when(place + AHEAD - 1 < chunks)
            def _():
                coming = place + AHEAD - 1
                tile_copies(pred_ref, pl.multiple_of(coming * H, H), coming, members)

            added = products()
            mean = mean_rows(ahead)
            column = pl.multiple_of(place * H, H)
            whiten_chunk(place, column, column)
            gram[...] += added
            keep_special(ahead, mean)
            return carry

        lax.fori_loop(1, chunks - 1, chunk_step, 0)
        inside = pl.ds(H, columns - 2 * H)
        out_copies = [pltpu.make_async_copy(row_out.at[:, inside], misfit_out.at[:, inside], sems.at[0])]
    for copy in out_copies:
        copy.start()
    gram[...] += products()

    tail = gram[pl.ds(members, 8), :]
    total = tail[0:1] + tail[1:2] + tail[2:3]
    both = gram[pl.ds(0, members), :]
    down = lax.broadcasted_iota(jnp.int32, (half, half), 0)
    across = lax.broadcasted_iota(jnp.int32, (half, half), 1)

    def tuck(block, piece):
        block = jnp.where((down == 1) & (across == half - 1), piece[:, :1], block)
        return jnp.where((down == 0) & (across > 0), piece, block)

    blocks = (
        tuck(both[:half, :half], total[:, :half]),
        both[half:, :half],
        tuck(both[half:, half:], total[:, half:]),
    )
    for index, block in enumerate(blocks):
        at = pl.ds(index * half, half)
        block = block * (1.0 / obs_total)
        gram_out[:, at] = block + gram_in[:, at] if edge else block
    for copy in out_copies:
        copy.wait()


def local_call(edge, obs_total, offsets, rows_count, predicted, observed, band, *more):
    members, columns = predicted.shape
    terms = band.shape[0]
    rows = members + PACK
    places = 6 if edge else columns // H
    tiles = places * (H // LANE)
    vmem = pl.BlockSpec(memory_space=pltpu.VMEM)
    smem = pl.BlockSpec(memory_space=pltpu.SMEM)
    far = pl.BlockSpec(memory_space=pltpu.HBM)
    in_specs = [smem, smem, far, far, far]
    if edge:
        in_specs += [far, far, vmem, far]
    scratch = [
        pltpu.VMEM((tiles, rows if edge else members, LANE), BF),
        pltpu.VMEM((tiles, SUB, LANE), F32),
        pltpu.VMEM((H // LANE, rows, LANE), BF),
        pltpu.VMEM((SUB * terms, H), F32),
        pltpu.VMEM((SUB, H), F32),
        pltpu.VMEM((rows, members), F32),
        pltpu.VMEM((1, places * H), F32),
        pltpu.VMEM((terms, 2 * H if edge else columns), F32),
        pltpu.VMEM((1, 2 * H if edge else columns), F32),
        pltpu.SMEM((8, 2), jnp.int32),
        pltpu.SemaphoreType.DMA((places + 4,)),
    ]
    work = 2 if edge else places - 2
    return pl.pallas_call(
        functools.partial(local_kernel, edge, columns, obs_total),
        out_shape=(
            jax.ShapeDtypeStruct((members // 2, members // 2 * 3), F32),
            jax.ShapeDtypeStruct((1, columns), F32),
        ),
        in_specs=in_specs,
        out_specs=[vmem, far],
        scratch_shapes=scratch,
        input_output_aliases={8: 1} if edge else {},
        compiler_params=pltpu.CompilerParams(vmem_limit_bytes=VMEM),
        cost_estimate=pl.CostEstimate(
            flops=2 * rows * members * H * work * 2, bytes_accessed=members * H * places * 2, transcendentals=0),
        name="edges" if edge else "inner",
    )(offsets, rows_count, predicted, observed, band, *more)


def update_kernel(sum_ref, params_ref, out_ref, work, params, sem):
    members = params_ref.shape[1]
    fetch = pltpu.make_async_copy(params_ref, params, sem)
    fetch.start()
    highest = lax.Precision.HIGHEST
    row_index = lax.broadcasted_iota(jnp.int32, (members, members), 0)
    col_index = lax.broadcasted_iota(jnp.int32, (members, members), 1)
    identity = jnp.where(row_index == col_index, 1.0, 0.0).astype(F32)
    half = members // 2
    eye_half = identity[:half, :half]
    lower = row_index[:half, :half] >= col_index[:half, :half]

    def mirrored(block):
        return jnp.where(lower, block, block.T) + eye_half

    def tucked(block):
        first = lax.broadcasted_iota(jnp.int32, (1, half), 1) == 0
        return jnp.where(first, block[1:2, half - 1:half], block[0:1, :])

    blocks = [sum_ref[:, pl.ds(index * half, half)] for index in range(3)]
    work[pl.ds(0, half), pl.ds(0, half)] = mirrored(blocks[0])
    work[pl.ds(0, half), pl.ds(half, half)] = blocks[1].T
    work[pl.ds(half, half), pl.ds(0, half)] = blocks[1]
    work[pl.ds(half, half), pl.ds(half, half)] = mirrored(blocks[2])
    projection = jnp.concatenate([tucked(blocks[0]), tucked(blocks[2])], 1)
    work[:, pl.ds(members, members)] = identity
    panels = BLOCK // PANEL
    sub = lax.broadcasted_iota(jnp.int32, (PANEL, LANE), 0)
    eye = identity[:BLOCK, :BLOCK]

    def across(tile, column):
        return jnp.broadcast_to(tile[:, column:column + 1], (PANEL, LANE))

    def down(tile, row):
        return jnp.broadcast_to(tile[row:row + 1, :], (PANEL, LANE))

    for block in range(members // BLOCK):
        r0 = block * BLOCK
        start = jnp.concatenate([work[pl.ds(r0, BLOCK), pl.ds(r0, BLOCK)], eye], axis=1)
        tiles = [start[PANEL * t:PANEL * (t + 1)] for t in range(panels)]
        done = []
        for p in range(panels):
            c0 = PANEL * p
            tile = tiles[p]
            upper = tile
            full = tile
            cols = [across(tile, c0 + j) for j in range(PANEL)]
            scale = jnp.zeros((PANEL, LANE), F32)
            for k in range(0, PANEL, 2):
                left, right = cols[k], cols[k + 1]
                a, b, c = down(left, k), down(left, k + 1), down(right, k + 1)
                det = a * c - b * b
                inverse = 1.0 / det
                ratio = b / a
                scale = jnp.where(sub == k, a, jnp.where(sub == k + 1, c - b * ratio, scale))
                from_left = c * left - b * right
                from_right = a * right - b * left

                def change_of(values):
                    x, y = down(values, k), down(values, k + 1)
                    return x, y, (from_left * x + from_right * y) * inverse

                def clear(values):
                    x, y, change = change_of(values)
                    own = jnp.where(sub == k, c * x - b * y, a * y - b * x) * inverse
                    return jnp.where((sub == k) | (sub == k + 1), own, values - change)

                x, y, change = change_of(upper)
                upper = upper - jnp.where(sub > k + 1, change, jnp.where(sub == k + 1, ratio * x, 0.0))
                full = clear(full)
                for j in range(k + 2, PANEL):
                    cols[j] = clear(cols[j])
            done.append(upper * lax.rsqrt(scale))
            rows_of = [down(full, k) for k in range(PANEL)]
            for t in range(p + 1, panels):
                tile_t = tiles[t]
                change = [across(tile_t, c0 + k) * rows_of[k] for k in range(PANEL)]
                while len(change) > 1:
                    change = [a + b for a, b in zip(change[::2], change[1::2])]
                tiles[t] = tile_t - change[0]
        lower_inverse = jnp.concatenate(done, axis=0)[:, BLOCK:2 * BLOCK]
        begin = (r0 + BLOCK) // LANE * LANE
        end = members + -(-(r0 + BLOCK) // LANE) * LANE
        wide = pl.ds(begin, end - begin)
        solved = jnp.dot(lower_inverse, work[pl.ds(r0, BLOCK), wide], precision=highest, preferred_element_type=F32)
        work[pl.ds(r0, BLOCK), wide] = solved
        if r0 + BLOCK < members:
            rest = members - r0 - BLOCK
            factor = solved[:, r0 + BLOCK - begin:members - begin]
            work[pl.ds(r0 + BLOCK, rest), wide] = work[pl.ds(r0 + BLOCK, rest), wide] - lax.dot_general(
                factor, solved, (((0,), (0,)), ((), ())), precision=highest, preferred_element_type=F32)

    inverse = jnp.where(row_index >= col_index, work[:, pl.ds(members, members)], 0.0)
    solved = jnp.sum(inverse * projection, axis=1, keepdims=True)
    weights = jnp.sum(inverse * solved, axis=0, keepdims=True)
    turned = inverse + weights
    turned = turned - jnp.mean(turned, axis=1, keepdims=True) + 1.0 / members
    high = turned.astype(BF)
    rest = turned - high.astype(F32)
    middle = rest.astype(BF)
    low = (rest - middle.astype(F32)).astype(BF)
    fetch.wait()

    def times(part):
        return lax.dot_general(params[...], part, (((1,), (1,)), ((), ())), preferred_element_type=F32)

    out_ref[...] = times(high) + (times(middle) + times(low))


def update(total, params):
    members = params.shape[1]
    vmem = pl.BlockSpec(memory_space=pltpu.VMEM)
    return pl.pallas_call(
        update_kernel,
        out_shape=jax.ShapeDtypeStruct(params.shape, F32),
        in_specs=[vmem, pl.BlockSpec(memory_space=pltpu.HBM)],
        out_specs=vmem,
        scratch_shapes=[
            pltpu.VMEM((members, 2 * members), F32), pltpu.VMEM(params.shape, BF), pltpu.SemaphoreType.DMA],
        compiler_params=pltpu.CompilerParams(vmem_limit_bytes=VMEM - 5 * total.size),
        name="update",
    )(total, params)


def halo_kernel(columns, pred_ref, obs_ref, first_ref, last_ref, obs, sems):
    members = pred_ref.shape[0]
    copies = []
    for side, (out, at) in enumerate(((first_ref, 0), (last_ref, columns - H))):
        copies.append(pltpu.make_async_copy(
            pred_ref.at[:, pl.ds(at, H)], out.at[pl.ds(0, members), :], sems.at[side]))
        copies.append(pltpu.make_async_copy(
            obs_ref.at[:, pl.ds(at, H)], obs.at[:, pl.ds(side * H, H)], sems.at[2 + side]))
    for copy in copies:
        copy.start()
    for copy in copies[1::2]:
        copy.wait()
    row = lax.broadcasted_iota(jnp.int32, (PACK, H), 0)
    for side, out in enumerate((first_ref, last_ref)):
        wide = jnp.broadcast_to(obs[:, pl.ds(side * H, H)], (PACK, H))
        high = wide.astype(BF).astype(F32)
        rest = wide - high
        middle = rest.astype(BF).astype(F32)
        low = rest - middle
        split = jnp.where(row == 0, high, jnp.where(row == 1, middle, jnp.where(row == 2, low, 0.0)))
        out[pl.ds(members, PACK), :] = split.astype(BF)
    for copy in copies[0::2]:
        copy.wait()


def halo_blocks(predicted, observed):
    members, columns = predicted.shape
    far = pl.BlockSpec(memory_space=pltpu.HBM)
    near = pl.BlockSpec(memory_space=pltpu.VMEM)
    block = jax.ShapeDtypeStruct((members + PACK, H), BF)
    return pl.pallas_call(
        functools.partial(halo_kernel, columns),
        out_shape=(block, block),
        in_specs=[far, far],
        out_specs=[near, near],
        scratch_shapes=[pltpu.VMEM((1, 2 * H), F32), pltpu.SemaphoreType.DMA((4,))],
        compiler_params=pltpu.CompilerParams(vmem_limit_bytes=VMEM),
        name="halos",
    )(predicted, observed)


def sum_over(values, axes):
    shards = lax.axis_size(axes)
    rows, width = values.shape
    parts = lax.all_to_all(values, axes, 0, 0, tiled=True)
    own = jnp.sum(parts.reshape(shards, rows // shards, width), axis=0)
    copies = jnp.broadcast_to(own[None], (shards, rows // shards, width)).reshape(rows, width)
    return lax.all_to_all(copies, axes, 0, 0, tiled=True)


def body(predicted, observed, band, offsets, rows_count, params):
    columns = predicted.shape[1]
    axes = ("obs", "par")
    shards = lax.axis_size(axes)
    obs_total = columns * shards
    up = [(i, i + 1) for i in range(shards - 1)]
    down = [(j, i) for i, j in up]
    obs_row = observed[None, :]
    first, last = halo_blocks(predicted, obs_row)
    left = lax.ppermute(last, axes, up)
    right = lax.ppermute(first, axes, down)
    gram, misfit = local_call(False, obs_total, offsets, rows_count, predicted, obs_row, band)
    gram, misfit = local_call(
        True, obs_total, offsets, rows_count, predicted, obs_row, band, left, right, gram, misfit)
    total = sum_over(gram, axes)
    return (update(total, params), misfit[0])


def solution(mesh):
    in_specs = (
        P(None, ("grp", "obs", "par")),
        P(("grp", "obs", "par")),
        P(None, ("grp", "obs", "par")),
        P(),
        P(("grp", "obs", "par")),
        P(("grp", "obs", "par"), None),
    )
    out_specs = (P(("grp", "obs", "par"), None), P(("grp", "obs", "par")))
    return jax.shard_map(body, mesh=mesh, in_specs=in_specs, out_specs=out_specs, check_vma=False)
```

```python
import functools
import math

import jax
import jax.numpy as jnp
from jax import lax
from jax.experimental import pallas as pl
from jax.experimental.pallas import tpu as pltpu
from jax.sharding import PartitionSpec as P

H = 1024
LANE = 128
SUB = 8
PACK = 16
TALL = 4
LATE = 1
AHEAD = 5
BLOCK = 64
PANEL = 8
VMEM = 64 * 2**20
BF = jnp.bfloat16
F32 = jnp.float32


def local_kernel(edge, columns, obs_total, *refs):
    if edge:
        (off_ref, count_ref, pred_ref, obs_ref, band_ref, left_ref, right_ref, gram_in, misfit_in,
         gram_out, misfit_out, raw, special, aw, coef, mean_white, gram, obs, band, row_out, slots,
         sems) = refs
    else:
        (off_ref, count_ref, pred_ref, obs_ref, band_ref,
         gram_out, misfit_out, raw, special, aw, coef, mean_white, gram, obs, band, row_out, slots,
         sems) = refs
    members = pred_ref.shape[0]
    terms = band_ref.shape[0]
    chunks = columns // H
    tiles = H // LANE
    half = members // 2
    row_factor = 1.0 / math.sqrt(obs_total)

    def tile_copies(source, column, place, height):
        for t in range(tiles):
            pltpu.make_async_copy(
                source.at[:, pl.ds(column + t * LANE, LANE)],
                raw.at[place * tiles + t, pl.ds(0, height), :], sems.at[place]).start()

    def tile_wait(place, height):
        whole = raw.at[pl.ds(place * tiles, tiles), pl.ds(0, height), :]
        pltpu.make_async_copy(whole, whole, sems.at[place]).wait()

    if edge:
        copies = []
        for which in range(2):
            there = which * (columns - 2 * H)
            copies.append(pltpu.make_async_copy(
                obs_ref.at[:, pl.ds(there, 2 * H)], obs.at[:, pl.ds((1 + which * 2) * H, 2 * H)], sems.at[6 + which]))
            there = which * (columns - H)
            copies.append(pltpu.make_async_copy(
                band_ref.at[:, pl.ds(there, H)], band.at[:, pl.ds(which * H, H)], sems.at[8 + which]))
    else:
        copies = [
            pltpu.make_async_copy(obs_ref, obs, sems.at[chunks]),
            pltpu.make_async_copy(band_ref, band, sems.at[chunks + 1]),
        ]
    for copy in copies:
        copy.start()
    if edge:
        tile_copies(left_ref, 0, 0, members + PACK)
        for place, chunk in ((1, 0), (2, 1), (3, chunks - 2), (4, chunks - 1)):
            tile_copies(pred_ref, chunk * H, place, members)
        tile_copies(right_ref, 0, 5, members + PACK)
    else:
        for place in range(AHEAD):
            tile_copies(pred_ref, place * H, place, members)

    slots[0, 0] = 0
    slots[0, 1] = 0
    free = jnp.int32(3)
    for term in range(1, terms):
        offset = off_ref[term]
        whole = (offset == H) | (offset == -H)
        place = jnp.where(offset == -H, 1, jnp.where(offset == H, 2, free))
        place = jnp.minimum(place, terms - 1)
        slots[place, 0] = jnp.int32(term)
        slots[place, 1] = offset
        free = free + jnp.where(whole, 0, 1)

    gram[...] = jnp.zeros_like(gram)
    aw[...] = jnp.zeros_like(aw)

    def mean_rows(place):
        block = jnp.concatenate(
            [raw[place * tiles + t, pl.ds(0, members), :] for t in range(tiles)], axis=1)
        return jnp.dot(jnp.full((PACK, members), 1.0 / members, BF), block, preferred_element_type=F32)[:SUB]

    def keep_special(place, mean):
        seen = obs[:, pl.ds(pl.multiple_of(place * H, H), H)]
        innovation = (seen - mean).astype(BF).astype(F32)
        value = jnp.where(lax.broadcasted_iota(jnp.int32, (SUB, H), 0) == 0, innovation, mean)
        for t in range(tiles):
            special[place * tiles + t] = value[:, t * LANE:(t + 1) * LANE]

    def coefficients(column, at):
        index = column + lax.broadcasted_iota(jnp.int32, (1, H), 1)
        strained = (index < count_ref[0]) | (index >= columns - H)
        strain = jnp.where(strained, 1.0, 0.0)
        for slot in range(terms):
            term = slots[slot, 0]
            row = band[pl.ds(term, 1), pl.ds(at, H)]
            if slot > 0:
                row = row * strain
            coef[pl.ds(slot * SUB, SUB), :] = jnp.broadcast_to(row, (SUB, H))

    def plan(place):
        lane = lax.broadcasted_iota(jnp.int32, (PACK, LANE), 1)
        low_lane = lax.broadcasted_iota(jnp.int32, (SUB, LANE), 1)
        steps = []
        for slot in range(terms):
            if slot < 3:
                steps.append((place * tiles + (0, -tiles, tiles)[slot], None, None, None))
            else:
                offset = slots[slot, 1] + 8 * LANE
                turn = lax.rem(offset, LANE)
                first = place * tiles + lax.div(offset, LANE) - 8
                back = lax.rem(LANE - turn, LANE)
                steps.append((first, back, lane < LANE - turn, low_lane < LANE - turn))
        return steps

    def shifted(load, back, keep, width):
        if back is None:
            return [load(t) for t in range(width)]
        rolled = [pltpu.roll(load(t), back, 1) for t in range(width + 1)]
        return [jnp.where(keep, rolled[t], rolled[t + 1]) for t in range(width)]

    def whiten_special(steps):
        acc = [None] * tiles
        for slot, (first, back, _, keep) in enumerate(steps):
            values = shifted(lambda t: special[first + t], back, keep, tiles)
            for t in range(tiles):
                product = values[t] * coef[pl.ds(slot * SUB, SUB), pl.ds(t * LANE, LANE)]
                acc[t] = product if acc[t] is None else acc[t] + product
        return acc

    def whiten_rows(steps, starts, low, width):
        def twice(ref, at_row, t):
            value = ref[pl.ds(at_row, SUB), pl.ds((low + t) * LANE, LANE)]
            return jnp.concatenate([value, value], 0)

        off = [twice(mean_white, 0, t) for t in range(width)]
        acc = [list(off) for _ in starts]
        for slot, (first, back, keep, _) in enumerate(steps):
            weights = [twice(coef, slot * SUB, t) for t in range(width)]
            for r, at_row in enumerate(starts):
                values = shifted(lambda t: raw[first + low + t, pl.ds(at_row, PACK), :], back, keep, width)
                for t in range(width):
                    product = values[t].astype(F32) * weights[t]
                    acc[r][t] = product - acc[r][t] if slot == 0 else acc[r][t] + product
        return acc

    def products():
        block = jnp.concatenate([aw[t] for t in range(tiles)], axis=1)
        return lax.dot_general(
            block, block[:members], (((1,), (1,)), ((), ())), preferred_element_type=F32)

    def whiten_chunk(place, column, at, meanwhile=None):
        coefficients(column, at)
        steps = plan(place)
        pending = []

        def store_oldest():
            for at_row, tile, value in pending.pop(0):
                aw[tile, pl.ds(at_row, PACK), :] = value

        acc = whiten_special(steps)
        row = lax.broadcasted_iota(jnp.int32, (PACK, LANE), 0)
        parts = []
        for t in range(tiles):
            mean_white[:, pl.ds(t * LANE, LANE)] = jnp.broadcast_to(acc[t][1:2], (SUB, LANE))
            wide = jnp.broadcast_to(acc[t][0:1], (PACK, LANE))
            high = wide.astype(BF).astype(F32)
            rest = wide - high
            middle = rest.astype(BF).astype(F32)
            low = rest - middle
            split = jnp.where(row == 0, high, jnp.where(row == 1, middle, jnp.where(row == 2, low, 0.0)))
            parts.append((members, t, split.astype(BF)))
        pending.append(parts)
        scale = math.sqrt(members - 1) * row_factor
        misfit = [acc[t][0:1] * scale for t in range(tiles)]
        width = tiles // 2
        for group in range(members // (TALL * PACK)):
            starts = [(group * TALL + r) * PACK for r in range(TALL)]
            for first in (0, width):
                out = whiten_rows(steps, starts, first, width)
                pending.append([
                    (at_row, first + t, out[r][t].astype(BF))
                    for r, at_row in enumerate(starts) for t in range(width)])
                if len(pending) > LATE:
                    store_oldest()
            if group == 0 and meanwhile is not None:
                meanwhile()
        while pending:
            store_oldest()
        for t in range(tiles):
            row_out[:, pl.ds(at + t * LANE, LANE)] = misfit[t]

    if edge:
        for copy in copies:
            copy.wait()
        for which in range(2):
            near = range(3 * which, 3 * which + 3)
            halo = 5 * which
            for place in near:
                tile_wait(place, members + (PACK if place == halo else 0))
            if which == 1:
                gram[...] += products()
            means = [mean_rows(place) for place in near]
            for t in range(tiles):
                pieces = raw[halo * tiles + t, pl.ds(members, PACK), :].astype(F32)
                obs[:, pl.ds(halo * H + t * LANE, LANE)] = pieces[0:1] + pieces[1:2] + pieces[2:3]
            for place, mean in zip(near, means):
                keep_special(place, mean)
            whiten_chunk(1 + 3 * which, which * (columns - H), which * H)
        out_copies = [
            pltpu.make_async_copy(row_out.at[:, pl.ds(0, H)], misfit_out.at[:, pl.ds(0, H)], sems.at[0]),
            pltpu.make_async_copy(row_out.at[:, pl.ds(H, H)], misfit_out.at[:, pl.ds(columns - H, H)], sems.at[1]),
        ]
    else:
        for copy in copies:
            copy.wait()

        def centre_step(place, carry):
            tile_wait(place, members)
            keep_special(place, mean_rows(place))
            return carry

        lax.fori_loop(0, 3, centre_step, 0)

        def chunk_step(place, carry):
            ahead = jnp.minimum(place + 2, chunks - 1)

            @pl.when(place + 2 < chunks)
            def _():
                tile_wait(ahead, members)

            @pl.when(place + AHEAD - 1 < chunks)
            def _():
                coming = place + AHEAD - 1
                tile_copies(pred_ref, pl.multiple_of(coming * H, H), coming, members)

            added = products()
            mean = mean_rows(ahead)
            column = pl.multiple_of(place * H, H)

            def meanwhile():
                gram[...] += added
                keep_special(ahead, mean)

            whiten_chunk(place, column, column, meanwhile)
            return carry

        lax.fori_loop(1, chunks - 1, chunk_step, 0)
        inside = pl.ds(H, columns - 2 * H)
        out_copies = [pltpu.make_async_copy(row_out.at[:, inside], misfit_out.at[:, inside], sems.at[0])]
    for copy in out_copies:
        copy.start()
    gram[...] += products()

    tail = gram[pl.ds(members, 8), :]
    total = tail[0:1] + tail[1:2] + tail[2:3]
    both = gram[pl.ds(0, members), :]
    down = lax.broadcasted_iota(jnp.int32, (half, half), 0)
    across = lax.broadcasted_iota(jnp.int32, (half, half), 1)

    def tuck(block, piece):
        block = jnp.where((down == 1) & (across == half - 1), piece[:, :1], block)
        return jnp.where((down == 0) & (across > 0), piece, block)

    blocks = (
        tuck(both[:half, :half], total[:, :half]),
        both[half:, :half],
        tuck(both[half:, half:], total[:, half:]),
    )
    for index, block in enumerate(blocks):
        at = pl.ds(index * half, half)
        block = block * (1.0 / obs_total)
        gram_out[:, at] = block + gram_in[:, at] if edge else block
    for copy in out_copies:
        copy.wait()


def local_call(edge, obs_total, offsets, rows_count, predicted, observed, band, *more):
    members, columns = predicted.shape
    terms = band.shape[0]
    rows = members + PACK
    places = 6 if edge else columns // H
    tiles = places * (H // LANE)
    vmem = pl.BlockSpec(memory_space=pltpu.VMEM)
    smem = pl.BlockSpec(memory_space=pltpu.SMEM)
    far = pl.BlockSpec(memory_space=pltpu.HBM)
    in_specs = [smem, smem, far, far, far]
    if edge:
        in_specs += [far, far, vmem, far]
    scratch = [
        pltpu.VMEM((tiles, rows if edge else members, LANE), BF),
        pltpu.VMEM((tiles, SUB, LANE), F32),
        pltpu.VMEM((H // LANE, rows, LANE), BF),
        pltpu.VMEM((SUB * terms, H), F32),
        pltpu.VMEM((SUB, H), F32),
        pltpu.VMEM((rows, members), F32),
        pltpu.VMEM((1, places * H), F32),
        pltpu.VMEM((terms, 2 * H if edge else columns), F32),
        pltpu.VMEM((1, 2 * H if edge else columns), F32),
        pltpu.SMEM((8, 2), jnp.int32),
        pltpu.SemaphoreType.DMA((places + 4,)),
    ]
    work = 2 if edge else places - 2
    return pl.pallas_call(
        functools.partial(local_kernel, edge, columns, obs_total),
        out_shape=(
            jax.ShapeDtypeStruct((members // 2, members // 2 * 3), F32),
            jax.ShapeDtypeStruct((1, columns), F32),
        ),
        in_specs=in_specs,
        out_specs=[vmem, far],
        scratch_shapes=scratch,
        input_output_aliases={8: 1} if edge else {},
        compiler_params=pltpu.CompilerParams(vmem_limit_bytes=VMEM),
        cost_estimate=pl.CostEstimate(
            flops=2 * rows * members * H * work * 2, bytes_accessed=members * H * places * 2, transcendentals=0),
        name="edges" if edge else "inner",
    )(offsets, rows_count, predicted, observed, band, *more)


def update_kernel(sum_ref, params_ref, out_ref, work):
    members = params_ref.shape[1]
    highest = lax.Precision.HIGHEST
    row_index = lax.broadcasted_iota(jnp.int32, (members, members), 0)
    col_index = lax.broadcasted_iota(jnp.int32, (members, members), 1)
    identity = jnp.where(row_index == col_index, 1.0, 0.0).astype(F32)
    half = members // 2
    eye_half = identity[:half, :half]
    lower = row_index[:half, :half] >= col_index[:half, :half]

    def mirrored(block):
        return jnp.where(lower, block, block.T) + eye_half

    def tucked(block):
        first = lax.broadcasted_iota(jnp.int32, (1, half), 1) == 0
        return jnp.where(first, block[1:2, half - 1:half], block[0:1, :])

    blocks = [sum_ref[:, pl.ds(index * half, half)] for index in range(3)]
    work[pl.ds(0, half), pl.ds(0, half)] = mirrored(blocks[0])
    work[pl.ds(0, half), pl.ds(half, half)] = blocks[1].T
    work[pl.ds(half, half), pl.ds(0, half)] = blocks[1]
    work[pl.ds(half, half), pl.ds(half, half)] = mirrored(blocks[2])
    projection = jnp.concatenate([tucked(blocks[0]), tucked(blocks[2])], 1)
    work[:, pl.ds(members, members)] = identity
    panels = BLOCK // PANEL
    sub = lax.broadcasted_iota(jnp.int32, (PANEL, LANE), 0)
    eye = identity[:BLOCK, :BLOCK]

    def across(tile, column):
        return jnp.broadcast_to(tile[:, column:column + 1], (PANEL, LANE))

    def down(tile, row):
        return jnp.broadcast_to(tile[row:row + 1, :], (PANEL, LANE))

    for block in range(members // BLOCK):
        r0 = block * BLOCK
        start = jnp.concatenate([work[pl.ds(r0, BLOCK), pl.ds(r0, BLOCK)], eye], axis=1)
        tiles = [start[PANEL * t:PANEL * (t + 1)] for t in range(panels)]
        done = []
        for p in range(panels):
            c0 = PANEL * p
            tile = tiles[p]
            upper = tile
            full = tile
            cols = [across(tile, c0 + j) for j in range(PANEL)]
            scale = jnp.zeros((PANEL, LANE), F32)
            for k in range(0, PANEL, 2):
                left, right = cols[k], cols[k + 1]
                a, b, c = down(left, k), down(left, k + 1), down(right, k + 1)
                det = a * c - b * b
                inverse = 1.0 / det
                ratio = b / a
                scale = jnp.where(sub == k, a, jnp.where(sub == k + 1, c - b * ratio, scale))
                from_left = c * left - b * right
                from_right = a * right - b * left

                def change_of(values):
                    x, y = down(values, k), down(values, k + 1)
                    return x, y, (from_left * x + from_right * y) * inverse

                def clear(values):
                    x, y, change = change_of(values)
                    own = jnp.where(sub == k, c * x - b * y, a * y - b * x) * inverse
                    return jnp.where((sub == k) | (sub == k + 1), own, values - change)

                x, y, change = change_of(upper)
                upper = upper - jnp.where(sub > k + 1, change, jnp.where(sub == k + 1, ratio * x, 0.0))
                full = clear(full)
                for j in range(k + 2, PANEL):
                    cols[j] = clear(cols[j])
            done.append(upper * lax.rsqrt(scale))
            rows_of = [down(full, k) for k in range(PANEL)]
            for t in range(p + 1, panels):
                tile_t = tiles[t]
                change = [across(tile_t, c0 + k) * rows_of[k] for k in range(PANEL)]
                while len(change) > 1:
                    change = [a + b for a, b in zip(change[::2], change[1::2])]
                tiles[t] = tile_t - change[0]
        lower_inverse = jnp.concatenate(done, axis=0)[:, BLOCK:2 * BLOCK]
        begin = (r0 + BLOCK) // LANE * LANE
        end = members + -(-(r0 + BLOCK) // LANE) * LANE
        wide = pl.ds(begin, end - begin)
        solved = jnp.dot(lower_inverse, work[pl.ds(r0, BLOCK), wide], precision=highest, preferred_element_type=F32)
        work[pl.ds(r0, BLOCK), wide] = solved
        if r0 + BLOCK < members:
            rest = members - r0 - BLOCK
            factor = solved[:, r0 + BLOCK - begin:members - begin]
            work[pl.ds(r0 + BLOCK, rest), wide] = work[pl.ds(r0 + BLOCK, rest), wide] - lax.dot_general(
                factor, solved, (((0,), (0,)), ((), ())), precision=highest, preferred_element_type=F32)

    inverse = jnp.where(row_index >= col_index, work[:, pl.ds(members, members)], 0.0)
    solved = jnp.sum(inverse * projection, axis=1, keepdims=True)
    weights = jnp.sum(inverse * solved, axis=0, keepdims=True)
    turned = inverse + weights
    turned = turned - jnp.mean(turned, axis=1, keepdims=True) + 1.0 / members
    high = turned.astype(BF)
    rest = turned - high.astype(F32)
    middle = rest.astype(BF)
    low = (rest - middle.astype(F32)).astype(BF)
    def times(part):
        return lax.dot_general(params_ref[...], part, (((1,), (1,)), ((), ())), preferred_element_type=F32)

    out_ref[...] = times(high) + (times(middle) + times(low))


def update(total, params):
    members = params.shape[1]
    vmem = pl.BlockSpec(memory_space=pltpu.VMEM)
    return pl.pallas_call(
        update_kernel,
        out_shape=jax.ShapeDtypeStruct(params.shape, F32),
        in_specs=[vmem, vmem],
        out_specs=vmem,
        scratch_shapes=[pltpu.VMEM((members, 2 * members), F32)],
        compiler_params=pltpu.CompilerParams(vmem_limit_bytes=VMEM // 4),
        name="update",
    )(total, params)


def halo_kernel(columns, pred_ref, obs_ref, first_ref, last_ref, obs, sems):
    members = pred_ref.shape[0]
    copies = []
    for side, (out, at) in enumerate(((first_ref, 0), (last_ref, columns - H))):
        copies.append(pltpu.make_async_copy(
            pred_ref.at[:, pl.ds(at, H)], out.at[pl.ds(0, members), :], sems.at[side]))
        copies.append(pltpu.make_async_copy(
            obs_ref.at[:, pl.ds(at, H)], obs.at[:, pl.ds(side * H, H)], sems.at[2 + side]))
    for copy in copies:
        copy.start()
    for copy in copies[1::2]:
        copy.wait()
    row = lax.broadcasted_iota(jnp.int32, (PACK, H), 0)
    for side, out in enumerate((first_ref, last_ref)):
        wide = jnp.broadcast_to(obs[:, pl.ds(side * H, H)], (PACK, H))
        high = wide.astype(BF).astype(F32)
        rest = wide - high
        middle = rest.astype(BF).astype(F32)
        low = rest - middle
        split = jnp.where(row == 0, high, jnp.where(row == 1, middle, jnp.where(row == 2, low, 0.0)))
        out[pl.ds(members, PACK), :] = split.astype(BF)
    for copy in copies[0::2]:
        copy.wait()


def halo_blocks(predicted, observed):
    members, columns = predicted.shape
    far = pl.BlockSpec(memory_space=pltpu.HBM)
    near = pl.BlockSpec(memory_space=pltpu.VMEM)
    block = jax.ShapeDtypeStruct((members + PACK, H), BF)
    return pl.pallas_call(
        functools.partial(halo_kernel, columns),
        out_shape=(block, block),
        in_specs=[far, far],
        out_specs=[near, near],
        scratch_shapes=[pltpu.VMEM((1, 2 * H), F32), pltpu.SemaphoreType.DMA((4,))],
        compiler_params=pltpu.CompilerParams(vmem_limit_bytes=VMEM),
        name="halos",
    )(predicted, observed)


def sum_over(values, axes):
    shards = lax.axis_size(axes)
    rows, width = values.shape
    parts = lax.all_to_all(values, axes, 0, 0, tiled=True)
    own = jnp.sum(parts.reshape(shards, rows // shards, width), axis=0)
    copies = jnp.broadcast_to(own[None], (shards, rows // shards, width)).reshape(rows, width)
    return lax.all_to_all(copies, axes, 0, 0, tiled=True)


def body(predicted, observed, band, offsets, rows_count, params):
    columns = predicted.shape[1]
    axes = ("obs", "par")
    shards = lax.axis_size(axes)
    obs_total = columns * shards
    up = [(i, i + 1) for i in range(shards - 1)]
    down = [(j, i) for i, j in up]
    obs_row = observed[None, :]
    first, last = halo_blocks(predicted, obs_row)
    left = lax.ppermute(last, axes, up)
    right = lax.ppermute(first, axes, down)
    gram, misfit = local_call(False, obs_total, offsets, rows_count, predicted, obs_row, band)
    gram, misfit = local_call(
        True, obs_total, offsets, rows_count, predicted, obs_row, band, left, right, gram, misfit)
    total = sum_over(gram, axes)
    return (update(total, params), misfit[0])


def solution(mesh):
    in_specs = (
        P(None, ("grp", "obs", "par")),
        P(("grp", "obs", "par")),
        P(None, ("grp", "obs", "par")),
        P(),
        P(("grp", "obs", "par")),
        P(("grp", "obs", "par"), None),
    )
    out_specs = (P(("grp", "obs", "par"), None), P(("grp", "obs", "par")))
    return jax.shard_map(body, mesh=mesh, in_specs=in_specs, out_specs=out_specs, check_vma=False)
```

```python
import functools
import math

import jax
import jax.numpy as jnp
from jax import lax
from jax.experimental import pallas as pl
from jax.experimental.pallas import tpu as pltpu
from jax.sharding import PartitionSpec as P

H = 1024
LANE = 128
SUB = 8
PACK = 16
TALL = 2
LATE = 2
AHEAD = 5
BLOCK = 64
PANEL = 8
VMEM = 64 * 2**20
BF = jnp.bfloat16
F32 = jnp.float32


def local_kernel(edge, columns, obs_total, *refs):
    if edge:
        (off_ref, count_ref, pred_ref, obs_ref, band_ref, left_ref, right_ref, gram_before, misfit_in,
         gram_out, misfit_out, raw, special, aw, coef, mean_white, gram, obs, band, row_out, slots,
         sems, gram_in) = refs
    else:
        (off_ref, count_ref, pred_ref, obs_ref, band_ref,
         gram_out, misfit_out, raw, special, aw, coef, mean_white, gram, obs, band, row_out, slots,
         sems) = refs
    members = pred_ref.shape[0]
    terms = band_ref.shape[0]
    chunks = columns // H
    tiles = H // LANE
    half = members // 2
    row_factor = 1.0 / math.sqrt(obs_total)

    def tile_copies(source, column, place, height):
        for t in range(tiles):
            pltpu.make_async_copy(
                source.at[:, pl.ds(column + t * LANE, LANE)],
                raw.at[place * tiles + t, pl.ds(0, height), :], sems.at[place]).start()

    def tile_wait(place, height):
        whole = raw.at[pl.ds(place * tiles, tiles), pl.ds(0, height), :]
        pltpu.make_async_copy(whole, whole, sems.at[place]).wait()

    if edge:
        copies = []
        for which in range(2):
            there = which * (columns - 2 * H)
            copies.append(pltpu.make_async_copy(
                obs_ref.at[:, pl.ds(there, 2 * H)], obs.at[:, pl.ds((1 + which * 2) * H, 2 * H)], sems.at[6 + which]))
            there = which * (columns - H)
            copies.append(pltpu.make_async_copy(
                band_ref.at[:, pl.ds(there, H)], band.at[:, pl.ds(which * H, H)], sems.at[8 + which]))
    else:
        copies = [
            pltpu.make_async_copy(obs_ref, obs, sems.at[chunks]),
            pltpu.make_async_copy(band_ref, band, sems.at[chunks + 1]),
        ]
    for copy in copies:
        copy.start()
    if edge:
        gram_copy = pltpu.make_async_copy(gram_before, gram_in, sems.at[10])
        gram_copy.start()
        tile_copies(left_ref, 0, 0, members + PACK)
        for place, chunk in ((1, 0), (2, 1), (3, chunks - 2), (4, chunks - 1)):
            tile_copies(pred_ref, chunk * H, place, members)
        tile_copies(right_ref, 0, 5, members + PACK)
    else:
        for place in range(AHEAD):
            tile_copies(pred_ref, place * H, place, members)

    slots[0, 0] = 0
    slots[0, 1] = 0
    free = jnp.int32(3)
    for term in range(1, terms):
        offset = off_ref[term]
        whole = (offset == H) | (offset == -H)
        place = jnp.where(offset == -H, 1, jnp.where(offset == H, 2, free))
        place = jnp.minimum(place, terms - 1)
        slots[place, 0] = jnp.int32(term)
        slots[place, 1] = offset
        free = free + jnp.where(whole, 0, 1)

    gram[...] = jnp.zeros_like(gram)
    aw[...] = jnp.zeros_like(aw)

    def mean_rows(place):
        block = jnp.concatenate(
            [raw[place * tiles + t, pl.ds(0, members), :] for t in range(tiles)], axis=1)
        return jnp.dot(jnp.full((PACK, members), 1.0 / members, BF), block, preferred_element_type=F32)[:SUB]

    def keep_special(place, mean):
        seen = obs[:, pl.ds(pl.multiple_of(place * H, H), H)]
        innovation = (seen - mean).astype(BF).astype(F32)
        value = jnp.where(lax.broadcasted_iota(jnp.int32, (SUB, H), 0) == 0, innovation, mean)
        for t in range(tiles):
            special[place * tiles + t] = value[:, t * LANE:(t + 1) * LANE]

    def coefficients(column, at):
        index = column + lax.broadcasted_iota(jnp.int32, (1, H), 1)
        strained = (index < count_ref[0]) | (index >= columns - H)
        strain = jnp.where(strained, 1.0, 0.0)
        for slot in range(terms):
            term = slots[slot, 0]
            row = band[pl.ds(term, 1), pl.ds(at, H)]
            if slot > 0:
                row = row * strain
            coef[pl.ds(slot * SUB, SUB), :] = jnp.broadcast_to(row, (SUB, H))

    def plan(place):
        lane = lax.broadcasted_iota(jnp.int32, (PACK, LANE), 1)
        low_lane = lax.broadcasted_iota(jnp.int32, (SUB, LANE), 1)
        steps = []
        for slot in range(terms):
            if slot < 3:
                steps.append((place * tiles + (0, -tiles, tiles)[slot], None, None, None))
            else:
                offset = slots[slot, 1] + 8 * LANE
                turn = lax.rem(offset, LANE)
                first = place * tiles + lax.div(offset, LANE) - 8
                back = lax.rem(LANE - turn, LANE)
                steps.append((first, back, lane < LANE - turn, low_lane < LANE - turn))
        return steps

    def shifted(load, back, keep, width):
        if back is None:
            return [load(t) for t in range(width)]
        rolled = [pltpu.roll(load(t), back, 1) for t in range(width + 1)]
        return [jnp.where(keep, rolled[t], rolled[t + 1]) for t in range(width)]

    def whiten_special(steps):
        acc = [None] * tiles
        for slot, (first, back, _, keep) in enumerate(steps):
            values = shifted(lambda t: special[first + t], back, keep, tiles)
            for t in range(tiles):
                product = values[t] * coef[pl.ds(slot * SUB, SUB), pl.ds(t * LANE, LANE)]
                acc[t] = product if acc[t] is None else acc[t] + product
        return acc

    def whiten_rows(steps, starts, low, width):
        def twice(ref, at_row, t):
            value = ref[pl.ds(at_row, SUB), pl.ds((low + t) * LANE, LANE)]
            return jnp.concatenate([value, value], 0)

        off = [twice(mean_white, 0, t) for t in range(width)]
        acc = [list(off) for _ in starts]
        for slot, (first, back, keep, _) in enumerate(steps):
            weights = [twice(coef, slot * SUB, t) for t in range(width)]
            for r, at_row in enumerate(starts):
                values = shifted(lambda t: raw[first + low + t, pl.ds(at_row, PACK), :], back, keep, width)
                for t in range(width):
                    product = values[t].astype(F32) * weights[t]
                    acc[r][t] = product - acc[r][t] if slot == 0 else acc[r][t] + product
        return acc

    def products():
        block = jnp.concatenate([aw[t] for t in range(tiles)], axis=1)
        return lax.dot_general(
            block, block[:members], (((1,), (1,)), ((), ())), preferred_element_type=F32)

    def whiten_chunk(place, column, at, meanwhile=None):
        coefficients(column, at)
        steps = plan(place)
        pending = []

        def store_oldest():
            for at_row, tile, value in pending.pop(0):
                aw[tile, pl.ds(at_row, PACK), :] = value

        acc = whiten_special(steps)
        row = lax.broadcasted_iota(jnp.int32, (PACK, LANE), 0)
        parts = []
        for t in range(tiles):
            mean_white[:, pl.ds(t * LANE, LANE)] = jnp.broadcast_to(acc[t][1:2], (SUB, LANE))
            wide = jnp.broadcast_to(acc[t][0:1], (PACK, LANE))
            high = wide.astype(BF).astype(F32)
            rest = wide - high
            middle = rest.astype(BF).astype(F32)
            low = rest - middle
            split = jnp.where(row == 0, high, jnp.where(row == 1, middle, jnp.where(row == 2, low, 0.0)))
            parts.append((members, t, split.astype(BF)))
        pending.append(parts)
        scale = math.sqrt(members - 1) * row_factor
        misfit = [acc[t][0:1] * scale for t in range(tiles)]
        width = tiles // 2
        for group in range(members // (TALL * PACK)):
            starts = [(group * TALL + r) * PACK for r in range(TALL)]
            for first in (0, width):
                out = whiten_rows(steps, starts, first, width)
                pending.append([
                    (at_row, first + t, out[r][t].astype(BF))
                    for r, at_row in enumerate(starts) for t in range(width)])
                if len(pending) > LATE:
                    store_oldest()
            if group == 0 and meanwhile is not None:
                meanwhile()
        while pending:
            store_oldest()
        for t in range(tiles):
            row_out[:, pl.ds(at + t * LANE, LANE)] = misfit[t]

    if edge:
        for copy in copies:
            copy.wait()
        for which in range(2):
            near = range(3 * which, 3 * which + 3)
            halo = 5 * which
            for place in near:
                tile_wait(place, members + (PACK if place == halo else 0))
            if which == 1:
                gram[...] += products()
            means = [mean_rows(place) for place in near]
            for t in range(tiles):
                pieces = raw[halo * tiles + t, pl.ds(members, PACK), :].astype(F32)
                obs[:, pl.ds(halo * H + t * LANE, LANE)] = pieces[0:1] + pieces[1:2] + pieces[2:3]
            for place, mean in zip(near, means):
                keep_special(place, mean)
            whiten_chunk(1 + 3 * which, which * (columns - H), which * H)
        out_copies = [
            pltpu.make_async_copy(row_out.at[:, pl.ds(0, H)], misfit_out.at[:, pl.ds(0, H)], sems.at[0]),
            pltpu.make_async_copy(row_out.at[:, pl.ds(H, H)], misfit_out.at[:, pl.ds(columns - H, H)], sems.at[1]),
        ]
    else:
        for copy in copies:
            copy.wait()

        def centre_step(place, carry):
            tile_wait(place, members)
            keep_special(place, mean_rows(place))
            return carry

        lax.fori_loop(0, 3, centre_step, 0)

        def chunk_step(place, carry):
            ahead = jnp.minimum(place + 2, chunks - 1)

            @pl.when(place + 2 < chunks)
            def _():
                tile_wait(ahead, members)

            @pl.when(place + AHEAD - 1 < chunks)
            def _():
                coming = place + AHEAD - 1
                tile_copies(pred_ref, pl.multiple_of(coming * H, H), coming, members)

            added = products()
            mean = mean_rows(ahead)
            column = pl.multiple_of(place * H, H)

            def meanwhile():
                gram[...] += added
                keep_special(ahead, mean)

            whiten_chunk(place, column, column, meanwhile)
            return carry

        lax.fori_loop(1, chunks - 1, chunk_step, 0)
        inside = pl.ds(H, columns - 2 * H)
        out_copies = [pltpu.make_async_copy(row_out.at[:, inside], misfit_out.at[:, inside], sems.at[0])]
    for copy in out_copies:
        copy.start()
    gram[...] += products()

    if edge:
        gram_copy.wait()
    tail = gram[pl.ds(members, 8), :]
    total = tail[0:1] + tail[1:2] + tail[2:3]
    both = gram[pl.ds(0, members), :]
    down = lax.broadcasted_iota(jnp.int32, (half, half), 0)
    across = lax.broadcasted_iota(jnp.int32, (half, half), 1)

    def tuck(block, piece):
        block = jnp.where((down == 1) & (across == half - 1), piece[:, :1], block)
        return jnp.where((down == 0) & (across > 0), piece, block)

    blocks = (
        tuck(both[:half, :half], total[:, :half]),
        both[half:, :half],
        tuck(both[half:, half:], total[:, half:]),
    )
    for index, block in enumerate(blocks):
        at = pl.ds(index * half, half)
        block = block * (1.0 / obs_total)
        gram_out[:, at] = block + gram_in[:, at] if edge else block
    for copy in out_copies:
        copy.wait()


def local_call(edge, obs_total, offsets, rows_count, predicted, observed, band, *more):
    members, columns = predicted.shape
    terms = band.shape[0]
    rows = members + PACK
    places = 6 if edge else columns // H
    tiles = places * (H // LANE)
    vmem = pl.BlockSpec(memory_space=pltpu.VMEM)
    smem = pl.BlockSpec(memory_space=pltpu.SMEM)
    far = pl.BlockSpec(memory_space=pltpu.HBM)
    in_specs = [smem, smem, far, far, far]
    if edge:
        in_specs += [far, far, far, far]
    scratch = [
        pltpu.VMEM((tiles, rows if edge else members, LANE), BF),
        pltpu.VMEM((tiles, SUB, LANE), F32),
        pltpu.VMEM((H // LANE, rows, LANE), BF),
        pltpu.VMEM((SUB * terms, H), F32),
        pltpu.VMEM((SUB, H), F32),
        pltpu.VMEM((rows, members), F32),
        pltpu.VMEM((1, places * H), F32),
        pltpu.VMEM((terms, 2 * H if edge else columns), F32),
        pltpu.VMEM((1, 2 * H if edge else columns), F32),
        pltpu.SMEM((8, 2), jnp.int32),
        pltpu.SemaphoreType.DMA((places + 5,)),
    ]
    if edge:
        scratch.append(pltpu.VMEM((members // 2, members // 2 * 3), F32))
    work = 2 if edge else places - 2
    return pl.pallas_call(
        functools.partial(local_kernel, edge, columns, obs_total),
        out_shape=(
            jax.ShapeDtypeStruct((members // 2, members // 2 * 3), F32),
            jax.ShapeDtypeStruct((1, columns), F32),
        ),
        in_specs=in_specs,
        out_specs=[vmem, far],
        scratch_shapes=scratch,
        input_output_aliases={8: 1} if edge else {},
        compiler_params=pltpu.CompilerParams(vmem_limit_bytes=VMEM),
        cost_estimate=pl.CostEstimate(
            flops=2 * rows * members * H * work * 2, bytes_accessed=members * H * places * 2, transcendentals=0),
        name="edges" if edge else "inner",
    )(offsets, rows_count, predicted, observed, band, *more)


def update_kernel(sum_ref, params_ref, out_ref, work):
    members = params_ref.shape[1]
    highest = lax.Precision.HIGHEST
    row_index = lax.broadcasted_iota(jnp.int32, (members, members), 0)
    col_index = lax.broadcasted_iota(jnp.int32, (members, members), 1)
    identity = jnp.where(row_index == col_index, 1.0, 0.0).astype(F32)
    half = members // 2
    eye_half = identity[:half, :half]
    lower = row_index[:half, :half] >= col_index[:half, :half]

    def mirrored(block):
        return jnp.where(lower, block, block.T) + eye_half

    def tucked(block):
        first = lax.broadcasted_iota(jnp.int32, (1, half), 1) == 0
        return jnp.where(first, block[1:2, half - 1:half], block[0:1, :])

    blocks = [sum_ref[:, pl.ds(index * half, half)] for index in range(3)]
    work[pl.ds(0, half), pl.ds(0, half)] = mirrored(blocks[0])
    work[pl.ds(0, half), pl.ds(half, half)] = blocks[1].T
    work[pl.ds(half, half), pl.ds(0, half)] = blocks[1]
    work[pl.ds(half, half), pl.ds(half, half)] = mirrored(blocks[2])
    projection = jnp.concatenate([tucked(blocks[0]), tucked(blocks[2])], 1)
    work[:, pl.ds(members, members)] = identity
    panels = BLOCK // PANEL
    sub = lax.broadcasted_iota(jnp.int32, (PANEL, LANE), 0)
    eye = identity[:BLOCK, :BLOCK]

    def reciprocal(value):
        guess = pl.reciprocal(value, approx=True)
        for _ in range(2):
            guess = guess * (2.0 - value * guess)
        return guess

    def across(tile, column):
        return jnp.broadcast_to(tile[:, column:column + 1], (PANEL, LANE))

    def down(tile, row):
        return jnp.broadcast_to(tile[row:row + 1, :], (PANEL, LANE))

    for block in range(members // BLOCK):
        r0 = block * BLOCK
        start = jnp.concatenate([work[pl.ds(r0, BLOCK), pl.ds(r0, BLOCK)], eye], axis=1)
        tiles = [start[PANEL * t:PANEL * (t + 1)] for t in range(panels)]
        done = []
        for p in range(panels):
            c0 = PANEL * p
            tile = tiles[p]
            upper = tile
            full = tile
            cols = [across(tile, c0 + j) for j in range(PANEL)]
            scale = jnp.zeros((PANEL, LANE), F32)
            for k in range(0, PANEL, 2):
                left, right = cols[k], cols[k + 1]
                a, b, c = down(left, k), down(left, k + 1), down(right, k + 1)
                det = a * c - b * b
                inverse = reciprocal(det)
                ratio = b * reciprocal(a)
                scale = jnp.where(sub == k, a, jnp.where(sub == k + 1, c - b * ratio, scale))
                from_left = c * left - b * right
                from_right = a * right - b * left

                def change_of(values):
                    x, y = down(values, k), down(values, k + 1)
                    return x, y, (from_left * x + from_right * y) * inverse

                def clear(values):
                    x, y, change = change_of(values)
                    own = jnp.where(sub == k, c * x - b * y, a * y - b * x) * inverse
                    return jnp.where((sub == k) | (sub == k + 1), own, values - change)

                x, y, change = change_of(upper)
                upper = upper - jnp.where(sub > k + 1, change, jnp.where(sub == k + 1, ratio * x, 0.0))
                full = clear(full)
                for j in range(k + 2, PANEL):
                    cols[j] = clear(cols[j])
            done.append(upper * lax.rsqrt(scale))
            rows_of = [down(full, k) for k in range(PANEL)]
            for t in range(p + 1, panels):
                tile_t = tiles[t]
                change = [across(tile_t, c0 + k) * rows_of[k] for k in range(PANEL)]
                while len(change) > 1:
                    change = [a + b for a, b in zip(change[::2], change[1::2])]
                tiles[t] = tile_t - change[0]
        lower_inverse = jnp.concatenate(done, axis=0)[:, BLOCK:2 * BLOCK]
        begin = (r0 + BLOCK) // LANE * LANE
        end = members + -(-(r0 + BLOCK) // LANE) * LANE
        wide = pl.ds(begin, end - begin)
        solved = jnp.dot(lower_inverse, work[pl.ds(r0, BLOCK), wide], precision=highest, preferred_element_type=F32)
        work[pl.ds(r0, BLOCK), wide] = solved
        if r0 + BLOCK < members:
            rest = members - r0 - BLOCK
            factor = solved[:, r0 + BLOCK - begin:members - begin]
            work[pl.ds(r0 + BLOCK, rest), wide] = work[pl.ds(r0 + BLOCK, rest), wide] - lax.dot_general(
                factor, solved, (((0,), (0,)), ((), ())), precision=highest, preferred_element_type=F32)

    inverse = jnp.where(row_index >= col_index, work[:, pl.ds(members, members)], 0.0)
    solved = jnp.sum(inverse * projection, axis=1, keepdims=True)
    weights = jnp.sum(inverse * solved, axis=0, keepdims=True)
    turned = inverse + weights
    turned = turned - jnp.mean(turned, axis=1, keepdims=True) + 1.0 / members
    high = turned.astype(BF)
    rest = turned - high.astype(F32)
    middle = rest.astype(BF)
    low = (rest - middle.astype(F32)).astype(BF)
    def times(part):
        return lax.dot_general(params_ref[...], part, (((1,), (1,)), ((), ())), preferred_element_type=F32)

    out_ref[...] = times(high) + (times(middle) + times(low))


def update(total, params):
    members = params.shape[1]
    vmem = pl.BlockSpec(memory_space=pltpu.VMEM)
    return pl.pallas_call(
        update_kernel,
        out_shape=jax.ShapeDtypeStruct(params.shape, F32),
        in_specs=[vmem, vmem],
        out_specs=vmem,
        scratch_shapes=[pltpu.VMEM((members, 2 * members), F32)],
        compiler_params=pltpu.CompilerParams(vmem_limit_bytes=VMEM // 4),
        name="update",
    )(total, params)


def halo_kernel(columns, pred_ref, obs_ref, first_ref, last_ref, obs, sems):
    members = pred_ref.shape[0]
    copies = []
    for side, (out, at) in enumerate(((first_ref, 0), (last_ref, columns - H))):
        copies.append(pltpu.make_async_copy(
            pred_ref.at[:, pl.ds(at, H)], out.at[pl.ds(0, members), :], sems.at[side]))
        copies.append(pltpu.make_async_copy(
            obs_ref.at[:, pl.ds(at, H)], obs.at[:, pl.ds(side * H, H)], sems.at[2 + side]))
    for copy in copies:
        copy.start()
    for copy in copies[1::2]:
        copy.wait()
    row = lax.broadcasted_iota(jnp.int32, (PACK, H), 0)
    for side, out in enumerate((first_ref, last_ref)):
        wide = jnp.broadcast_to(obs[:, pl.ds(side * H, H)], (PACK, H))
        high = wide.astype(BF).astype(F32)
        rest = wide - high
        middle = rest.astype(BF).astype(F32)
        low = rest - middle
        split = jnp.where(row == 0, high, jnp.where(row == 1, middle, jnp.where(row == 2, low, 0.0)))
        out[pl.ds(members, PACK), :] = split.astype(BF)
    for copy in copies[0::2]:
        copy.wait()


def halo_blocks(predicted, observed):
    members, columns = predicted.shape
    far = pl.BlockSpec(memory_space=pltpu.HBM)
    near = pl.BlockSpec(memory_space=pltpu.VMEM)
    block = jax.ShapeDtypeStruct((members + PACK, H), BF)
    return pl.pallas_call(
        functools.partial(halo_kernel, columns),
        out_shape=(block, block),
        in_specs=[far, far],
        out_specs=[near, near],
        scratch_shapes=[pltpu.VMEM((1, 2 * H), F32), pltpu.SemaphoreType.DMA((4,))],
        compiler_params=pltpu.CompilerParams(vmem_limit_bytes=VMEM),
        name="halos",
    )(predicted, observed)


def sum_over(values, axes):
    shards = lax.axis_size(axes)
    rows, width = values.shape
    parts = lax.all_to_all(values, axes, 0, 0, tiled=True)
    own = jnp.sum(parts.reshape(shards, rows // shards, width), axis=0)
    copies = jnp.broadcast_to(own[None], (shards, rows // shards, width)).reshape(rows, width)
    return lax.all_to_all(copies, axes, 0, 0, tiled=True)


def body(predicted, observed, band, offsets, rows_count, params):
    columns = predicted.shape[1]
    axes = ("obs", "par")
    shards = lax.axis_size(axes)
    obs_total = columns * shards
    up = [(i, i + 1) for i in range(shards - 1)]
    down = [(j, i) for i, j in up]
    obs_row = observed[None, :]
    first, last = halo_blocks(predicted, obs_row)
    left = lax.ppermute(last, axes, up)
    right = lax.ppermute(first, axes, down)
    gram, misfit = local_call(False, obs_total, offsets, rows_count, predicted, obs_row, band)
    gram, misfit = local_call(
        True, obs_total, offsets, rows_count, predicted, obs_row, band, left, right, gram, misfit)
    total = sum_over(gram, axes)
    return (update(total, params), misfit[0])


def solution(mesh):
    in_specs = (
        P(None, ("grp", "obs", "par")),
        P(("grp", "obs", "par")),
        P(None, ("grp", "obs", "par")),
        P(),
        P(("grp", "obs", "par")),
        P(("grp", "obs", "par"), None),
    )
    out_specs = (P(("grp", "obs", "par"), None), P(("grp", "obs", "par")))
    return jax.shard_map(body, mesh=mesh, in_specs=in_specs, out_specs=out_specs, check_vma=False)
```

```python
import functools
import math

import jax
import jax.numpy as jnp
from jax import lax
from jax.experimental import pallas as pl
from jax.experimental.pallas import tpu as pltpu
from jax.sharding import PartitionSpec as P

H = 1024
LANE = 128
SUB = 8
PACK = 16
TALL = 2
LATE = 2
AHEAD = 5
BLOCK = 64
PANEL = 8
VMEM = 64 * 2**20
BF = jnp.bfloat16
F32 = jnp.float32


def local_kernel(edge, columns, obs_total, *refs):
    if edge:
        (off_ref, count_ref, pred_ref, obs_ref, band_ref, left_ref, right_ref, gram_before, misfit_in,
         gram_out, misfit_out, raw, special, aw, coef, mean_white, gram, obs, band, row_out, slots,
         sems, gram_in) = refs
    else:
        (off_ref, count_ref, pred_ref, obs_ref, band_ref,
         gram_out, misfit_out, raw, special, aw, coef, mean_white, gram, obs, band, row_out, slots,
         sems) = refs
    members = pred_ref.shape[0]
    terms = band_ref.shape[0]
    chunks = columns // H
    tiles = H // LANE
    half = members // 2
    row_factor = 1.0 / math.sqrt(obs_total)

    def tile_copies(source, column, place, height):
        for t in range(tiles):
            pltpu.make_async_copy(
                source.at[:, pl.ds(column + t * LANE, LANE)],
                raw.at[place * tiles + t, pl.ds(0, height), :], sems.at[place]).start()

    def tile_wait(place, height):
        whole = raw.at[pl.ds(place * tiles, tiles), pl.ds(0, height), :]
        pltpu.make_async_copy(whole, whole, sems.at[place]).wait()

    if edge:
        copies = []
        for which in range(2):
            there = which * (columns - 2 * H)
            copies.append(pltpu.make_async_copy(
                obs_ref.at[:, pl.ds(there, 2 * H)], obs.at[:, pl.ds((1 + which * 2) * H, 2 * H)], sems.at[6 + which]))
            there = which * (columns - H)
            copies.append(pltpu.make_async_copy(
                band_ref.at[:, pl.ds(there, H)], band.at[:, pl.ds(which * H, H)], sems.at[8 + which]))
    else:
        copies = [
            pltpu.make_async_copy(obs_ref, obs, sems.at[chunks]),
            pltpu.make_async_copy(band_ref, band, sems.at[chunks + 1]),
        ]
    for copy in copies:
        copy.start()
    if edge:
        gram_copy = pltpu.make_async_copy(gram_before, gram_in, sems.at[10])
        gram_copy.start()
        tile_copies(left_ref, 0, 0, members + PACK)
        for place, chunk in ((1, 0), (2, 1), (3, chunks - 2), (4, chunks - 1)):
            tile_copies(pred_ref, chunk * H, place, members)
        tile_copies(right_ref, 0, 5, members + PACK)
    else:
        for place in range(AHEAD):
            tile_copies(pred_ref, place * H, place, members)

    slots[0, 0] = 0
    slots[0, 1] = 0
    free = jnp.int32(3)
    for term in range(1, terms):
        offset = off_ref[term]
        whole = (offset == H) | (offset == -H)
        place = jnp.where(offset == -H, 1, jnp.where(offset == H, 2, free))
        place = jnp.minimum(place, terms - 1)
        slots[place, 0] = jnp.int32(term)
        slots[place, 1] = offset
        free = free + jnp.where(whole, 0, 1)

    gram[...] = jnp.zeros_like(gram)
    aw[...] = jnp.zeros_like(aw)

    def mean_rows(place):
        block = jnp.concatenate(
            [raw[place * tiles + t, pl.ds(0, members), :] for t in range(tiles)], axis=1)
        return jnp.dot(jnp.full((PACK, members), 1.0 / members, BF), block, preferred_element_type=F32)[:SUB]

    def keep_special(place, mean):
        seen = obs[:, pl.ds(pl.multiple_of(place * H, H), H)]
        innovation = (seen - mean).astype(BF).astype(F32)
        value = jnp.where(lax.broadcasted_iota(jnp.int32, (SUB, H), 0) == 0, innovation, mean)
        for t in range(tiles):
            special[place * tiles + t] = value[:, t * LANE:(t + 1) * LANE]

    def coefficients(column, at):
        index = column + lax.broadcasted_iota(jnp.int32, (1, H), 1)
        strained = (index < count_ref[0]) | (index >= columns - H)
        strain = jnp.where(strained, 1.0, 0.0)
        for slot in range(terms):
            term = slots[slot, 0]
            row = band[pl.ds(term, 1), pl.ds(at, H)]
            if slot > 0:
                row = row * strain
            coef[pl.ds(slot * SUB, SUB), :] = jnp.broadcast_to(row, (SUB, H))

    def plan(place):
        lane = lax.broadcasted_iota(jnp.int32, (PACK, LANE), 1)
        low_lane = lax.broadcasted_iota(jnp.int32, (SUB, LANE), 1)
        steps = []
        for slot in range(terms):
            if slot < 3:
                steps.append((place * tiles + (0, -tiles, tiles)[slot], None, None, None))
            else:
                offset = slots[slot, 1] + 8 * LANE
                turn = lax.rem(offset, LANE)
                first = place * tiles + lax.div(offset, LANE) - 8
                back = lax.rem(LANE - turn, LANE)
                steps.append((first, back, lane < LANE - turn, low_lane < LANE - turn))
        return steps

    def shifted(load, back, keep, width):
        if back is None:
            return [load(t) for t in range(width)]
        rolled = [pltpu.roll(load(t), back, 1) for t in range(width + 1)]
        return [jnp.where(keep, rolled[t], rolled[t + 1]) for t in range(width)]

    def whiten_special(steps):
        acc = [None] * tiles
        for slot, (first, back, _, keep) in enumerate(steps):
            values = shifted(lambda t: special[first + t], back, keep, tiles)
            for t in range(tiles):
                product = values[t] * coef[pl.ds(slot * SUB, SUB), pl.ds(t * LANE, LANE)]
                acc[t] = product if acc[t] is None else acc[t] + product
        return acc

    def whiten_rows(steps, starts, low, width):
        def twice(ref, at_row, t):
            value = ref[pl.ds(at_row, SUB), pl.ds((low + t) * LANE, LANE)]
            return jnp.concatenate([value, value], 0)

        off = [twice(mean_white, 0, t) for t in range(width)]
        acc = [list(off) for _ in starts]
        for slot, (first, back, keep, _) in enumerate(steps):
            weights = [twice(coef, slot * SUB, t) for t in range(width)]
            for r, at_row in enumerate(starts):
                values = shifted(lambda t: raw[first + low + t, pl.ds(at_row, PACK), :], back, keep, width)
                for t in range(width):
                    product = values[t].astype(F32) * weights[t]
                    acc[r][t] = product - acc[r][t] if slot == 0 else acc[r][t] + product
        return acc

    def products():
        block = jnp.concatenate([aw[t] for t in range(tiles)], axis=1)
        return lax.dot_general(
            block, block[:members], (((1,), (1,)), ((), ())), preferred_element_type=F32)

    def whiten_chunk(place, column, at, meanwhile=None):
        coefficients(column, at)
        steps = plan(place)
        pending = []

        def store_oldest():
            for at_row, tile, value in pending.pop(0):
                aw[tile, pl.ds(at_row, PACK), :] = value

        acc = whiten_special(steps)
        row = lax.broadcasted_iota(jnp.int32, (PACK, LANE), 0)
        parts = []
        for t in range(tiles):
            mean_white[:, pl.ds(t * LANE, LANE)] = jnp.broadcast_to(acc[t][1:2], (SUB, LANE))
            wide = jnp.broadcast_to(acc[t][0:1], (PACK, LANE))
            high = wide.astype(BF).astype(F32)
            rest = wide - high
            middle = rest.astype(BF).astype(F32)
            low = rest - middle
            split = jnp.where(row == 0, high, jnp.where(row == 1, middle, jnp.where(row == 2, low, 0.0)))
            parts.append((members, t, split.astype(BF)))
        pending.append(parts)
        scale = math.sqrt(members - 1) * row_factor
        misfit = [acc[t][0:1] * scale for t in range(tiles)]
        width = tiles // 2
        for group in range(members // (TALL * PACK)):
            starts = [(group * TALL + r) * PACK for r in range(TALL)]
            for first in (0, width):
                out = whiten_rows(steps, starts, first, width)
                pending.append([
                    (at_row, first + t, out[r][t].astype(BF))
                    for r, at_row in enumerate(starts) for t in range(width)])
                if len(pending) > LATE:
                    store_oldest()
            if group == 0 and meanwhile is not None:
                meanwhile()
        while pending:
            store_oldest()
        for t in range(tiles):
            row_out[:, pl.ds(at + t * LANE, LANE)] = misfit[t]

    if edge:
        for copy in copies:
            copy.wait()
        for which in range(2):
            near = range(3 * which, 3 * which + 3)
            halo = 5 * which
            for place in near:
                tile_wait(place, members + (PACK if place == halo else 0))
            if which == 1:
                gram[...] += products()
            means = [mean_rows(place) for place in near]
            for t in range(tiles):
                pieces = raw[halo * tiles + t, pl.ds(members, PACK), :].astype(F32)
                obs[:, pl.ds(halo * H + t * LANE, LANE)] = pieces[0:1] + pieces[1:2] + pieces[2:3]
            for place, mean in zip(near, means):
                keep_special(place, mean)
            whiten_chunk(1 + 3 * which, which * (columns - H), which * H)
        out_copies = [
            pltpu.make_async_copy(row_out.at[:, pl.ds(0, H)], misfit_out.at[:, pl.ds(0, H)], sems.at[0]),
            pltpu.make_async_copy(row_out.at[:, pl.ds(H, H)], misfit_out.at[:, pl.ds(columns - H, H)], sems.at[1]),
        ]
    else:
        for copy in copies:
            copy.wait()

        def centre_step(place, carry):
            tile_wait(place, members)
            keep_special(place, mean_rows(place))
            return carry

        lax.fori_loop(0, 3, centre_step, 0)

        def chunk_step(place, carry):
            ahead = jnp.minimum(place + 2, chunks - 1)

            @pl.when(place + 2 < chunks)
            def _():
                tile_wait(ahead, members)

            @pl.when(place + AHEAD - 1 < chunks)
            def _():
                coming = place + AHEAD - 1
                tile_copies(pred_ref, pl.multiple_of(coming * H, H), coming, members)

            added = products()
            mean = mean_rows(ahead)
            column = pl.multiple_of(place * H, H)

            def meanwhile():
                gram[...] += added
                keep_special(ahead, mean)

            whiten_chunk(place, column, column, meanwhile)
            return carry

        lax.fori_loop(1, chunks - 1, chunk_step, 0)
        inside = pl.ds(H, columns - 2 * H)
        out_copies = [pltpu.make_async_copy(row_out.at[:, inside], misfit_out.at[:, inside], sems.at[0])]
    for copy in out_copies:
        copy.start()
    gram[...] += products()

    if edge:
        gram_copy.wait()
    tail = gram[pl.ds(members, 8), :]
    total = tail[0:1] + tail[1:2] + tail[2:3]
    both = gram[pl.ds(0, members), :]
    down = lax.broadcasted_iota(jnp.int32, (half, half), 0)
    across = lax.broadcasted_iota(jnp.int32, (half, half), 1)

    def tuck(block, piece):
        block = jnp.where((down == 1) & (across == half - 1), piece[:, :1], block)
        return jnp.where((down == 0) & (across > 0), piece, block)

    blocks = (
        tuck(both[:half, :half], total[:, :half]),
        both[half:, :half],
        tuck(both[half:, half:], total[:, half:]),
    )
    for index, block in enumerate(blocks):
        at = pl.ds(index * half, half)
        block = block * (1.0 / obs_total)
        gram_out[:, at] = block + gram_in[:, at] if edge else block
    for copy in out_copies:
        copy.wait()


def local_call(edge, obs_total, offsets, rows_count, predicted, observed, band, *more):
    members, columns = predicted.shape
    terms = band.shape[0]
    rows = members + PACK
    places = 6 if edge else columns // H
    tiles = places * (H // LANE)
    vmem = pl.BlockSpec(memory_space=pltpu.VMEM)
    smem = pl.BlockSpec(memory_space=pltpu.SMEM)
    far = pl.BlockSpec(memory_space=pltpu.HBM)
    in_specs = [smem, smem, far, far, far]
    if edge:
        in_specs += [far, far, far, far]
    scratch = [
        pltpu.VMEM((tiles, rows if edge else members, LANE), BF),
        pltpu.VMEM((tiles, SUB, LANE), F32),
        pltpu.VMEM((H // LANE, rows, LANE), BF),
        pltpu.VMEM((SUB * terms, H), F32),
        pltpu.VMEM((SUB, H), F32),
        pltpu.VMEM((rows, members), F32),
        pltpu.VMEM((1, places * H), F32),
        pltpu.VMEM((terms, 2 * H if edge else columns), F32),
        pltpu.VMEM((1, 2 * H if edge else columns), F32),
        pltpu.SMEM((8, 2), jnp.int32),
        pltpu.SemaphoreType.DMA((places + 5,)),
    ]
    if edge:
        scratch.append(pltpu.VMEM((members // 2, members // 2 * 3), F32))
    work = 2 if edge else places - 2
    return pl.pallas_call(
        functools.partial(local_kernel, edge, columns, obs_total),
        out_shape=(
            jax.ShapeDtypeStruct((members // 2, members // 2 * 3), F32),
            jax.ShapeDtypeStruct((1, columns), F32),
        ),
        in_specs=in_specs,
        out_specs=[vmem, far],
        scratch_shapes=scratch,
        input_output_aliases={8: 1} if edge else {},
        compiler_params=pltpu.CompilerParams(vmem_limit_bytes=VMEM),
        cost_estimate=pl.CostEstimate(
            flops=2 * rows * members * H * work * 2, bytes_accessed=members * H * places * 2, transcendentals=0),
        name="edges" if edge else "inner",
    )(offsets, rows_count, predicted, observed, band, *more)


def update_kernel(sum_ref, params_ref, out_ref, work):
    members = params_ref.shape[1]
    highest = lax.Precision.HIGHEST
    row_index = lax.broadcasted_iota(jnp.int32, (members, members), 0)
    col_index = lax.broadcasted_iota(jnp.int32, (members, members), 1)
    identity = jnp.where(row_index == col_index, 1.0, 0.0).astype(F32)
    half = members // 2
    eye_half = identity[:half, :half]
    lower = row_index[:half, :half] >= col_index[:half, :half]

    def mirrored(block):
        return jnp.where(lower, block, block.T) + eye_half

    def tucked(block):
        first = lax.broadcasted_iota(jnp.int32, (1, half), 1) == 0
        return jnp.where(first, block[1:2, half - 1:half], block[0:1, :])

    blocks = [sum_ref[:, pl.ds(index * half, half)] for index in range(3)]
    work[pl.ds(0, half), pl.ds(0, half)] = mirrored(blocks[0])
    work[pl.ds(0, half), pl.ds(half, half)] = blocks[1].T
    work[pl.ds(half, half), pl.ds(0, half)] = blocks[1]
    work[pl.ds(half, half), pl.ds(half, half)] = mirrored(blocks[2])
    projection = jnp.concatenate([tucked(blocks[0]), tucked(blocks[2])], 1)
    work[:, pl.ds(members, members)] = identity
    panels = BLOCK // PANEL
    sub = lax.broadcasted_iota(jnp.int32, (PANEL, LANE), 0)
    eye = identity[:BLOCK, :BLOCK]

    def across(tile, column):
        return jnp.broadcast_to(tile[:, column:column + 1], (PANEL, LANE))

    def down(tile, row):
        return jnp.broadcast_to(tile[row:row + 1, :], (PANEL, LANE))

    for block in range(members // BLOCK):
        r0 = block * BLOCK
        start = jnp.concatenate([work[pl.ds(r0, BLOCK), pl.ds(r0, BLOCK)], eye], axis=1)
        tiles = [start[PANEL * t:PANEL * (t + 1)] for t in range(panels)]
        done = []
        for p in range(panels):
            c0 = PANEL * p
            tile = tiles[p]
            upper = tile
            full = tile
            cols = [across(tile, c0 + j) for j in range(PANEL)]
            scale = jnp.zeros((PANEL, LANE), F32)
            for k in range(0, PANEL, 2):
                left, right = cols[k], cols[k + 1]
                a, b, c = down(left, k), down(left, k + 1), down(right, k + 1)
                det = a * c - b * b
                inverse = 1.0 / det
                ratio = b / a
                scale = jnp.where(sub == k, a, jnp.where(sub == k + 1, c - b * ratio, scale))
                from_left = c * left - b * right
                from_right = a * right - b * left

                def change_of(values):
                    x, y = down(values, k), down(values, k + 1)
                    return x, y, (from_left * x + from_right * y) * inverse

                def clear(values):
                    x, y, change = change_of(values)
                    own = jnp.where(sub == k, c * x - b * y, a * y - b * x) * inverse
                    return jnp.where((sub == k) | (sub == k + 1), own, values - change)

                x, y, change = change_of(upper)
                upper = upper - jnp.where(sub > k + 1, change, jnp.where(sub == k + 1, ratio * x, 0.0))
                full = clear(full)
                for j in range(k + 2, PANEL):
                    cols[j] = clear(cols[j])
            done.append(upper * lax.rsqrt(scale))
            rows_of = [down(full, k) for k in range(PANEL)]
            for t in range(p + 1, panels):
                tile_t = tiles[t]
                change = [across(tile_t, c0 + k) * rows_of[k] for k in range(PANEL)]
                while len(change) > 1:
                    change = [a + b for a, b in zip(change[::2], change[1::2])]
                tiles[t] = tile_t - change[0]
        lower_inverse = jnp.concatenate(done, axis=0)[:, BLOCK:2 * BLOCK]
        begin = (r0 + BLOCK) // LANE * LANE
        end = members + -(-(r0 + BLOCK) // LANE) * LANE
        wide = pl.ds(begin, end - begin)
        solved = jnp.dot(lower_inverse, work[pl.ds(r0, BLOCK), wide], precision=highest, preferred_element_type=F32)
        work[pl.ds(r0, BLOCK), wide] = solved
        if r0 + BLOCK < members:
            rest = members - r0 - BLOCK
            factor = solved[:, r0 + BLOCK - begin:members - begin]
            work[pl.ds(r0 + BLOCK, rest), wide] = work[pl.ds(r0 + BLOCK, rest), wide] - lax.dot_general(
                factor, solved, (((0,), (0,)), ((), ())), precision=highest, preferred_element_type=F32)

    inverse = jnp.where(row_index >= col_index, work[:, pl.ds(members, members)], 0.0)
    solved = jnp.sum(inverse * projection, axis=1, keepdims=True)
    weights = jnp.sum(inverse * solved, axis=0, keepdims=True)
    turned = inverse + weights
    turned = turned - jnp.mean(turned, axis=1, keepdims=True) + 1.0 / members
    high = turned.astype(BF)
    rest = turned - high.astype(F32)
    middle = rest.astype(BF)
    low = (rest - middle.astype(F32)).astype(BF)
    def times(part):
        return lax.dot_general(params_ref[...], part, (((1,), (1,)), ((), ())), preferred_element_type=F32)

    out_ref[...] = times(high) + (times(middle) + times(low))


def update(total, params):
    members = params.shape[1]
    vmem = pl.BlockSpec(memory_space=pltpu.VMEM)
    return pl.pallas_call(
        update_kernel,
        out_shape=jax.ShapeDtypeStruct(params.shape, F32),
        in_specs=[vmem, vmem],
        out_specs=vmem,
        scratch_shapes=[pltpu.VMEM((members, 2 * members), F32)],
        compiler_params=pltpu.CompilerParams(vmem_limit_bytes=VMEM // 4),
        name="update",
    )(total, params)


def halo_kernel(columns, pred_ref, obs_ref, first_ref, last_ref, obs, sems):
    members = pred_ref.shape[0]
    copies = []
    for side, (out, at) in enumerate(((first_ref, 0), (last_ref, columns - H))):
        copies.append(pltpu.make_async_copy(
            pred_ref.at[:, pl.ds(at, H)], out.at[pl.ds(0, members), :], sems.at[side]))
        copies.append(pltpu.make_async_copy(
            obs_ref.at[:, pl.ds(at, H)], obs.at[:, pl.ds(side * H, H)], sems.at[2 + side]))
    for copy in copies:
        copy.start()
    for copy in copies[1::2]:
        copy.wait()
    row = lax.broadcasted_iota(jnp.int32, (PACK, H), 0)
    for side, out in enumerate((first_ref, last_ref)):
        wide = jnp.broadcast_to(obs[:, pl.ds(side * H, H)], (PACK, H))
        high = wide.astype(BF).astype(F32)
        rest = wide - high
        middle = rest.astype(BF).astype(F32)
        low = rest - middle
        split = jnp.where(row == 0, high, jnp.where(row == 1, middle, jnp.where(row == 2, low, 0.0)))
        out[pl.ds(members, PACK), :] = split.astype(BF)
    for copy in copies[0::2]:
        copy.wait()


def halo_blocks(predicted, observed):
    members, columns = predicted.shape
    far = pl.BlockSpec(memory_space=pltpu.HBM)
    near = pl.BlockSpec(memory_space=pltpu.VMEM)
    block = jax.ShapeDtypeStruct((members + PACK, H), BF)
    return pl.pallas_call(
        functools.partial(halo_kernel, columns),
        out_shape=(block, block),
        in_specs=[far, far],
        out_specs=[near, near],
        scratch_shapes=[pltpu.VMEM((1, 2 * H), F32), pltpu.SemaphoreType.DMA((4,))],
        compiler_params=pltpu.CompilerParams(vmem_limit_bytes=VMEM),
        name="halos",
    )(predicted, observed)


def sum_over(values, axes):
    shards = lax.axis_size(axes)
    rows, width = values.shape
    parts = lax.all_to_all(values, axes, 0, 0, tiled=True)
    own = jnp.sum(parts.reshape(shards, rows // shards, width), axis=0)
    copies = jnp.broadcast_to(own[None], (shards, rows // shards, width)).reshape(rows, width)
    return lax.all_to_all(copies, axes, 0, 0, tiled=True)


def body(predicted, observed, band, offsets, rows_count, params):
    columns = predicted.shape[1]
    axes = ("obs", "par")
    shards = lax.axis_size(axes)
    obs_total = columns * shards
    up = [(i, i + 1) for i in range(shards - 1)]
    down = [(j, i) for i, j in up]
    obs_row = observed[None, :]
    first, last = halo_blocks(predicted, obs_row)
    left = lax.ppermute(last, axes, up)
    right = lax.ppermute(first, axes, down)
    gram, misfit = local_call(False, obs_total, offsets, rows_count, predicted, obs_row, band)
    gram, misfit = local_call(
        True, obs_total, offsets, rows_count, predicted, obs_row, band, left, right, gram, misfit)
    total = sum_over(gram, axes)
    return (update(total, params), misfit[0])


def solution(mesh):
    in_specs = (
        P(None, ("grp", "obs", "par")),
        P(("grp", "obs", "par")),
        P(None, ("grp", "obs", "par")),
        P(),
        P(("grp", "obs", "par")),
        P(("grp", "obs", "par"), None),
    )
    out_specs = (P(("grp", "obs", "par"), None), P(("grp", "obs", "par")))
    return jax.shard_map(body, mesh=mesh, in_specs=in_specs, out_specs=out_specs, check_vma=False)
```

```python
import functools
import math

import jax
import jax.numpy as jnp
from jax import lax
from jax.experimental import pallas as pl
from jax.experimental.pallas import tpu as pltpu
from jax.sharding import PartitionSpec as P

H = 1024
LANE = 128
SUB = 8
PACK = 16
TALL = 2
LATE = 3
AHEAD = 5
BLOCK = 64
PANEL = 8
VMEM = 64 * 2**20
BF = jnp.bfloat16
F32 = jnp.float32


def local_kernel(edge, columns, obs_total, *refs):
    if edge:
        (off_ref, count_ref, pred_ref, obs_ref, band_ref, left_ref, right_ref, gram_before, misfit_in,
         gram_out, misfit_out, raw, special, aw, coef, mean_white, gram, obs, band, row_out, slots,
         sems, gram_in) = refs
    else:
        (off_ref, count_ref, pred_ref, obs_ref, band_ref,
         gram_out, misfit_out, raw, special, aw, coef, mean_white, gram, obs, band, row_out, slots,
         sems) = refs
    members = pred_ref.shape[0]
    terms = band_ref.shape[0]
    chunks = columns // H
    tiles = H // LANE
    half = members // 2
    row_factor = 1.0 / math.sqrt(obs_total)

    def tile_copies(source, column, place, height):
        for t in range(tiles):
            pltpu.make_async_copy(
                source.at[:, pl.ds(column + t * LANE, LANE)],
                raw.at[place * tiles + t, pl.ds(0, height), :], sems.at[place]).start()

    def tile_wait(place, height):
        whole = raw.at[pl.ds(place * tiles, tiles), pl.ds(0, height), :]
        pltpu.make_async_copy(whole, whole, sems.at[place]).wait()

    if edge:
        copies = []
        for which in range(2):
            there = which * (columns - 2 * H)
            copies.append(pltpu.make_async_copy(
                obs_ref.at[:, pl.ds(there, 2 * H)], obs.at[:, pl.ds((1 + which * 2) * H, 2 * H)], sems.at[6 + which]))
            there = which * (columns - H)
            copies.append(pltpu.make_async_copy(
                band_ref.at[:, pl.ds(there, H)], band.at[:, pl.ds(which * H, H)], sems.at[8 + which]))
    else:
        copies = [
            pltpu.make_async_copy(obs_ref, obs, sems.at[chunks]),
            pltpu.make_async_copy(band_ref, band, sems.at[chunks + 1]),
        ]
    for copy in copies:
        copy.start()
    if edge:
        gram_copy = pltpu.make_async_copy(gram_before, gram_in, sems.at[10])
        gram_copy.start()
        tile_copies(left_ref, 0, 0, members + PACK)
        for place, chunk in ((1, 0), (2, 1), (3, chunks - 2), (4, chunks - 1)):
            tile_copies(pred_ref, chunk * H, place, members)
        tile_copies(right_ref, 0, 5, members + PACK)
    else:
        for place in range(AHEAD):
            tile_copies(pred_ref, place * H, place, members)

    slots[0, 0] = 0
    slots[0, 1] = 0
    free = jnp.int32(3)
    for term in range(1, terms):
        offset = off_ref[term]
        whole = (offset == H) | (offset == -H)
        place = jnp.where(offset == -H, 1, jnp.where(offset == H, 2, free))
        place = jnp.minimum(place, terms - 1)
        slots[place, 0] = jnp.int32(term)
        slots[place, 1] = offset
        free = free + jnp.where(whole, 0, 1)

    gram[...] = jnp.zeros_like(gram)
    aw[...] = jnp.zeros_like(aw)

    def mean_rows(place):
        block = jnp.concatenate(
            [raw[place * tiles + t, pl.ds(0, members), :] for t in range(tiles)], axis=1)
        return jnp.dot(jnp.full((PACK, members), 1.0 / members, BF), block, preferred_element_type=F32)[:SUB]

    def keep_special(place, mean):
        seen = obs[:, pl.ds(pl.multiple_of(place * H, H), H)]
        innovation = (seen - mean).astype(BF).astype(F32)
        value = jnp.where(lax.broadcasted_iota(jnp.int32, (SUB, H), 0) == 0, innovation, mean)
        for t in range(tiles):
            special[place * tiles + t] = value[:, t * LANE:(t + 1) * LANE]

    def coefficients(column, at):
        index = column + lax.broadcasted_iota(jnp.int32, (1, H), 1)
        strained = (index < count_ref[0]) | (index >= columns - H)
        strain = jnp.where(strained, 1.0, 0.0)
        for slot in range(terms):
            term = slots[slot, 0]
            row = band[pl.ds(term, 1), pl.ds(at, H)]
            if slot > 0:
                row = row * strain
            coef[pl.ds(slot * SUB, SUB), :] = jnp.broadcast_to(row, (SUB, H))

    def plan(place):
        lane = lax.broadcasted_iota(jnp.int32, (PACK, LANE), 1)
        low_lane = lax.broadcasted_iota(jnp.int32, (SUB, LANE), 1)
        steps = []
        for slot in range(terms):
            if slot < 3:
                steps.append((place * tiles + (0, -tiles, tiles)[slot], None, None, None))
            else:
                offset = slots[slot, 1] + 8 * LANE
                turn = lax.rem(offset, LANE)
                first = place * tiles + lax.div(offset, LANE) - 8
                back = lax.rem(LANE - turn, LANE)
                steps.append((first, back, lane < LANE - turn, low_lane < LANE - turn))
        return steps

    def shifted(load, back, keep, width):
        if back is None:
            return [load(t) for t in range(width)]
        rolled = [pltpu.roll(load(t), back, 1) for t in range(width + 1)]
        return [jnp.where(keep, rolled[t], rolled[t + 1]) for t in range(width)]

    def whiten_special(steps):
        acc = [None] * tiles
        for slot, (first, back, _, keep) in enumerate(steps):
            values = shifted(lambda t: special[first + t], back, keep, tiles)
            for t in range(tiles):
                product = values[t] * coef[pl.ds(slot * SUB, SUB), pl.ds(t * LANE, LANE)]
                acc[t] = product if acc[t] is None else acc[t] + product
        return acc

    def whiten_rows(steps, starts, low, width):
        def twice(ref, at_row, t):
            value = ref[pl.ds(at_row, SUB), pl.ds((low + t) * LANE, LANE)]
            return jnp.concatenate([value, value], 0)

        off = [twice(mean_white, 0, t) for t in range(width)]
        acc = [list(off) for _ in starts]
        for slot, (first, back, keep, _) in enumerate(steps):
            weights = [twice(coef, slot * SUB, t) for t in range(width)]
            for r, at_row in enumerate(starts):
                values = shifted(lambda t: raw[first + low + t, pl.ds(at_row, PACK), :], back, keep, width)
                for t in range(width):
                    product = values[t].astype(F32) * weights[t]
                    acc[r][t] = product - acc[r][t] if slot == 0 else acc[r][t] + product
        return acc

    def products():
        block = jnp.concatenate([aw[t] for t in range(tiles)], axis=1)
        return lax.dot_general(
            block, block[:members], (((1,), (1,)), ((), ())), preferred_element_type=F32)

    def whiten_chunk(place, column, at, meanwhile=None):
        coefficients(column, at)
        steps = plan(place)
        pending = []

        def store_oldest():
            for at_row, tile, value in pending.pop(0):
                aw[tile, pl.ds(at_row, PACK), :] = value

        acc = whiten_special(steps)
        row = lax.broadcasted_iota(jnp.int32, (PACK, LANE), 0)
        parts = []
        for t in range(tiles):
            mean_white[:, pl.ds(t * LANE, LANE)] = jnp.broadcast_to(acc[t][1:2], (SUB, LANE))
            wide = jnp.broadcast_to(acc[t][0:1], (PACK, LANE))
            high = wide.astype(BF).astype(F32)
            rest = wide - high
            middle = rest.astype(BF).astype(F32)
            low = rest - middle
            split = jnp.where(row == 0, high, jnp.where(row == 1, middle, jnp.where(row == 2, low, 0.0)))
            parts.append((members, t, split.astype(BF)))
        pending.append(parts)
        scale = math.sqrt(members - 1) * row_factor
        misfit = [acc[t][0:1] * scale for t in range(tiles)]
        width = tiles // 2
        for group in range(members // (TALL * PACK)):
            starts = [(group * TALL + r) * PACK for r in range(TALL)]
            for first in (0, width):
                out = whiten_rows(steps, starts, first, width)
                pending.append([
                    (at_row, first + t, out[r][t].astype(BF))
                    for r, at_row in enumerate(starts) for t in range(width)])
                if len(pending) > LATE:
                    store_oldest()
            if group == 0 and meanwhile is not None:
                meanwhile()
        while pending:
            store_oldest()
        for t in range(tiles):
            row_out[:, pl.ds(at + t * LANE, LANE)] = misfit[t]

    if edge:
        for copy in copies:
            copy.wait()
        for which in range(2):
            near = range(3 * which, 3 * which + 3)
            halo = 5 * which
            for place in near:
                tile_wait(place, members + (PACK if place == halo else 0))
            if which == 1:
                gram[...] += products()
            means = [mean_rows(place) for place in near]
            for t in range(tiles):
                pieces = raw[halo * tiles + t, pl.ds(members, PACK), :].astype(F32)
                obs[:, pl.ds(halo * H + t * LANE, LANE)] = pieces[0:1] + pieces[1:2] + pieces[2:3]
            for place, mean in zip(near, means):
                keep_special(place, mean)
            whiten_chunk(1 + 3 * which, which * (columns - H), which * H)
        out_copies = [
            pltpu.make_async_copy(row_out.at[:, pl.ds(0, H)], misfit_out.at[:, pl.ds(0, H)], sems.at[0]),
            pltpu.make_async_copy(row_out.at[:, pl.ds(H, H)], misfit_out.at[:, pl.ds(columns - H, H)], sems.at[1]),
        ]
    else:
        for copy in copies:
            copy.wait()

        def centre_step(place, carry):
            tile_wait(place, members)
            keep_special(place, mean_rows(place))
            return carry

        lax.fori_loop(0, 3, centre_step, 0)

        def chunk_step(place, carry):
            ahead = jnp.minimum(place + 2, chunks - 1)

            @pl.when(place + 2 < chunks)
            def _():
                tile_wait(ahead, members)

            @pl.when(place + AHEAD - 1 < chunks)
            def _():
                coming = place + AHEAD - 1
                tile_copies(pred_ref, pl.multiple_of(coming * H, H), coming, members)

            added = products()
            mean = mean_rows(ahead)
            column = pl.multiple_of(place * H, H)

            def meanwhile():
                gram[...] += added
                keep_special(ahead, mean)

            whiten_chunk(place, column, column, meanwhile)
            return carry

        lax.fori_loop(1, chunks - 1, chunk_step, 0)
        inside = pl.ds(H, columns - 2 * H)
        out_copies = [pltpu.make_async_copy(row_out.at[:, inside], misfit_out.at[:, inside], sems.at[0])]
    for copy in out_copies:
        copy.start()
    gram[...] += products()

    if edge:
        gram_copy.wait()
    tail = gram[pl.ds(members, 8), :]
    total = tail[0:1] + tail[1:2] + tail[2:3]
    both = gram[pl.ds(0, members), :]
    down = lax.broadcasted_iota(jnp.int32, (half, half), 0)
    across = lax.broadcasted_iota(jnp.int32, (half, half), 1)

    def tuck(block, piece):
        block = jnp.where((down == 1) & (across == half - 1), piece[:, :1], block)
        return jnp.where((down == 0) & (across > 0), piece, block)

    blocks = (
        tuck(both[:half, :half], total[:, :half]),
        both[half:, :half],
        tuck(both[half:, half:], total[:, half:]),
    )
    for index, block in enumerate(blocks):
        at = pl.ds(index * half, half)
        block = block * (1.0 / obs_total)
        gram_out[:, at] = block + gram_in[:, at] if edge else block
    for copy in out_copies:
        copy.wait()


def local_call(edge, obs_total, offsets, rows_count, predicted, observed, band, *more):
    members, columns = predicted.shape
    terms = band.shape[0]
    rows = members + PACK
    places = 6 if edge else columns // H
    tiles = places * (H // LANE)
    vmem = pl.BlockSpec(memory_space=pltpu.VMEM)
    smem = pl.BlockSpec(memory_space=pltpu.SMEM)
    far = pl.BlockSpec(memory_space=pltpu.HBM)
    in_specs = [smem, smem, far, far, far]
    if edge:
        in_specs += [far, far, far, far]
    scratch = [
        pltpu.VMEM((tiles, rows if edge else members, LANE), BF),
        pltpu.VMEM((tiles, SUB, LANE), F32),
        pltpu.VMEM((H // LANE, rows, LANE), BF),
        pltpu.VMEM((SUB * terms, H), F32),
        pltpu.VMEM((SUB, H), F32),
        pltpu.VMEM((rows, members), F32),
        pltpu.VMEM((1, places * H), F32),
        pltpu.VMEM((terms, 2 * H if edge else columns), F32),
        pltpu.VMEM((1, 2 * H if edge else columns), F32),
        pltpu.SMEM((8, 2), jnp.int32),
        pltpu.SemaphoreType.DMA((places + 5,)),
    ]
    if edge:
        scratch.append(pltpu.VMEM((members // 2, members // 2 * 3), F32))
    work = 2 if edge else places - 2
    return pl.pallas_call(
        functools.partial(local_kernel, edge, columns, obs_total),
        out_shape=(
            jax.ShapeDtypeStruct((members // 2, members // 2 * 3), F32),
            jax.ShapeDtypeStruct((1, columns), F32),
        ),
        in_specs=in_specs,
        out_specs=[vmem, far],
        scratch_shapes=scratch,
        input_output_aliases={8: 1} if edge else {},
        compiler_params=pltpu.CompilerParams(vmem_limit_bytes=VMEM),
        cost_estimate=pl.CostEstimate(
            flops=2 * rows * members * H * work * 2, bytes_accessed=members * H * places * 2, transcendentals=0),
        name="edges" if edge else "inner",
    )(offsets, rows_count, predicted, observed, band, *more)


def update_kernel(sum_ref, params_ref, out_ref, work):
    members = params_ref.shape[1]
    highest = lax.Precision.HIGHEST
    row_index = lax.broadcasted_iota(jnp.int32, (members, members), 0)
    col_index = lax.broadcasted_iota(jnp.int32, (members, members), 1)
    identity = jnp.where(row_index == col_index, 1.0, 0.0).astype(F32)
    half = members // 2
    eye_half = identity[:half, :half]
    lower = row_index[:half, :half] >= col_index[:half, :half]

    def mirrored(block):
        return jnp.where(lower, block, block.T) + eye_half

    def tucked(block):
        first = lax.broadcasted_iota(jnp.int32, (1, half), 1) == 0
        return jnp.where(first, block[1:2, half - 1:half], block[0:1, :])

    blocks = [sum_ref[:, pl.ds(index * half, half)] for index in range(3)]
    work[pl.ds(0, half), pl.ds(0, half)] = mirrored(blocks[0])
    work[pl.ds(0, half), pl.ds(half, half)] = blocks[1].T
    work[pl.ds(half, half), pl.ds(0, half)] = blocks[1]
    work[pl.ds(half, half), pl.ds(half, half)] = mirrored(blocks[2])
    projection = jnp.concatenate([tucked(blocks[0]), tucked(blocks[2])], 1)
    work[:, pl.ds(members, members)] = identity
    panels = BLOCK // PANEL
    sub = lax.broadcasted_iota(jnp.int32, (PANEL, LANE), 0)
    eye = identity[:BLOCK, :BLOCK]

    def across(tile, column):
        return jnp.broadcast_to(tile[:, column:column + 1], (PANEL, LANE))

    def down(tile, row):
        return jnp.broadcast_to(tile[row:row + 1, :], (PANEL, LANE))

    for block in range(members // BLOCK):
        r0 = block * BLOCK
        start = jnp.concatenate([work[pl.ds(r0, BLOCK), pl.ds(r0, BLOCK)], eye], axis=1)
        tiles = [start[PANEL * t:PANEL * (t + 1)] for t in range(panels)]
        done = []
        for p in range(panels):
            c0 = PANEL * p
            tile = tiles[p]
            upper = tile
            full = tile
            cols = [across(tile, c0 + j) for j in range(PANEL)]
            scale = jnp.zeros((PANEL, LANE), F32)
            for k in range(0, PANEL, 2):
                left, right = cols[k], cols[k + 1]
                a, b, c = down(left, k), down(left, k + 1), down(right, k + 1)
                det = a * c - b * b
                inverse = 1.0 / det
                ratio = b / a
                scale = jnp.where(sub == k, a, jnp.where(sub == k + 1, c - b * ratio, scale))
                from_left = c * left - b * right
                from_right = a * right - b * left

                def change_of(values):
                    x, y = down(values, k), down(values, k + 1)
                    return x, y, (from_left * x + from_right * y) * inverse

                def clear(values):
                    x, y, change = change_of(values)
                    own = jnp.where(sub == k, c * x - b * y, a * y - b * x) * inverse
                    return jnp.where((sub == k) | (sub == k + 1), own, values - change)

                x, y, change = change_of(upper)
                upper = upper - jnp.where(sub > k + 1, change, jnp.where(sub == k + 1, ratio * x, 0.0))
                full = clear(full)
                for j in range(k + 2, PANEL):
                    cols[j] = clear(cols[j])
            done.append(upper * lax.rsqrt(scale))
            rows_of = [down(full, k) for k in range(PANEL)]
            for t in range(p + 1, panels):
                tile_t = tiles[t]
                change = [across(tile_t, c0 + k) * rows_of[k] for k in range(PANEL)]
                while len(change) > 1:
                    change = [a + b for a, b in zip(change[::2], change[1::2])]
                tiles[t] = tile_t - change[0]
        lower_inverse = jnp.concatenate(done, axis=0)[:, BLOCK:2 * BLOCK]
        begin = (r0 + BLOCK) // LANE * LANE
        end = members + -(-(r0 + BLOCK) // LANE) * LANE
        wide = pl.ds(begin, end - begin)
        solved = jnp.dot(lower_inverse, work[pl.ds(r0, BLOCK), wide], precision=highest, preferred_element_type=F32)
        work[pl.ds(r0, BLOCK), wide] = solved
        if r0 + BLOCK < members:
            rest = members - r0 - BLOCK
            factor = solved[:, r0 + BLOCK - begin:members - begin]
            work[pl.ds(r0 + BLOCK, rest), wide] = work[pl.ds(r0 + BLOCK, rest), wide] - lax.dot_general(
                factor, solved, (((0,), (0,)), ((), ())), precision=highest, preferred_element_type=F32)

    inverse = jnp.where(row_index >= col_index, work[:, pl.ds(members, members)], 0.0)
    solved = jnp.sum(inverse * projection, axis=1, keepdims=True)
    weights = jnp.sum(inverse * solved, axis=0, keepdims=True)
    turned = inverse + weights
    turned = turned - jnp.mean(turned, axis=1, keepdims=True) + 1.0 / members
    high = turned.astype(BF)
    rest = turned - high.astype(F32)
    middle = rest.astype(BF)
    low = (rest - middle.astype(F32)).astype(BF)
    def times(part):
        return lax.dot_general(params_ref[...], part, (((1,), (1,)), ((), ())), preferred_element_type=F32)

    out_ref[...] = times(high) + (times(middle) + times(low))


def update(total, params):
    members = params.shape[1]
    vmem = pl.BlockSpec(memory_space=pltpu.VMEM)
    return pl.pallas_call(
        update_kernel,
        out_shape=jax.ShapeDtypeStruct(params.shape, F32),
        in_specs=[vmem, vmem],
        out_specs=vmem,
        scratch_shapes=[pltpu.VMEM((members, 2 * members), F32)],
        compiler_params=pltpu.CompilerParams(vmem_limit_bytes=VMEM // 4),
        name="update",
    )(total, params)


def halo_kernel(columns, pred_ref, obs_ref, first_ref, last_ref, obs, sems):
    members = pred_ref.shape[0]
    copies = []
    for side, (out, at) in enumerate(((first_ref, 0), (last_ref, columns - H))):
        copies.append(pltpu.make_async_copy(
            pred_ref.at[:, pl.ds(at, H)], out.at[pl.ds(0, members), :], sems.at[side]))
        copies.append(pltpu.make_async_copy(
            obs_ref.at[:, pl.ds(at, H)], obs.at[:, pl.ds(side * H, H)], sems.at[2 + side]))
    for copy in copies:
        copy.start()
    for copy in copies[1::2]:
        copy.wait()
    row = lax.broadcasted_iota(jnp.int32, (PACK, H), 0)
    for side, out in enumerate((first_ref, last_ref)):
        wide = jnp.broadcast_to(obs[:, pl.ds(side * H, H)], (PACK, H))
        high = wide.astype(BF).astype(F32)
        rest = wide - high
        middle = rest.astype(BF).astype(F32)
        low = rest - middle
        split = jnp.where(row == 0, high, jnp.where(row == 1, middle, jnp.where(row == 2, low, 0.0)))
        out[pl.ds(members, PACK), :] = split.astype(BF)
    for copy in copies[0::2]:
        copy.wait()


def halo_blocks(predicted, observed):
    members, columns = predicted.shape
    far = pl.BlockSpec(memory_space=pltpu.HBM)
    near = pl.BlockSpec(memory_space=pltpu.VMEM)
    block = jax.ShapeDtypeStruct((members + PACK, H), BF)
    return pl.pallas_call(
        functools.partial(halo_kernel, columns),
        out_shape=(block, block),
        in_specs=[far, far],
        out_specs=[near, near],
        scratch_shapes=[pltpu.VMEM((1, 2 * H), F32), pltpu.SemaphoreType.DMA((4,))],
        compiler_params=pltpu.CompilerParams(vmem_limit_bytes=VMEM),
        name="halos",
    )(predicted, observed)


def sum_over(values, axes):
    shards = lax.axis_size(axes)
    rows, width = values.shape
    parts = lax.all_to_all(values, axes, 0, 0, tiled=True)
    own = jnp.sum(parts.reshape(shards, rows // shards, width), axis=0)
    copies = jnp.broadcast_to(own[None], (shards, rows // shards, width)).reshape(rows, width)
    return lax.all_to_all(copies, axes, 0, 0, tiled=True)


def body(predicted, observed, band, offsets, rows_count, params):
    columns = predicted.shape[1]
    axes = ("obs", "par")
    shards = lax.axis_size(axes)
    obs_total = columns * shards
    up = [(i, i + 1) for i in range(shards - 1)]
    down = [(j, i) for i, j in up]
    obs_row = observed[None, :]
    first, last = halo_blocks(predicted, obs_row)
    left = lax.ppermute(last, axes, up)
    right = lax.ppermute(first, axes, down)
    gram, misfit = local_call(False, obs_total, offsets, rows_count, predicted, obs_row, band)
    gram, misfit = local_call(
        True, obs_total, offsets, rows_count, predicted, obs_row, band, left, right, gram, misfit)
    total = sum_over(gram, axes)
    return (update(total, params), misfit[0])


def solution(mesh):
    in_specs = (
        P(None, ("grp", "obs", "par")),
        P(("grp", "obs", "par")),
        P(None, ("grp", "obs", "par")),
        P(),
        P(("grp", "obs", "par")),
        P(("grp", "obs", "par"), None),
    )
    out_specs = (P(("grp", "obs", "par"), None), P(("grp", "obs", "par")))
    return jax.shard_map(body, mesh=mesh, in_specs=in_specs, out_specs=out_specs, check_vma=False)
```
